32 devices in a mesh: shard: 16 (over z, y, core), ctx: 2 (over x).
Axes of the slice: x: 2, y: 2, z: 4, core: 2. Of those that a mesh axis runs over, the one named last changes fastest.
Arguments:
- tokens: bfloat16 [16, 1152, 1024], P('shard', 'ctx'), may hold values from -6 to 6
- segments: int32 [16, 1152], P('shard', 'ctx'), may hold values from 0 to 7, never falling along the last dimension, each value on 1 to 1024 neighbouring positions
- w_qkv: bfloat16 [1024, 3072], P('shard'), may hold values from -0.1875 to 0.1875
- qv_bias: bfloat16 [2, 1024], P(None, 'shard'), may hold values from -3 to 3
- w_out: bfloat16 [1024, 1024], P('shard'), may hold values from -0.75 to 0.75
- out_bias: bfloat16 [1024], P('shard'), may hold values from -2 to 2
- w_in: bfloat16 [1024, 4096], P('shard'), may hold values from -0.1875 to 0.1875
- in_bias: bfloat16 [4096], P('shard'), may hold values from -3 to 3
- w_down: bfloat16 [4096, 1024], P('shard'), may hold values from -0.09375 to 0.09375
- down_bias: bfloat16 [1024], P('shard'), may hold values from -2 to 2
- gains: bfloat16 [2, 1024], P(None, 'shard'), may hold values from 0.5 to 1.5
- shifts: bfloat16 [2, 1024], P(None, 'shard'), may hold values from -1.5 to 1.5
- cotangent: float32 [16, 1152, 1024], P('shard', 'ctx'), may hold values from -6 to 6
Outputs:
- outputs: bfloat16 [16, 1152, 1024], P('shard', 'ctx')
- grad_tokens: float32 [16, 1152, 1024], P('shard', 'ctx')
- grad_w_qkv: float32 [1024, 3072], P('shard')
- grad_qv_bias: float32 [2, 1024], P(None, 'shard')
- grad_w_out: float32 [1024, 1024], P('shard')
- grad_out_bias: float32 [1024], P('shard')
- grad_w_in: float32 [1024, 4096], P('shard')
- grad_in_bias: float32 [4096], P('shard')
- grad_w_down: float32 [4096, 1024], P('shard')
- grad_down_bias: float32 [1024], P('shard')
- grad_gains: float32 [2, 1024], P(None, 'shard')
- grad_shifts: float32 [2, 1024], P(None, 'shard')
The draws below stay inside these ranges and needn't reach their ends.
Inputs may be any that keep to these rules, and one draw needn't show every extreme that they name: `segments`: along each row the document numbers never fall; a document holds at most 1024 positions, and every row holds one document of exactly 1024 positions.
All inputs are finite; a program needn't handle non-finite values.
Results may differ from the reference program's by a relative error of at most 0.018.
Values may be sent and summed in bfloat16 or wider, within the bound.
No kernel may reach another device: no remote copies, remote signals or barrier semaphores. Data moves between devices by JAX's collectives and lax.ppermute only.
A program may use at most 256 MiB of HBM per device.

```python
import math
import jax
import jax.numpy as jnp
import numpy as np
from jax import lax

D = 1024
H = 16
HD = 64
FF = 4096
SEQ = 1152
LONGEST = 1024
DOCS = 8
ROWS = 16


def level_of(key, shape, shards, smallest, largest):
    level = 1.0
    for position, parts in shards:
        draws = jax.random.uniform(jax.random.fold_in(jax.random.fold_in(key, 6), position), (parts,), jnp.float32, smallest / len(shards), largest / len(shards))
        level = level * jnp.repeat(jnp.exp(draws), shape[position] // parts).reshape((-1,) + (1,) * (len(shape) - 1 - position))
    return level


def profile(number_of, total, most, slope):
    portions = [(1 << 20) // math.isqrt(rank ** slope) + 1 for rank in range(2, number_of + 1)]
    surplus, holding = total - most - (number_of - 1), [1] * (number_of - 1)
    while surplus > 0:
        candidates = [i for i in range(number_of - 1) if holding[i] < most]
        pool, remaining = sum([portions[i] for i in candidates]), surplus
        for i in candidates:
            more = min(most - holding[i], max(1, remaining * portions[i] // pool), surplus)
            holding[i] = holding[i] + more
            surplus = surplus - more
    return np.array([most] + holding)


def ragged_sizes(own_key, count, total, reach, skew):
    if count == 2:
        one = jax.random.randint(own_key, (), max(1, total - reach), min(reach, total - 1) + 1)
        return jnp.stack([one, total - one])
    lengths = jnp.asarray(profile(count, total, reach, skew), jnp.int32)
    pairs = (count - 1) // 2
    source_of, receiver = lengths[1:1 + 2 * pairs:2], lengths[2:2 + 2 * pairs:2]
    slack = jnp.minimum(source_of - 1, reach - receiver)
    moved = jax.random.randint(jax.random.fold_in(own_key, 1), (pairs,), 0, 1 << 20) % (slack + 1)
    lengths = lengths.at[1:1 + 2 * pairs:2].set(source_of - moved).at[2:2 + 2 * pairs:2].set(receiver + moved)
    return lengths[jax.random.permutation(jax.random.fold_in(own_key, 2), count)]


def bell_draw(key, extent, scale, reach, shards=(), kind=jnp.bfloat16):
    entries = jax.random.normal(key, extent, jnp.float32) * scale
    if len(shards) > 0:
        entries = level_of(key, extent, shards, -0.22, 0.18) * entries
    return jnp.clip(entries, min=-reach, max=reach).astype(kind)


def setup_inputs(seed: int = 0) -> dict:
    streams_of = jax.random.split(jax.random.key(seed), 14)
    tokens = bell_draw(streams_of[0], (ROWS, SEQ, D), 1.0, 6.0, ((0, 16), (1, 2)))
    segments = jax.vmap(lambda own: jnp.searchsorted(jnp.cumsum(ragged_sizes(own, DOCS, SEQ, LONGEST, 0)), jnp.arange(SEQ), side="right"))(jax.random.split(streams_of[1], ROWS)).reshape((ROWS, SEQ)).astype(jnp.int32)
    w_qkv = bell_draw(streams_of[2], (D, 3 * D), D ** -0.5, 0.1875, ((0, 16),))
    qv_bias = bell_draw(streams_of[3], (2, D), 0.5, 3.0, ((1, 16),))
    w_out = bell_draw(streams_of[4], (D, D), (D // 16) ** -0.5, 0.75, ((0, 16),))
    out_bias = bell_draw(streams_of[5], (D,), 0.3, 2.0, ((0, 16),))
    w_in = bell_draw(streams_of[6], (D, FF), D ** -0.5, 0.1875, ((0, 16),))
    in_bias = bell_draw(streams_of[7], (FF,), 0.5, 3.0, ((0, 16),))
    w_down = bell_draw(streams_of[8], (FF, D), FF ** -0.5, 0.09375, ((0, 16),))
    down_bias = bell_draw(streams_of[9], (D,), 0.3, 2.0, ((0, 16),))
    gains = jnp.clip(1.0 + 0.1 * jax.random.normal(streams_of[10], (2, D), jnp.float32), 0.5, 1.5).astype(jnp.bfloat16)
    shifts = bell_draw(streams_of[11], (2, D), 0.2, 1.5, ((1, 16),))
    cotangent = bell_draw(streams_of[12], (ROWS, SEQ, D), 1.0, 6.0, ((0, 16), (1, 2)), jnp.float32)
    return dict(tokens=tokens, segments=segments, w_qkv=w_qkv, qv_bias=qv_bias, w_out=w_out, out_bias=out_bias, w_in=w_in, in_bias=in_bias, w_down=w_down, down_bias=down_bias, gains=gains, shifts=shifts, cotangent=cotangent)


@jax.custom_vjp
def low(v):
    return lax.optimization_barrier(v.astype(jnp.bfloat16)).astype(jnp.float32)

@jax.custom_vjp
def low_back(v):
    return v

def low_keep(v):
    return (low(v), None)

def low_pass(kept, grad):
    return (grad,)

def back_keep(v):
    return (v, None)

def back_low(kept, grad):
    return (low(grad),)
low.defvjp(low_keep, low_pass)
low_back.defvjp(back_keep, back_low)
HIGHEST_MODE = lax.Precision.HIGHEST
MASKED_SCORE = -1e+30

def layer_norm(value, gain, shift):
    center = value - lax.optimization_barrier(jnp.mean(value, axis=-1, keepdims=True))
    spread = lax.optimization_barrier(jnp.mean(center * center, axis=-1, keepdims=True))
    return center * lax.rsqrt(spread + 1e-06) * gain + shift

def gelu_exact(value):
    return 0.5 * value * (1.0 + lax.erf(value * 0.7071067811865476))

def forward(params, x_row, seg_row):
    w_qkv, qv_bias, w_out, out_bias, w_in, in_bias, w_down, down_bias, gains, shifts = params
    seq_len = x_row.shape[0]
    bias_row = jnp.concatenate([qv_bias[0], jnp.zeros_like(qv_bias[0]), qv_bias[1]])
    proj = jnp.dot(x_row, w_qkv, precision=HIGHEST_MODE) + bias_row
    proj = low_back(low(proj)).reshape(seq_len, 3, H, HD)
    query, keys_row, value = (proj[:, 0], proj[:, 1], proj[:, 2])
    raw = jnp.einsum('qhd,khd->hqk', query, keys_row, precision=HIGHEST_MODE) * HD ** (-0.5)
    same = seg_row[:, None] == seg_row[None, :]
    scores = low_back(jnp.where(same[None], raw, MASKED_SCORE))
    row_max = lax.optimization_barrier(jnp.max(scores, axis=-1, keepdims=True))
    exponent = jnp.exp(scores - row_max)
    weights = low(exponent / lax.optimization_barrier(jnp.sum(exponent, axis=-1, keepdims=True)))
    attended = jnp.einsum('hqk,khd->qhd', weights, value, precision=HIGHEST_MODE).reshape(seq_len, H * HD)
    attended = low_back(low(attended))
    branch = low_back(jnp.dot(attended, w_out, precision=HIGHEST_MODE) + out_bias)
    normed = layer_norm(x_row + branch, gains[0], shifts[0])
    hidden = low_back(jnp.dot(low(normed), w_in, precision=HIGHEST_MODE) + in_bias)
    active = low(gelu_exact(hidden))
    mixed = low_back(jnp.dot(active, w_down, precision=HIGHEST_MODE) + down_bias)
    return layer_norm(normed + mixed, gains[1], shifts[1])

def reference(tokens, segments, w_qkv, qv_bias, w_out, out_bias, w_in, in_bias, w_down, down_bias, gains, shifts, cotangent):
    params = tuple((item.astype(jnp.float32) for item in (w_qkv, qv_bias, w_out, out_bias, w_in, in_bias, w_down, down_bias, gains, shifts)))

    def row_step(totals, row):
        x_row, seg_row, cot_row = row

        def apply_row(p, x):
            return forward(p, x, seg_row)
        out_row, pullback = jax.vjp(apply_row, params, x_row.astype(jnp.float32))
        grad_params, grad_x = pullback(cot_row.astype(jnp.float32))
        totals = jax.tree.map(lambda a, b: a + b, totals, grad_params)
        return (totals, (out_row.astype(jnp.bfloat16), grad_x))
    zeros = jax.tree.map(jnp.zeros_like, params)
    totals, (outputs, grad_tokens) = lax.scan(row_step, zeros, (tokens, segments, cotangent))
    return (outputs, grad_tokens, totals[0], totals[1], totals[2], totals[3], totals[4], totals[5], totals[6], totals[7], totals[8], totals[9])
```

```python
import functools

import jax
import jax.numpy as jnp
from jax import lax
from jax.experimental import pallas as pl
from jax.experimental.pallas import tpu as pltpu
from jax.sharding import PartitionSpec as P

H = 16
HD = 64
PAIR = 2 * HD
FAR = -1e30
VMEM = 56 * 1024 * 1024
CORE, SIDE, NEAR, WIDE = 1, 2, 4, 8

F32 = jnp.float32
BF16 = jnp.bfloat16


def layer_norm(value, gain, shift):
    center = value - jnp.mean(value, axis=-1, keepdims=True)
    spread = jnp.mean(center * center, axis=-1, keepdims=True)
    return center * lax.rsqrt(spread + 1e-06) * gain + shift


def inner_left(left, right):
    return lax.dot_general(left, right, (((0,), (0,)), ((), ())), preferred_element_type=F32)


def inner_right(left, right):
    return lax.dot_general(left, right, (((1,), (1,)), ((), ())), preferred_element_type=F32)


def swap(value, axis, bit=1):
    return lax.ppermute(value, axis, [(i, i ^ bit) for i in range(lax.axis_size(axis))])


def by_side(own_is_first, own, other, axis):
    return jnp.where(
        own_is_first,
        jnp.concatenate([own, other], axis),
        jnp.concatenate([other, own], axis),
    )


def place():
    shard, ctx = lax.axis_index("shard"), lax.axis_index("ctx")
    return shard % 2, (shard // 2) % 2, (shard // 4) % 2, shard // 8, ctx


def assemble_body(depth, width, where_ref, *refs):
    pieces, out, sems = refs[:16], refs[16], refs[17]
    core, side, near, wide, ctx = (where_ref[i] for i in range(5))
    copies = []
    for index in range(16):
        part, far_core, second, first = index // 8, (index // 4) % 2, (index // 2) % 2, index % 2
        side_rel, ctx_rel = (first, second) if part == 0 else (second, first)
        column = ((core ^ far_core) * 2 + (ctx ^ ctx_rel)) * 2 + part
        for k in range(4):
            row = (((wide ^ (k % 2)) * 2 + (near ^ (k // 2))) * 2) + (side ^ side_rel)
            target = out.at[
                pl.ds(pl.multiple_of(row * depth, depth), depth),
                pl.ds(pl.multiple_of(column * width, width), width),
            ]
            copies.append(
                pltpu.make_async_copy(pieces[index].at[k], target, sems.at[index * 4 + k])
            )
    for copy in copies:
        copy.start()
    for copy in copies:
        copy.wait()


def gather_weight(shard, spot):
    rows, columns = shard.shape
    width = columns // 8
    core, side, near, wide, ctx = spot
    split = shard.reshape(rows, 8, width).transpose(1, 0, 2).reshape(2, 2, 2, rows, width)
    mine = lax.dynamic_index_in_dim(split, ctx, 1, False)
    own = lax.dynamic_index_in_dim(mine, core, 0, False)
    other = lax.dynamic_index_in_dim(mine, 1 - core, 0, False)
    chip = by_side(core == 0, own, swap(other, "shard", CORE), 1)
    pieces = []
    for part in range(2):
        held = chip[part][None]
        held = jnp.concatenate([held, swap(held, "shard", WIDE)], 0)
        held = jnp.concatenate([held, swap(held, "shard", NEAR)], 0)
        along = (("shard", SIDE), ("ctx", 1))
        first, second = along if part == 0 else along[::-1]
        near_side = [held, swap(held, *first)]
        near_side += [swap(item, *second) for item in near_side]
        pieces += near_side + [swap(item, "shard", CORE) for item in near_side]
    return pl.pallas_call(
        functools.partial(assemble_body, 2 * rows, width),
        out_shape=jax.ShapeDtypeStruct((16 * rows, columns), shard.dtype),
        in_specs=[pl.BlockSpec(memory_space=pltpu.SMEM)]
        + [pl.BlockSpec(memory_space=pl.ANY)] * 16,
        out_specs=pl.BlockSpec(memory_space=pl.ANY),
        scratch_shapes=[pltpu.SemaphoreType.DMA((64,))],
        cost_estimate=pl.CostEstimate(
            flops=0, bytes_accessed=64 * rows * columns, transcendentals=0
        ),
        name="assemble",
    )(jnp.stack(spot).astype(jnp.int32), *pieces)


def gather_small(flat):
    held = flat[None]
    for bit in (CORE, SIDE, NEAR, WIDE):
        held = jnp.concatenate([held, swap(held, "shard", bit)], 0)
    return pick_rows(held)


def pick_rows(held):
    count = held.shape[0]
    index = lax.iota(jnp.int32, count) ^ lax.axis_index("shard")
    choose = (index[:, None] == lax.iota(jnp.int32, count)[None, :]).astype(F32)
    return jnp.dot(choose, held.astype(F32), precision=lax.Precision.HIGHEST)


def product_body(chunks, parts, depth, width, adds, where_ref, left_ref, right_ref, *refs):
    out = refs[-1]
    side, near, wide, ctx = (where_ref[i] for i in range(1, 5))
    result = lax.dot_general(
        left_ref[...], right_ref[...], (((0,), (0,)), ((), ())), preferred_element_type=F32
    )
    for i in range(chunks):
        z, y = i // 2, i % 2
        if chunks == 1:
            row = 0
        else:
            row = (y ^ side) * 4 + ((z % 2) ^ near) * 2 + ((z // 2) ^ wide)
        for j in range(parts):
            piece = 0 if parts == 1 else ((j // 2) ^ ctx) * 2 + j % 2
            value = result[i * depth : (i + 1) * depth, j * width : (j + 1) * width]
            if adds:
                value = value + refs[0][piece, row].astype(F32)
            out[piece, row] = value.astype(out.dtype)


def product_pieces(left, right, spot, far_core, received=None):
    tokens, rows = left.shape
    columns = right.shape[1]
    depth, width = rows // 8, columns // 8
    by_rows = rows > columns or width % 256
    by_rows = rows >= columns
    chunks, parts = (1, 4) if by_rows else (8, 1)
    core = spot[0] ^ far_core
    where = jnp.stack([core, *spot[1:]]).astype(jnp.int32)

    def row_of(i, w):
        z, y = i // 2, i % 2
        return (y ^ w[1]) * 4 + ((z % 2) ^ w[2]) * 2 + ((z // 2) ^ w[3])

    if by_rows:
        grid = (8,)
        left_spec = pl.BlockSpec((tokens, depth), lambda i, w: (0, i))
        right_spec = pl.BlockSpec((tokens, 4 * width), lambda i, w: (0, w[0]))
        out_spec = pl.BlockSpec((4, 1, depth, width), lambda i, w: (0, row_of(i, w), 0, 0))
    else:
        grid = (4,)
        left_spec = pl.BlockSpec((tokens, rows), lambda j, w: (0, 0))
        right_spec = pl.BlockSpec((tokens, width), lambda j, w: (0, w[0] * 4 + j))
        out_spec = pl.BlockSpec(
            (1, 8, depth, width), lambda j, w: (((j // 2) ^ w[4]) * 2 + j % 2, 0, 0, 0)
        )
    adds = received is not None
    return pl.pallas_call(
        functools.partial(product_body, chunks, parts, depth, width, adds),
        grid_spec=pltpu.PrefetchScalarGridSpec(
            num_scalar_prefetch=1,
            grid=grid,
            in_specs=[left_spec, right_spec] + ([out_spec] if adds else []),
            out_specs=out_spec,
        ),
        out_shape=jax.ShapeDtypeStruct((4, 8, depth, width), BF16),
        compiler_params=pltpu.CompilerParams(vmem_limit_bytes=VMEM),
        cost_estimate=pl.CostEstimate(
            flops=tokens * rows * columns,
            bytes_accessed=2 * rows * columns,
            transcendentals=0,
        ),
        name="weight_gradient",
    )(where, left, right, *([received] if adds else []))


def add_low(left, right):
    return (left.astype(F32) + right.astype(F32)).astype(BF16)


def scatter_pieces(pieces, spot):
    depth, width = pieces.shape[2:]
    core, ctx = spot[0], spot[4]
    full = pieces.reshape(2, 2, 2, 2, 2, depth, width)
    parts = []
    for part in range(2):
        held = full[:, part]
        if part == 0:
            held = add_low(held[:, 0], swap(held[:, 1], "shard", SIDE))
            held = add_low(held[0], swap(held[1], "ctx"))
        else:
            held = add_low(held[0], swap(held[1], "ctx"))
            held = add_low(held[0], swap(held[1], "shard", SIDE))
        held = add_low(held[0], swap(held[1], "shard", NEAR))
        parts.append(add_low(held[0], swap(held[1], "shard", WIDE)))
    mine = jnp.stack(parts)
    half = by_side(ctx == 0, mine, swap(mine, "ctx"), 0)
    rows = depth // 2
    keep = lax.dynamic_slice_in_dim(half, core * rows, rows, 1)
    send = lax.dynamic_slice_in_dim(half, (1 - core) * rows, rows, 1)
    owned = by_side(core == 0, keep, swap(send, "shard", CORE), 0)
    return owned.transpose(1, 0, 2).reshape(rows, 8 * width).astype(F32)


def reduce_weight(left, right, spot):
    if spot is None:
        partial = inner_left(left, right).astype(BF16)
        owned = lax.psum_scatter(partial, "shard", scatter_dimension=0, tiled=True)
        return lax.psum(owned, "ctx").astype(F32)
    far = product_pieces(left, right, spot, 1)
    near = product_pieces(left, right, spot, 0, swap(far, "shard", CORE))
    return scatter_pieces(near, spot)


def reduce_small(table, spot):
    if spot is None:
        owned = lax.psum_scatter(table.astype(BF16), "shard", scatter_dimension=0, tiled=True)
        return lax.psum(owned, "ctx").astype(F32)[0]
    held = pick_rows(table)
    for bit in (WIDE, NEAR, SIDE, CORE):
        half = held.shape[0] // 2
        held = held[:half] + swap(held[half:].astype(BF16), "shard", bit).astype(F32)
    held = held.astype(BF16)
    return (held.astype(F32) + swap(held, "ctx").astype(F32))[0]


def head_lanes(shape, head):
    lane = lax.broadcasted_iota(jnp.int32, shape, 1)
    return (lane // HD) == head


def attend_body(part_len, proj_ref, mark_ref, veto_ref, out_ref, norm_ref):
    block = proj_ref[0]
    query, keys, value = (
        block[:part_len, :PAIR],
        block[:, PAIR : 2 * PAIR],
        block[:, 2 * PAIR :],
    )
    scaled = query * jnp.asarray(HD**-0.5, BF16)
    keys_marked = jnp.concatenate([keys, veto_ref[0]], 1)
    results, norms = [], []
    for head in range(2):
        alone = jnp.where(head_lanes(scaled.shape, head), scaled, jnp.zeros_like(scaled))
        scores = inner_right(keys_marked, jnp.concatenate([alone, mark_ref[0]], 1))
        top = jnp.max(scores, axis=0, keepdims=True)
        weights = jnp.exp(scores - top)
        total = jnp.sum(weights, axis=0, keepdims=True)
        result = inner_left(value, weights.astype(BF16))
        results.append(result[head * HD : (head + 1) * HD] * (1.0 / total))
        norms.append(top + jnp.log(total))
    out_ref[0] = jnp.concatenate(results, 0).T.astype(out_ref.dtype)
    norm_ref[0, 0] = jnp.concatenate(norms, 0)


def attend(proj, mark, veto):
    rows, seq_len, columns = proj.shape
    part_len = mark.shape[1]
    pairs = columns // (3 * PAIR)
    return pl.pallas_call(
        functools.partial(attend_body, part_len),
        grid=(rows, pairs),
        in_specs=[
            pl.BlockSpec((1, seq_len, 3 * PAIR), lambda r, j: (r, 0, j)),
            pl.BlockSpec((1, part_len, PAIR), lambda r, j: (r, 0, 0)),
            pl.BlockSpec((1, seq_len, PAIR), lambda r, j: (r, 0, 0)),
        ],
        out_specs=[
            pl.BlockSpec((1, part_len, PAIR), lambda r, j: (r, 0, j)),
            pl.BlockSpec((1, 1, 2, part_len), lambda r, j: (r, j, 0, 0)),
        ],
        out_shape=[
            jax.ShapeDtypeStruct((rows, part_len, pairs * PAIR), BF16),
            jax.ShapeDtypeStruct((rows, pairs, 2, part_len), F32),
        ],
        compiler_params=pltpu.CompilerParams(vmem_limit_bytes=VMEM),
        cost_estimate=pl.CostEstimate(
            flops=16 * rows * pairs * part_len * seq_len * PAIR,
            bytes_accessed=2 * rows * seq_len * columns,
            transcendentals=2 * rows * pairs * part_len * seq_len,
        ),
        name="attend",
    )(proj, mark, veto)


def attend_back_body(
    part_len, proj_ref, mark_ref, veto_ref, grad_ref, result_ref, norm_ref, out_ref
):
    block = proj_ref[0]
    seq_len = block.shape[0]
    query, keys, value = (
        block[:part_len, :PAIR],
        block[:, PAIR : 2 * PAIR],
        block[:, 2 * PAIR :],
    )
    scaled = query * jnp.asarray(HD**-0.5, BF16)
    keys_marked = jnp.concatenate([keys, veto_ref[0]], 1)
    grad = grad_ref[0]
    product = (grad.astype(F32) * result_ref[0].astype(F32)).T
    d_query, d_keys, d_value = [], None, None
    for head in range(2):
        lanes = head_lanes(scaled.shape, head)
        alone = jnp.where(lanes, scaled, jnp.zeros_like(scaled))
        grad_alone = jnp.where(lanes, grad, jnp.zeros_like(grad))
        scores = inner_right(keys_marked, jnp.concatenate([alone, mark_ref[0]], 1))
        weights = jnp.exp(scores - norm_ref[0, 0, head : head + 1, :])
        d_weights = inner_right(value, grad_alone)
        inner = jnp.sum(product[head * HD : (head + 1) * HD], axis=0, keepdims=True)
        d_scores = (weights * (d_weights - inner)).astype(BF16)
        more_value = jnp.dot(weights.astype(BF16), grad_alone, preferred_element_type=F32)
        more_keys = jnp.dot(d_scores, alone, preferred_element_type=F32)
        d_value = more_value if d_value is None else d_value + more_value
        d_keys = more_keys if d_keys is None else d_keys + more_keys
        d_query.append(inner_left(keys, d_scores)[head * HD : (head + 1) * HD])
    out_ref[0, :part_len, :PAIR] = (jnp.concatenate(d_query, 0).T * HD**-0.5).astype(BF16)
    if seq_len > part_len:
        out_ref[0, part_len:, :PAIR] = jnp.zeros((seq_len - part_len, PAIR), BF16)
    out_ref[0, :, PAIR : 2 * PAIR] = d_keys.astype(BF16)
    out_ref[0, :, 2 * PAIR :] = d_value.astype(BF16)


def attend_back(proj, mark, veto, grad, result, norm):
    rows, seq_len, columns = proj.shape
    part_len = mark.shape[1]
    pairs = columns // (3 * PAIR)
    mine = pl.BlockSpec((1, part_len, PAIR), lambda r, j: (r, 0, j))
    return pl.pallas_call(
        functools.partial(attend_back_body, part_len),
        grid=(rows, pairs),
        in_specs=[
            pl.BlockSpec((1, seq_len, 3 * PAIR), lambda r, j: (r, 0, j)),
            pl.BlockSpec((1, part_len, PAIR), lambda r, j: (r, 0, 0)),
            pl.BlockSpec((1, seq_len, PAIR), lambda r, j: (r, 0, 0)),
            mine,
            mine,
            pl.BlockSpec((1, 1, 2, part_len), lambda r, j: (r, j, 0, 0)),
        ],
        out_specs=pl.BlockSpec((1, seq_len, 3 * PAIR), lambda r, j: (r, 0, j)),
        out_shape=jax.ShapeDtypeStruct(proj.shape, BF16),
        compiler_params=pltpu.CompilerParams(vmem_limit_bytes=VMEM),
        cost_estimate=pl.CostEstimate(
            flops=40 * rows * pairs * part_len * seq_len * PAIR,
            bytes_accessed=4 * rows * seq_len * columns,
            transcendentals=2 * rows * pairs * part_len * seq_len,
        ),
        name="attend_back",
    )(proj, mark, veto, grad, result, norm)


def own_first(value, axis):
    if lax.axis_size("ctx") == 2:
        return jnp.concatenate([value, swap(value, "ctx")], axis)
    whole = lax.all_gather(value, "ctx", axis=axis, tiled=True)
    return jnp.roll(whole, -lax.axis_index("ctx") * value.shape[axis], axis)


def sum_to_owners(value, own_len):
    own = value[:, :own_len].astype(F32)
    if lax.axis_size("ctx") == 2:
        return own + swap(value[:, own_len:].astype(BF16), "ctx").astype(F32)
    whole = jnp.roll(value, lax.axis_index("ctx") * own_len, 1).astype(BF16)
    return lax.psum_scatter(whole, "ctx", scatter_dimension=1, tiled=True).astype(F32)


def on_device(
    tokens,
    segments,
    w_qkv,
    qv_bias,
    w_out,
    out_bias,
    w_in,
    in_bias,
    w_down,
    down_bias,
    gains,
    shifts,
    cotangent,
):
    staged = lax.axis_size("shard") == 16 and lax.axis_size("ctx") == 2
    spot = place() if staged else None
    row_count, part_len, width = tokens.shape
    owned_rows = w_qkv.shape[0]
    pairs = H // 2
    token_count = row_count * part_len

    def gather(shard):
        if spot is None:
            return lax.all_gather(shard, "shard", axis=0, tiled=True)
        return gather_weight(shard, spot)

    w_pairs = (
        w_qkv.reshape(owned_rows, 3, pairs, PAIR).transpose(0, 2, 1, 3).reshape(w_qkv.shape)
    )
    small = [qv_bias, out_bias, in_bias, down_bias, gains, shifts]
    sizes = [item.size for item in small]
    flat = jnp.concatenate([item.reshape(-1) for item in small])
    if spot is None:
        table = lax.all_gather(flat, "shard", axis=0).astype(F32)
    else:
        table = gather_small(flat)
    pieces = jnp.split(table, [sum(sizes[:i]) for i in range(1, len(sizes))], axis=1)

    def two(piece):
        return piece.reshape(-1, 2, owned_rows).transpose(1, 0, 2).reshape(2, width)

    qv_all, gain_all, shift_all = two(pieces[0]), two(pieces[4]), two(pieces[5])
    out_all, in_all, down_all = (pieces[i].reshape(-1) for i in (1, 2, 3))

    tokens_row = own_first(tokens, 1)
    segments_row = own_first(segments, 1)
    seq_len = tokens_row.shape[1]
    lanes = lax.iota(jnp.int32, PAIR)
    mark = (segments[:, :, None] == lanes).astype(BF16)
    veto = jnp.where(segments_row[:, :, None] == lanes, 0.0, FAR).astype(BF16)

    w_qkv_all = gather(w_pairs)
    w_out_all = gather(w_out)
    w_in_all = gather(w_in)
    w_down_all = gather(w_down)

    flat_row = tokens_row.reshape(row_count * seq_len, width)
    bias_row = jnp.stack(
        [qv_all[0].reshape(pairs, PAIR), jnp.zeros((pairs, PAIR), F32), qv_all[1].reshape(pairs, PAIR)],
        1,
    ).reshape(-1)
    proj = (jnp.dot(flat_row, w_qkv_all, preferred_element_type=F32) + bias_row).astype(BF16)
    proj = proj.reshape(row_count, seq_len, 3 * width)
    attended_rows, norm = attend(proj, mark, veto)
    attended = attended_rows.reshape(token_count, width)
    residual_in = tokens.reshape(token_count, width).astype(F32)
    branch = jnp.dot(attended, w_out_all, preferred_element_type=F32) + out_all
    normed, pull_first = jax.vjp(layer_norm, residual_in + branch, gain_all[0], shift_all[0])
    normed_low = normed.astype(BF16)
    hidden = jnp.dot(normed_low, w_in_all, preferred_element_type=F32) + in_all
    below = 0.5 * (1.0 + lax.erf(hidden * 0.7071067811865476))
    active = (hidden * below).astype(BF16)
    slope = (below + hidden * 0.3989422804014327 * jnp.exp(-0.5 * hidden * hidden)).astype(BF16)
    mixed = jnp.dot(active, w_down_all, preferred_element_type=F32) + down_all
    result_f, pull_second = jax.vjp(layer_norm, normed + mixed, gain_all[1], shift_all[1])
    outputs = result_f.astype(BF16).reshape(row_count, part_len, width)
    d_second, gain_second, shift_second = pull_second(cotangent.reshape(token_count, width))
    d_mixed = d_second.astype(BF16)
    grad_w_down = reduce_weight(active, d_mixed, spot)
    d_hidden = (inner_right(d_mixed, w_down_all) * slope.astype(F32)).astype(BF16)
    grad_w_in = reduce_weight(normed_low, d_hidden, spot)
    d_normed = d_second + inner_right(d_hidden, w_in_all)
    d_first, gain_first, shift_first = pull_first(d_normed)
    d_branch = d_first.astype(BF16)
    grad_w_out = reduce_weight(attended, d_branch, spot)
    d_attended = inner_right(d_branch, w_out_all).astype(BF16)
    d_proj = attend_back(
        proj, mark, veto, d_attended.reshape(attended_rows.shape), attended_rows, norm
    )
    flat_d = d_proj.reshape(row_count * seq_len, 3 * width)
    d_tokens = inner_right(flat_d, w_qkv_all).reshape(row_count, seq_len, width)
    grad_tokens = d_first.reshape(row_count, part_len, width) + sum_to_owners(d_tokens, part_len)
    grad_pairs = reduce_weight(flat_row, flat_d, spot)
    grad_w_qkv = (
        grad_pairs.reshape(owned_rows, pairs, 3, PAIR).transpose(0, 2, 1, 3).reshape(w_qkv.shape)
    )

    def column_sum(value):
        return jnp.sum(value.astype(F32), axis=0)

    d_bias = column_sum(flat_d).reshape(pairs, 3, PAIR)
    shards = lax.axis_size("shard")

    def owners(*vectors):
        stacked = jnp.stack(vectors).reshape(len(vectors), shards, -1)
        return stacked.transpose(1, 0, 2).reshape(shards, -1)

    sums = jnp.concatenate(
        [
            owners(d_bias[:, 0].reshape(-1), d_bias[:, 2].reshape(-1)),
            owners(column_sum(d_branch)),
            owners(column_sum(d_hidden)),
            owners(column_sum(d_mixed)),
            owners(gain_first, gain_second),
            owners(shift_first, shift_second),
        ],
        axis=1,
    )
    owned = jnp.split(
        reduce_small(sums, spot), [sum(sizes[:i]) for i in range(1, len(sizes))]
    )
    return (
        outputs,
        grad_tokens,
        grad_w_qkv,
        owned[0].reshape(qv_bias.shape),
        grad_w_out,
        owned[1],
        grad_w_in,
        owned[2],
        grad_w_down,
        owned[3],
        owned[4].reshape(gains.shape),
        owned[5].reshape(shifts.shape),
    )


def solution(mesh):
    row, flat = P("shard", None), P("shard")
    wide, whole = P(None, "shard"), P("shard", "ctx", None)
    return jax.shard_map(
        on_device,
        mesh=mesh,
        in_specs=(
            whole,
            P("shard", "ctx"),
            row,
            wide,
            row,
            flat,
            row,
            flat,
            row,
            flat,
            wide,
            wide,
            whole,
        ),
        out_specs=(whole, whole, row, wide, row, flat, row, flat, row, flat, wide, wide),
        check_vma=False,
    )
```

```python
import functools

import jax
import jax.numpy as jnp
from jax import lax
from jax.experimental import pallas as pl
from jax.experimental.pallas import tpu as pltpu
from jax.sharding import PartitionSpec as P

H = 16
HD = 64
PAIR = 2 * HD
FAR = -1e30
LIGHT = pl.CostEstimate(flops=0, bytes_accessed=0, transcendentals=0)
VMEM = 56 * 1024 * 1024
CORE, SIDE, NEAR, WIDE = 1, 2, 4, 8

F32 = jnp.float32
BF16 = jnp.bfloat16


def inner_left(left, right):
    return lax.dot_general(left, right, (((0,), (0,)), ((), ())), preferred_element_type=F32)


def inner_right(left, right):
    return lax.dot_general(left, right, (((1,), (1,)), ((), ())), preferred_element_type=F32)


def swap(value, axis, bit=1):
    return lax.ppermute(value, axis, [(i, i ^ bit) for i in range(lax.axis_size(axis))])


def by_side(own_is_first, own, other, axis):
    return jnp.where(
        own_is_first,
        jnp.concatenate([own, other], axis),
        jnp.concatenate([other, own], axis),
    )


def place():
    shard, ctx = lax.axis_index("shard"), lax.axis_index("ctx")
    return shard % 2, (shard // 2) % 2, (shard // 4) % 2, shard // 8, ctx


def assemble_body(depth, width, where_ref, *refs):
    pieces, out, sems = refs[:2], refs[2], refs[3]
    core, side, near, wide, ctx = (where_ref[i] for i in range(5))
    copies = []
    for index in range(16):
        far_core, part, second, first = index // 8, (index // 4) % 2, (index // 2) % 2, index % 2
        side_rel, ctx_rel = (first, second) if part == 0 else (second, first)
        column = ((core ^ far_core) * 2 + (ctx ^ ctx_rel)) * 2 + part
        for k in range(4):
            row = (((wide ^ (k % 2)) * 2 + (near ^ (k // 2))) * 2) + (side ^ side_rel)
            target = out.at[
                pl.ds(pl.multiple_of(row * depth, depth), depth),
                pl.ds(pl.multiple_of(column * width, width), width),
            ]
            source = pieces[far_core].at[index % 8 * 4 + k]
            copies.append(pltpu.make_async_copy(source, target, sems.at[len(copies)]))
    for copy in copies:
        copy.start()
    for copy in copies:
        copy.wait()


def gather_pairwise(shard, spot):
    rows, columns = shard.shape
    width = columns // 8
    core, side, near, wide, ctx = spot
    split = shard.reshape(rows, 8, width).transpose(1, 0, 2).reshape(2, 2, 2, rows, width)
    mine = lax.dynamic_index_in_dim(split, ctx, 1, False)
    own = lax.dynamic_index_in_dim(mine, core, 0, False)
    other = lax.dynamic_index_in_dim(mine, 1 - core, 0, False)
    held = by_side(core == 0, own, swap(other, "shard", CORE), 1)[None]
    for bit in (WIDE, NEAR):
        held = jnp.concatenate([held, swap(held, "shard", bit)], 0)
    begun = held
    held = [held[:, 0], held[:, 1]]
    along = (("shard", SIDE), ("ctx", 1))
    for routes in (along, along[::-1]):
        held = [
            jnp.concatenate([value, swap(value, *route)], 0)
            for value, route in zip(held, routes, strict=True)
        ]
    here = jnp.concatenate(held, 0)
    whole = pl.pallas_call(
        functools.partial(assemble_body, 2 * rows, width),
        out_shape=jax.ShapeDtypeStruct((16 * rows, columns), BF16),
        in_specs=[pl.BlockSpec(memory_space=pltpu.SMEM)]
        + [pl.BlockSpec(memory_space=pl.ANY)] * 2,
        out_specs=pl.BlockSpec(memory_space=pltpu.VMEM),
        scratch_shapes=[pltpu.SemaphoreType.DMA((64,))],
        compiler_params=pltpu.CompilerParams(vmem_limit_bytes=VMEM),
        cost_estimate=LIGHT,
        name="assemble",
    )(jnp.stack(spot).astype(jnp.int32), here, swap(here, "shard", CORE))
    return whole, begun


def gather_small(flat):
    held = flat[None]
    for bit in (CORE, SIDE, NEAR, WIDE):
        held = jnp.concatenate([held, swap(held, "shard", bit)], 0)
    return pick_rows(held)


def pick_rows(held):
    count = held.shape[0]
    index = lax.iota(jnp.int32, count) ^ lax.axis_index("shard")
    choose = (index[:, None] == lax.iota(jnp.int32, count)[None, :]).astype(F32)
    return jnp.dot(choose, held.astype(F32), precision=lax.Precision.HIGHEST)


def product_body(depth, beside, adds, where_ref, left_ref, right_ref, *refs):
    out = refs[-1]
    side, near, wide = (where_ref[i] for i in range(1, 4))
    result = inner_left(left_ref[...], right_ref[...])
    if beside:
        result = jnp.concatenate([result, inner_left(refs[0][...], refs[1][...])], 1)
    for i in range(8):
        z, y = i // 2, i % 2
        row = (y ^ side) * 4 + ((z % 2) ^ near) * 2 + ((z // 2) ^ wide)
        value = result[i * depth : (i + 1) * depth]
        if adds:
            value = value + refs[-2][0, row].astype(F32)
        out[0, row] = value.astype(out.dtype)


def product_pieces(left, right, spot, far, received=None, beside=()):
    tokens, rows = left.shape
    depth = rows // 8
    pairs = [(left, right), *([beside] if beside else [])]
    specs, full = [], 0
    for one, two in pairs:
        width = two.shape[1] // 4
        full += width
        specs += [
            pl.BlockSpec(one.shape, lambda j, w: (0, 0)),
            pl.BlockSpec((two.shape[0], width), lambda j, w: (0, (w[0] ^ far) * 2 + (w[4] ^ j))),
        ]
    out_spec = pl.BlockSpec((1, 8, depth, full), lambda j, w: (j, 0, 0, 0))
    adds = received is not None
    return pl.pallas_call(
        functools.partial(product_body, depth, bool(beside), adds),
        grid_spec=pltpu.PrefetchScalarGridSpec(
            num_scalar_prefetch=1,
            grid=(2,),
            in_specs=specs + ([out_spec] if adds else []),
            out_specs=out_spec,
        ),
        out_shape=jax.ShapeDtypeStruct((2, 8, depth, full), BF16),
        compiler_params=pltpu.CompilerParams(vmem_limit_bytes=VMEM),
        cost_estimate=LIGHT,
        name="weight_gradient",
    )(jnp.stack(spot).astype(jnp.int32), left, right, *beside, *([received] if adds else []))


def add_low(left, right):
    return (left.astype(F32) + right.astype(F32)).astype(BF16)


def scatter_steps(pieces, spot, ctx_first=False):
    depth, width = pieces.shape[-2:]
    core, ctx = spot[0], spot[4]
    full = pieces.reshape(2, 2, 2, 2, depth, width)

    def meet(dep, left, arrived):
        arrived = lax.optimization_barrier((arrived, dep))[0] if dep is not None else arrived
        return add_low(left, arrived)

    keep, sent = (full[0], full[1]) if ctx_first else (full[:, 0], full[:, 1])
    routes = (("shard", SIDE), ("ctx", 1))
    routes = routes[::-1] if ctx_first else routes
    for route in (*routes, ("shard", NEAR), ("shard", WIDE)):
        dep = yield sent
        held = meet(dep, keep, swap(sent, *route))
        keep, sent = held[0], held[1] if held.ndim > 2 else None
    yield held
    held = held[None]
    half = by_side(ctx == 0, held, swap(held, "ctx"), 0)
    rows = depth // 2
    kept = lax.dynamic_slice_in_dim(half, core * rows, rows, 1)
    send = lax.dynamic_slice_in_dim(half, (1 - core) * rows, rows, 1)
    yield by_side(core == 0, kept, swap(send, "shard", CORE), 0)


def owned_rows_of(pieces):
    count, rows, width = pieces.shape
    return pieces.transpose(1, 0, 2).reshape(rows, count * width).astype(F32)


def reduce_partial(partial, spot, late=None):
    owned = lax.psum_scatter(partial, "shard", scatter_dimension=0, tiled=True)
    if spot is None:
        return lax.psum(owned, "ctx").astype(F32)
    owned = owned if late is None else after(owned, late)
    return owned.astype(F32) + swap(owned, "ctx").astype(F32)


def after(value, *others):
    return lax.optimization_barrier((value, *others))[0]


def reduce_small(table, spot):
    if spot is None:
        owned = lax.psum_scatter(table.astype(BF16), "shard", scatter_dimension=0, tiled=True)
        return lax.psum(owned, "ctx").astype(F32)[0]
    held = pick_rows(table)
    for bit in (WIDE, NEAR, SIDE, CORE):
        half = held.shape[0] // 2
        held = held[:half] + swap(held[half:].astype(BF16), "shard", bit).astype(F32)
    held = held.astype(BF16)
    return (held.astype(F32) + swap(held, "ctx").astype(F32))[0]


def head_lanes(shape, head):
    lane = lax.broadcasted_iota(jnp.int32, shape, 1)
    return (lane // HD) == head


def attend_body(part_len, proj_ref, mark_ref, veto_ref, out_ref, norm_ref):
    block = proj_ref[0]
    query, keys, value = (
        block[:part_len, :PAIR],
        block[:, PAIR : 2 * PAIR],
        block[:, 2 * PAIR :],
    )
    scaled = query * jnp.asarray(HD**-0.5, BF16)
    keys_marked = jnp.concatenate([keys, veto_ref[0]], 1)
    results, norms = [], []
    for head in range(2):
        alone = jnp.where(head_lanes(scaled.shape, head), scaled, jnp.zeros_like(scaled))
        scores = inner_right(keys_marked, jnp.concatenate([alone, mark_ref[0]], 1))
        top = jnp.max(scores, axis=0, keepdims=True)
        weights = jnp.exp(scores - top)
        total = jnp.sum(weights, axis=0, keepdims=True)
        result = inner_left(value, weights.astype(BF16))
        results.append(result[head * HD : (head + 1) * HD] * (1.0 / total))
        norms.append(top + jnp.log(total))
    out_ref[0] = jnp.concatenate(results, 0).T.astype(out_ref.dtype)
    norm_ref[0, 0] = jnp.concatenate(norms, 0)


def attend(proj, mark, veto):
    rows, seq_len, columns = proj.shape
    part_len = mark.shape[1]
    pairs = columns // (3 * PAIR)
    return pl.pallas_call(
        functools.partial(attend_body, part_len),
        grid=(rows, pairs),
        in_specs=[
            pl.BlockSpec((1, seq_len, 3 * PAIR), lambda r, j: (r, 0, j)),
            pl.BlockSpec((1, part_len, PAIR), lambda r, j: (r, 0, 0)),
            pl.BlockSpec((1, seq_len, PAIR), lambda r, j: (r, 0, 0)),
        ],
        out_specs=[
            pl.BlockSpec((1, part_len, PAIR), lambda r, j: (r, 0, j)),
            pl.BlockSpec((1, 1, 2, part_len), lambda r, j: (r, j, 0, 0)),
        ],
        out_shape=[
            jax.ShapeDtypeStruct((rows, part_len, pairs * PAIR), BF16),
            jax.ShapeDtypeStruct((rows, pairs, 2, part_len), F32),
        ],
        compiler_params=pltpu.CompilerParams(vmem_limit_bytes=VMEM),
        cost_estimate=LIGHT,
        name="attend",
    )(proj, mark, veto)


def attend_back_body(
    part_len, proj_ref, mark_ref, veto_ref, grad_ref, result_ref, norm_ref, out_ref
):
    block = proj_ref[0]
    seq_len = block.shape[0]
    query, keys, value = (
        block[:part_len, :PAIR],
        block[:, PAIR : 2 * PAIR],
        block[:, 2 * PAIR :],
    )
    scaled = query * jnp.asarray(HD**-0.5, BF16)
    keys_marked = jnp.concatenate([keys, veto_ref[0]], 1)
    grad = grad_ref[0]
    product = (grad.astype(F32) * result_ref[0].astype(F32)).T
    d_query, d_keys, d_value = [], None, None
    for head in range(2):
        lanes = head_lanes(scaled.shape, head)
        alone = jnp.where(lanes, scaled, jnp.zeros_like(scaled))
        grad_alone = jnp.where(lanes, grad, jnp.zeros_like(grad))
        scores = inner_right(keys_marked, jnp.concatenate([alone, mark_ref[0]], 1))
        weights = jnp.exp(scores - norm_ref[0, 0, head : head + 1, :])
        d_weights = inner_right(value, grad_alone)
        inner = jnp.sum(product[head * HD : (head + 1) * HD], axis=0, keepdims=True)
        d_scores = (weights * (d_weights - inner)).astype(BF16)
        more_value = jnp.dot(weights.astype(BF16), grad_alone, preferred_element_type=F32)
        more_keys = jnp.dot(d_scores, alone, preferred_element_type=F32)
        d_value = more_value if d_value is None else d_value + more_value
        d_keys = more_keys if d_keys is None else d_keys + more_keys
        d_query.append(inner_left(keys, d_scores)[head * HD : (head + 1) * HD])
    out_ref[0, :part_len, :PAIR] = (jnp.concatenate(d_query, 0).T * HD**-0.5).astype(BF16)
    if seq_len > part_len:
        out_ref[0, part_len:, :PAIR] = jnp.zeros((seq_len - part_len, PAIR), BF16)
    out_ref[0, :, PAIR : 2 * PAIR] = d_keys.astype(BF16)
    out_ref[0, :, 2 * PAIR :] = d_value.astype(BF16)


def attend_back(part, proj, mark, veto, grad, result, norm):
    rows, seq_len, columns = proj.shape
    part_len = mark.shape[1]
    pairs = columns // (3 * PAIR) // 2
    own = pl.BlockSpec((1, part_len, PAIR), lambda r, j: (r, 0, part * pairs + j))
    return pl.pallas_call(
        functools.partial(attend_back_body, part_len),
        grid=(rows, pairs),
        in_specs=[
            pl.BlockSpec((1, seq_len, 3 * PAIR), lambda r, j: (r, 0, part * pairs + j)),
            pl.BlockSpec((1, part_len, PAIR), lambda r, j: (r, 0, 0)),
            pl.BlockSpec((1, seq_len, PAIR), lambda r, j: (r, 0, 0)),
            own,
            own,
            pl.BlockSpec((1, 1, 2, part_len), lambda r, j: (r, part * pairs + j, 0, 0)),
        ],
        out_specs=pl.BlockSpec((1, seq_len, 3 * PAIR), lambda r, j: (r, 0, j)),
        out_shape=jax.ShapeDtypeStruct((rows, seq_len, columns // 2), BF16),
        compiler_params=pltpu.CompilerParams(vmem_limit_bytes=VMEM),
        cost_estimate=LIGHT,
        name="attend_back",
    )(proj, mark, veto, grad, result, norm)


CUTS = 4


def cuts(rows):
    step = rows // CUTS
    return [slice(i * step, (i + 1) * step) for i in range(CUTS)]


def mean_of(value):
    return jnp.mean(value, axis=-1, keepdims=True)


def normalise(value):
    center = value - mean_of(value)
    scale = lax.rsqrt(mean_of(center * center) + 1e-06)
    return center * scale, scale


def normalise_back(unit, scale, incoming, gain):
    edge = incoming * gain
    return scale * (edge - mean_of(edge) - unit * mean_of(edge * unit))


def total(value):
    return jnp.sum(value, axis=0, keepdims=True)


def whole_block(shape):
    return pl.BlockSpec(shape, lambda *_: (0,) * len(shape))


def down_block(packed):
    shards, rows, width = packed.shape
    return pl.BlockSpec((shards // 4, rows // 9 * 4, width), lambda k: (k, 0, 0))


def in_block(packed):
    shards, rows, width = packed.shape
    return pl.BlockSpec((shards, rows // 9, width), lambda k: (0, 4 + k, 0))


def out_block(packed):
    shards, rows, width = packed.shape
    return pl.BlockSpec((shards, rows // 9, width), lambda *_: (0, 8, 0))


def square(ref):
    return ref[...].reshape(-1, ref.shape[-1])


def kernel(body, grid, name, in_specs, outs, out_specs, scratch=()):
    return pl.pallas_call(
        body,
        grid=grid,
        in_specs=in_specs,
        out_shape=[jax.ShapeDtypeStruct(*out) for out in outs],
        out_specs=out_specs,
        scratch_shapes=scratch,
        compiler_params=pltpu.CompilerParams(vmem_limit_bytes=VMEM),
        cost_estimate=LIGHT,
        name=name,
    )


def first_norm_body(attended, tokens, weight, bias, gain, shift, unit, scale, low):
    matrix = square(weight)
    for cut in cuts(attended.shape[0]):
        branch = jnp.dot(attended[cut], matrix, preferred_element_type=F32) + bias[...]
        u, r = normalise(tokens[cut].astype(F32) + branch)
        unit[cut] = u
        scale[cut] = jnp.broadcast_to(r, (r.shape[0], PAIR))
        low[cut] = (u * gain[...] + shift[...]).astype(BF16)


def first_norm(attended, tokens, packed, bias, gain, shift):
    count, width = tokens.shape
    row, flat = whole_block((count, width)), whole_block((1, width))
    narrow = whole_block((count, PAIR))
    return kernel(
        first_norm_body,
        (1,),
        "first_norm",
        [row, row, out_block(packed), flat, flat, flat],
        [((count, width), F32), ((count, PAIR), F32), ((count, width), BF16)],
        [row, narrow, row],
    )(attended, tokens, packed, bias, gain, shift)


def hidden_body(low, weight, bias, active, slope):
    matrix = square(weight)
    for cut in cuts(low.shape[0]):
        hidden = jnp.dot(low[cut], matrix, preferred_element_type=F32) + bias[...]
        below = 0.5 * (1.0 + lax.erf(hidden * 0.7071067811865476))
        active[cut] = (hidden * below).astype(BF16)
        bell = 0.3989422804014327 * jnp.exp(-0.5 * hidden * hidden)
        slope[cut] = (below + hidden * bell).astype(BF16)


def hidden_layer(low, packed, bias):
    count, width = low.shape
    column = pl.BlockSpec((count, width), lambda k: (0, k))
    return kernel(
        hidden_body,
        (4,),
        "hidden_layer",
        [whole_block(low.shape), in_block(packed), pl.BlockSpec((1, width), lambda k: (0, k))],
        [((count, 4 * width), BF16)] * 2,
        [column] * 2,
    )(low, packed, bias)


def second_norm_body(
    active, weight, bias, unit, vectors, cotangent, outputs, second, low, sums, held
):
    step = pl.program_id(0)
    more = jnp.dot(active[...], square(weight), preferred_element_type=F32)

    @pl.when(step == 0)
    def _():
        held[...] = more

    @pl.when(step > 0)
    def _():
        held[...] += more

    @pl.when(step == pl.num_programs(0) - 1)
    def _():
        gain_one, shift_one, gain, shift = (vectors[i : i + 1] for i in range(4))
        totals = []
        for cut in cuts(held.shape[0]):
            normed = unit[cut] * gain_one + shift_one
            u, r = normalise(normed + held[cut] + bias[...])
            outputs[cut] = (u * gain + shift).astype(BF16)
            incoming = cotangent[cut]
            back = normalise_back(u, r, incoming, gain)
            second[cut] = back
            low[cut] = back.astype(BF16)
            totals.append((total(incoming * u), total(incoming), total(low[cut].astype(F32))))
        sums[...] = jnp.concatenate([sum(item) for item in zip(*totals, strict=True)], 0)


def second_norm(active, packed, bias, unit, vectors, cotangent):
    count, width = unit.shape
    row = whole_block((count, width))
    return kernel(
        second_norm_body,
        (4,),
        "second_norm",
        [
            pl.BlockSpec((count, width), lambda k: (0, k)),
            down_block(packed),
            whole_block((1, width)),
            row,
            whole_block((4, width)),
            row,
        ],
        [((count, width), BF16), ((count, width), F32), ((count, width), BF16), ((3, width), F32)],
        [row, row, row, whole_block((3, width))],
        [pltpu.VMEM((count, width), F32)],
    )(active, packed, bias, unit, vectors, cotangent)


def hidden_back_body(low, weight, slope, d_hidden, sums):
    matrix = square(weight)
    totals = []
    for cut in cuts(low.shape[0]):
        grad = (inner_right(low[cut], matrix) * slope[cut].astype(F32)).astype(BF16)
        d_hidden[cut] = grad
        totals.append(total(grad.astype(F32)))
    sums[...] = sum(totals)


def hidden_back(low, packed, slope):
    count, width = low.shape
    column = pl.BlockSpec((count, width), lambda k: (0, k))
    return kernel(
        hidden_back_body,
        (4,),
        "hidden_back",
        [whole_block(low.shape), down_block(packed), column],
        [((count, 4 * width), BF16), ((1, 4 * width), F32)],
        [column, pl.BlockSpec((1, width), lambda k: (0, k))],
    )(low, packed, slope)


def first_back_body(
    d_hidden, weight, last, second, unit, scale, gain, first, low, d_attended, sums, held
):
    step = pl.program_id(0)
    more = inner_right(d_hidden[...], square(weight))

    @pl.when(step == 0)
    def _():
        held[...] = second[...] + more

    @pl.when(step > 0)
    def _():
        held[...] += more

    @pl.when(step == pl.num_programs(0) - 1)
    def _():
        matrix = square(last)
        totals = []
        for cut in cuts(held.shape[0]):
            incoming, u = held[cut], unit[cut]
            back = normalise_back(u, scale[cut][:, :1], incoming, gain[...])
            first[cut] = back
            low[cut] = back.astype(BF16)
            d_attended[cut] = inner_right(low[cut], matrix).astype(BF16)
            totals.append((total(incoming * u), total(incoming), total(low[cut].astype(F32))))
        sums[...] = jnp.concatenate([sum(item) for item in zip(*totals, strict=True)], 0)


def first_back(d_hidden, packed, second, unit, scale, gain):
    count, width = unit.shape
    row = whole_block((count, width))
    return kernel(
        first_back_body,
        (4,),
        "first_back",
        [
            pl.BlockSpec((count, width), lambda k: (0, k)),
            in_block(packed),
            out_block(packed),
            row,
            row,
            whole_block((count, PAIR)),
            whole_block((1, width)),
        ],
        [((count, width), F32), ((count, width), BF16), ((count, width), BF16), ((3, width), F32)],
        [row, row, row, whole_block((3, width))],
        [pltpu.VMEM((count, width), F32)],
    )(d_hidden, packed, packed, second, unit, scale, gain)


def own_first(value, axis):
    if lax.axis_size("ctx") == 2:
        return jnp.concatenate([value, swap(value, "ctx")], axis)
    whole = lax.all_gather(value, "ctx", axis=axis, tiled=True)
    return jnp.roll(whole, -lax.axis_index("ctx") * value.shape[axis], axis)


def sum_to_owners(value, own_len):
    own = value[:, :own_len].astype(F32)
    if lax.axis_size("ctx") == 2:
        return own + swap(value[:, own_len:].astype(BF16), "ctx").astype(F32)
    whole = jnp.roll(value, lax.axis_index("ctx") * own_len, 1).astype(BF16)
    return lax.psum_scatter(whole, "ctx", scatter_dimension=1, tiled=True).astype(F32)


def on_device(
    tokens,
    segments,
    w_qkv,
    qv_bias,
    w_out,
    out_bias,
    w_in,
    in_bias,
    w_down,
    down_bias,
    gains,
    shifts,
    cotangent,
):
    staged = lax.axis_size("shard") == 16 and lax.axis_size("ctx") == 2
    spot = place() if staged else None
    row_count, part_len, width = tokens.shape
    owned_rows = w_qkv.shape[0]
    pairs = H // 2
    token_count = row_count * part_len

    w_pairs = (
        w_qkv.reshape(owned_rows, 3, pairs, PAIR).transpose(0, 2, 1, 3).reshape(w_qkv.shape)
    )
    small = [qv_bias, out_bias, in_bias, down_bias, gains, shifts]
    sizes = [item.size for item in small]
    flat = jnp.concatenate([item.reshape(-1) for item in small])
    tokens_row = own_first(tokens, 1)
    segments_row = own_first(segments, 1)
    seq_len = tokens_row.shape[1]
    lanes = lax.iota(jnp.int32, PAIR)
    mark = (segments[:, :, None] == lanes).astype(BF16)
    veto = jnp.where(segments_row[:, :, None] == lanes, 0.0, FAR).astype(BF16)

    packed = jnp.concatenate(
        [
            w_down,
            w_in.reshape(owned_rows, 4, width).transpose(1, 0, 2).reshape(-1, width),
            w_out,
        ],
        0,
    )
    if staged:
        w_qkv_all, begun = gather_pairwise(w_pairs, spot)
        flat = after(flat, begun)
        packed = after(packed, begun)
    else:
        w_qkv_all = lax.all_gather(w_pairs, "shard", axis=0, tiled=True)
    packed = lax.all_gather(packed, "shard", axis=0)
    if spot is None:
        table = lax.all_gather(flat, "shard", axis=0).astype(F32)
    else:
        table = gather_small(flat)
    pieces = jnp.split(table, [sum(sizes[:i]) for i in range(1, len(sizes))], axis=1)

    def two(piece):
        return piece.reshape(-1, 2, owned_rows).transpose(1, 0, 2).reshape(2, width)

    qv_all, gain_all, shift_all = two(pieces[0]), two(pieces[4]), two(pieces[5])
    out_all, in_all, down_all = (pieces[i].reshape(-1) for i in (1, 2, 3))

    flat_row = tokens_row.reshape(row_count * seq_len, width)
    bias_row = jnp.stack(
        [qv_all[0].reshape(pairs, PAIR), jnp.zeros((pairs, PAIR), F32), qv_all[1].reshape(pairs, PAIR)],
        1,
    )
    raw = jnp.dot(flat_row, w_qkv_all, preferred_element_type=F32) + bias_row.reshape(-1)
    proj = raw.astype(BF16).reshape(row_count, seq_len, 3 * width)
    attended_rows, norm = attend(proj, mark, veto)
    attended = attended_rows.reshape(token_count, width)
    flat_tokens = tokens.reshape(token_count, width)
    unit, scale, normed_low = first_norm(
        attended, flat_tokens, packed, out_all[None], gain_all[:1], shift_all[:1]
    )
    active, slope = hidden_layer(normed_low, packed, in_all[None])
    vectors = jnp.stack([gain_all[0], shift_all[0], gain_all[1], shift_all[1]])
    outputs, d_second, d_mixed, second_sums = second_norm(
        active, packed, down_all[None], unit, vectors, cotangent.reshape(token_count, width)
    )
    outputs = outputs.reshape(row_count, part_len, width)
    part_down = inner_left(active, d_mixed).astype(BF16)
    d_hidden, in_sums = hidden_back(after(d_mixed, part_down), packed, slope)
    if staged:
        far_in = product_pieces(normed_low, d_hidden, spot, 1)
        here_in = swap(far_in, "shard", CORE)
        d_hidden = after(d_hidden, far_in)
    else:
        grad_w_in = reduce_partial(inner_left(normed_low, d_hidden).astype(BF16), spot)
    d_first, d_branch, d_attended, first_sums = first_back(
        d_hidden, packed, d_second, unit, scale, gain_all[:1]
    )
    d_attended = d_attended.reshape(attended_rows.shape)
    if staged:
        near_in = product_pieces(after(normed_low, d_branch), d_hidden, spot, 0, here_in)
        inner = scatter_steps(near_in, spot, True)
        d_attended = after(d_attended, next(inner))
    d_proj, d_tokens, groups = [], None, []
    for part in range(2):
        block = attend_back(part, proj, mark, veto, d_attended, attended_rows, norm)
        block = block.reshape(row_count * seq_len, -1)
        if staged:
            left = flat_row
            if part:
                left = after(flat_row, inner.send(block))
            beside = () if part else (attended, d_branch)
            far = product_pieces(left, block, spot, 1, None, beside)
            here = swap(far, "shard", CORE)
            block = after(block, far)
        weight = lax.slice_in_dim(w_qkv_all, part * 3 * width // 2, (part + 1) * 3 * width // 2, axis=1)
        more = inner_right(block, weight)
        d_tokens = more if part == 0 else d_tokens + more
        if part:
            d_tokens = d_tokens.reshape(row_count, seq_len, width)
            d_tokens_row = sum_to_owners(d_tokens, part_len)
        if staged:
            left = after(flat_row, d_tokens)
            left = after(left, inner.send(far) if part else inner.send(d_tokens))
            near = product_pieces(left, block, spot, 0, here, beside)
            steps = scatter_steps(near, spot)
            groups.append(steps)
            if part:
                sent = next(steps)
                groups[0].send(after(sent, inner.send(near)))
                late = steps.send(after(sent, groups[0].send(near)))
            else:
                d_attended = after(d_attended, next(steps))
        d_proj.append(block)
    grad_tokens = d_first.reshape(row_count, part_len, width) + d_tokens_row
    grad_w_down = reduce_partial(part_down, spot, far if staged else None)
    if staged:

        def rest(steps):
            for pieces in steps:
                pass
            return pieces

        second, first, third = (rest(s) for s in (groups[1], groups[0], inner))
        grad_w_in = owned_rows_of(third)
        both = jnp.concatenate([first[..., : 3 * PAIR], second], 0)
        grad_pairs = owned_rows_of(both)
        grad_w_out = owned_rows_of(first[..., 3 * PAIR :])
    else:
        grad_w_out = reduce_partial(inner_left(attended, d_branch).astype(BF16), spot)
        together = inner_left(flat_row, jnp.concatenate(d_proj, 1))
        grad_pairs = reduce_partial(together.astype(BF16), spot)
    grad_w_qkv = (
        grad_pairs.reshape(owned_rows, pairs, 3, PAIR).transpose(0, 2, 1, 3).reshape(w_qkv.shape)
    )

    def column_sum(value):
        return jnp.sum(value.astype(F32), axis=0)

    if staged:
        d_proj = [after(block, late) for block in d_proj]
    d_bias = jnp.concatenate([column_sum(block) for block in d_proj]).reshape(pairs, 3, PAIR)
    shards = lax.axis_size("shard")

    def owners(*vectors):
        stacked = jnp.stack(vectors).reshape(len(vectors), shards, -1)
        return stacked.transpose(1, 0, 2).reshape(shards, -1)

    sums = jnp.concatenate(
        [
            owners(d_bias[:, 0].reshape(-1), d_bias[:, 2].reshape(-1)),
            owners(first_sums[2]),
            owners(in_sums[0]),
            owners(second_sums[2]),
            owners(first_sums[0], second_sums[0]),
            owners(first_sums[1], second_sums[1]),
        ],
        axis=1,
    )
    owned = jnp.split(
        reduce_small(sums, spot), [sum(sizes[:i]) for i in range(1, len(sizes))]
    )
    return (
        outputs,
        grad_tokens,
        grad_w_qkv,
        owned[0].reshape(qv_bias.shape),
        grad_w_out,
        owned[1],
        grad_w_in,
        owned[2],
        grad_w_down,
        owned[3],
        owned[4].reshape(gains.shape),
        owned[5].reshape(shifts.shape),
    )


def solution(mesh):
    row, flat = P("shard", None), P("shard")
    wide, whole = P(None, "shard"), P("shard", "ctx", None)
    return jax.shard_map(
        on_device,
        mesh=mesh,
        in_specs=(
            whole,
            P("shard", "ctx"),
            row,
            wide,
            row,
            flat,
            row,
            flat,
            row,
            flat,
            wide,
            wide,
            whole,
        ),
        out_specs=(whole, whole, row, wide, row, flat, row, flat, row, flat, wide, wide),
        check_vma=False,
    )
```

```python
import functools

import jax
import jax.numpy as jnp
from jax import lax
from jax.experimental import pallas as pl
from jax.experimental.pallas import tpu as pltpu
from jax.sharding import PartitionSpec as P

H = 16
HD = 64
PAIR = 2 * HD
FAR = -1e30
LIGHT = pl.CostEstimate(flops=0, bytes_accessed=0, transcendentals=0)
VMEM = 60 * 1024 * 1024
CORE, SIDE, NEAR, WIDE = 1, 2, 4, 8

F32 = jnp.float32
BF16 = jnp.bfloat16


def inner_left(left, right):
    return lax.dot_general(left, right, (((0,), (0,)), ((), ())), preferred_element_type=F32)


def inner_right(left, right):
    return lax.dot_general(left, right, (((1,), (1,)), ((), ())), preferred_element_type=F32)


def swap(value, axis, bit=1):
    return lax.ppermute(value, axis, [(i, i ^ bit) for i in range(lax.axis_size(axis))])


def by_side(own_is_first, own, other, axis):
    return jnp.where(
        own_is_first,
        jnp.concatenate([own, other], axis),
        jnp.concatenate([other, own], axis),
    )


def place():
    shard, ctx = lax.axis_index("shard"), lax.axis_index("ctx")
    return shard % 2, (shard // 2) % 2, (shard // 4) % 2, shard // 8, ctx


def assemble_body(depth, width, where_ref, *refs):
    pieces, out, sems = refs[:2], refs[2], refs[3]
    core, side, near, wide, ctx = (where_ref[i] for i in range(5))
    copies = []
    for index in range(16):
        far_core, part, second, first = index // 8, (index // 4) % 2, (index // 2) % 2, index % 2
        side_rel, ctx_rel = (first, second) if part == 0 else (second, first)
        column = ((core ^ far_core) * 2 + (ctx ^ ctx_rel)) * 2 + part
        for k in range(4):
            row = (((wide ^ (k % 2)) * 2 + (near ^ (k // 2))) * 2) + (side ^ side_rel)
            target = out.at[
                pl.ds(pl.multiple_of(row * depth, depth), depth),
                pl.ds(pl.multiple_of(column * width, width), width),
            ]
            source = pieces[far_core].at[index % 8 * 4 + k]
            copies.append(pltpu.make_async_copy(source, target, sems.at[len(copies)]))
    for copy in copies:
        copy.start()
    for copy in copies:
        copy.wait()


def gather_pairwise(shard, spot, others):
    rows, columns = shard.shape
    width = columns // 8
    core, side, near, wide, ctx = spot
    split = shard.reshape(rows, 8, width).transpose(1, 0, 2).reshape(2, 2, 2, rows, width)
    mine = lax.dynamic_index_in_dim(split, ctx, 1, False)
    own = lax.dynamic_index_in_dim(mine, core, 0, False)
    other = lax.dynamic_index_in_dim(mine, 1 - core, 0, False)
    held = by_side(core == 0, own, swap(other, "shard", CORE), 1)[None]
    for bit in (WIDE, NEAR):
        held = jnp.concatenate([held, swap(held, "shard", bit)], 0)
        begun = held if bit == WIDE else begun
    held = [held[:, 0], held[:, 1]]
    along = (("shard", SIDE), ("ctx", 1))
    for routes in (along, along[::-1]):
        held = [
            jnp.concatenate([value, swap(value, *route)], 0)
            for value, route in zip(held, routes, strict=True)
        ]
        if routes is along:
            held = [after(value, *others) for value in held]
    here = jnp.concatenate(held, 0)
    whole = pl.pallas_call(
        functools.partial(assemble_body, 2 * rows, width),
        out_shape=jax.ShapeDtypeStruct((16 * rows, columns), BF16),
        in_specs=[pl.BlockSpec(memory_space=pltpu.SMEM)]
        + [pl.BlockSpec(memory_space=pl.ANY)] * 2,
        out_specs=pl.BlockSpec(memory_space=pltpu.VMEM),
        scratch_shapes=[pltpu.SemaphoreType.DMA((64,))],
        compiler_params=pltpu.CompilerParams(vmem_limit_bytes=VMEM),
        cost_estimate=LIGHT,
        name="assemble",
    )(jnp.stack(spot).astype(jnp.int32), here, swap(here, "shard", CORE))
    return whole, begun


def gather_small(flat):
    held = flat[None]
    for bit in (CORE, SIDE, NEAR, WIDE):
        held = jnp.concatenate([held, swap(held, "shard", bit)], 0)
    return pick_rows(held)


def pick_rows(held):
    count = held.shape[0]
    index = lax.iota(jnp.int32, count) ^ lax.axis_index("shard")
    choose = (index[:, None] == lax.iota(jnp.int32, count)[None, :]).astype(F32)
    return jnp.dot(choose, held.astype(F32), precision=lax.Precision.HIGHEST)


def product_body(depth, beside, adds, split, where_ref, left_ref, right_ref, *refs):
    side, near, wide = (where_ref[i] for i in range(1, 4))
    result = inner_left(left_ref[...], right_ref[...])
    if beside:
        result = jnp.concatenate([result, inner_left(refs[0][...], refs[1][...])], 1)
    outs = refs[-4:] if split == "both" else refs[-2:] if split else refs[-1:]

    def values():
        for i in range(8):
            z, y = i // 2, i % 2
            row = (y ^ side) * 4 + ((z % 2) ^ near) * 2 + ((z // 2) ^ wide)
            value = result[i * depth : (i + 1) * depth]
            if adds:
                value = value + refs[2 * beside][0, row].astype(F32)
            yield y ^ side, row, value.astype(BF16)

    def by_ctx(pair, pick):
        for index in range(2):

            @pl.when(pl.program_id(0) == index)
            def _(index=index):
                for _, row, value in values():
                    pair[index][row] = pick(value)

    def by_row(pair, pick):
        for far_side, row, value in values():
            for index in range(2):

                @pl.when(far_side == index)
                def _(index=index, row=row, value=value):
                    pair[index][0, row - 4 * index] = pick(value)

    if split == "both":
        middle = outs[0].shape[-1]
        by_ctx(outs[:2], lambda value: value[:, :middle])
        by_row(outs[2:], lambda value: value[:, middle:])
    elif split == "ctx":
        by_ctx(outs, lambda value: value)
    elif split == "side":
        by_row(outs, lambda value: value)
    else:
        for _, row, value in values():
            outs[0][0, row] = value


def product_pieces(left, right, spot, far, received=None, beside=(), split=None):
    tokens, rows = left.shape
    depth = rows // 8
    pairs = [(left, right), *([beside] if beside else [])]
    specs, full = [], 0
    for one, two in pairs:
        width = two.shape[1] // 4
        full += width
        specs += [
            pl.BlockSpec(one.shape, lambda j, w: (0, 0)),
            pl.BlockSpec((two.shape[0], width), lambda j, w: (0, (w[0] ^ far) * 2 + (w[4] ^ j))),
        ]
    out_spec = pl.BlockSpec((1, 8, depth, full), lambda j, w: (j, 0, 0, 0))
    in_specs = specs + ([out_spec] if received is not None else [])
    along_ctx = lambda n: ((8, depth, n), pl.BlockSpec((8, depth, n), lambda j, w: (0, 0, 0)))
    along_side = lambda n: (
        (2, 4, depth, n),
        pl.BlockSpec((1, 4, depth, n), lambda j, w: (j, 0, 0, 0)),
    )
    if split == "both":
        last = full // 2 if not beside else width
        outs = [along_ctx(full - last)] * 2 + [along_side(last)] * 2
    elif split:
        outs = [along_ctx(full) if split == "ctx" else along_side(full)] * 2
    else:
        outs = [((2, 8, depth, full), out_spec)]
    adds = received is not None
    return pl.pallas_call(
        functools.partial(product_body, depth, bool(beside), adds, split),
        grid_spec=pltpu.PrefetchScalarGridSpec(
            num_scalar_prefetch=1,
            grid=(2,),
            in_specs=in_specs,
            out_specs=[spec for _, spec in outs],
        ),
        out_shape=[jax.ShapeDtypeStruct(shape, BF16) for shape, _ in outs],
        compiler_params=pltpu.CompilerParams(vmem_limit_bytes=VMEM),
        cost_estimate=LIGHT,
        name="weight_gradient",
    )(jnp.stack(spot).astype(jnp.int32), left, right, *beside, *([received] if adds else []))


def meet_body(parts, refs, outs):
    value = [
        refs[2 * i][...].astype(F32) + refs[2 * i + 1][...].astype(F32) for i in range(parts)
    ]
    value = value[0] if parts == 1 else jnp.concatenate(value, -1)
    if len(outs) == 1:
        outs[0][...] = value.astype(outs[0].dtype)
    else:
        outs[0][...] = value[0].astype(BF16)
        outs[1][...] = value[1].astype(BF16)


def meet(*pairs, dtype=BF16):
    rows = pairs[0][0].shape[-2]
    halves = pairs[0][0].ndim == 3
    widths = [left.shape[-1] for left, _ in pairs]
    columns = sum(widths)
    steps = 4 if rows % 64 == 0 and rows * columns > 1 << 18 else 1
    count = 2 * len(pairs)

    def spec(width, leading):
        if leading:
            return pl.BlockSpec((2, rows // steps, width), lambda i: (0, i, 0))
        return pl.BlockSpec((rows // steps, width), lambda i: (i, 0))

    outs = 2 if halves else 1
    return pl.pallas_call(
        lambda *refs: meet_body(len(pairs), refs[:count], refs[count:]),
        grid=(steps,),
        in_specs=[spec(width, halves) for width in widths for _ in range(2)],
        out_specs=[spec(columns, False)] * outs,
        out_shape=[jax.ShapeDtypeStruct((rows, columns), dtype)] * outs,
        compiler_params=pltpu.CompilerParams(vmem_limit_bytes=VMEM),
        cost_estimate=LIGHT,
        name="meet",
    )(*[item for pair in pairs for item in pair])


def scatter_steps(parts, spot):
    depth = parts[0][0].shape[-2]
    core, ctx = spot[0], spot[4]

    def both(value):
        return value.reshape(2, value.size // value.shape[-1] // 2, value.shape[-1])

    def gated(dep, got):
        return got if dep is None else lax.optimization_barrier((got, dep))[0]

    along = {"side": ("shard", SIDE), "ctx": ("ctx", 1)}
    other = {"side": "ctx", "ctx": "side"}
    dep = yield [sent for _, sent, _ in parts]
    moved = []
    for keep, sent, name in parts:
        got = gated(dep, swap(sent, *along[name]))
        keep, sent = meet((both(keep), both(got)))
        moved.append((keep, sent, other[name]))
    dep = yield [sent for _, sent, _ in moved]
    keep, sent = meet(
        *[(both(keep), both(gated(dep, swap(sent, *along[name])))) for keep, sent, name in moved]
    )
    dep = yield [sent]
    keep, sent = meet((both(keep), both(gated(dep, swap(sent, "shard", NEAR)))))
    dep = yield [sent]
    (held,) = meet((keep, gated(dep, swap(sent, "shard", WIDE))))
    yield held
    held = held[None]
    half = by_side(ctx == 0, held, swap(held, "ctx"), 0)
    rows = depth // 2
    kept = lax.dynamic_slice_in_dim(half, core * rows, rows, 1)
    send = lax.dynamic_slice_in_dim(half, (1 - core) * rows, rows, 1)
    yield by_side(core == 0, kept, swap(send, "shard", CORE), 0)


def owned_rows_of(pieces):
    count, rows, width = pieces.shape
    return pieces.transpose(1, 0, 2).reshape(rows, count * width).astype(F32)


def reduce_partial(partial):
    owned = lax.psum_scatter(partial, "shard", scatter_dimension=0, tiled=True)
    return lax.psum(owned, "ctx").astype(F32)


def after(value, *others):
    return lax.optimization_barrier((value, *others))[0]


def small_steps(table):
    held = pick_rows(table)
    for axis, bit in (("shard", WIDE), ("shard", NEAR), ("shard", SIDE), ("shard", CORE), ("ctx", 1)):
        half = held.shape[0] // 2
        keep, sent = (held, held) if axis == "ctx" else (held[:half], held[half:])
        sent = sent.astype(BF16)
        dep = yield sent
        got = lax.optimization_barrier((swap(sent, axis, bit), dep))[0]
        held = keep + got.astype(F32)
    yield held


def reduce_small(table):
    owned = lax.psum_scatter(table.astype(BF16), "shard", scatter_dimension=0, tiled=True)
    return lax.psum(owned, "ctx").astype(F32)


def head_lanes(shape, head):
    lane = lax.broadcasted_iota(jnp.int32, shape, 1)
    return (lane // HD) == head


def attend_body(part_len, proj_ref, mark_ref, veto_ref, out_ref, norm_ref):
    block = proj_ref[0]
    query, keys, value = (
        block[:part_len, :PAIR],
        block[:, PAIR : 2 * PAIR],
        block[:, 2 * PAIR :],
    )
    scaled = query * jnp.asarray(HD**-0.5, BF16)
    keys_marked = jnp.concatenate([keys, veto_ref[0]], 1)
    results, norms = [], []
    for head in range(2):
        alone = jnp.where(head_lanes(scaled.shape, head), scaled, jnp.zeros_like(scaled))
        scores = inner_right(keys_marked, jnp.concatenate([alone, mark_ref[0]], 1))
        top = jnp.max(scores, axis=0, keepdims=True)
        weights = jnp.exp(scores - top)
        total = jnp.sum(weights, axis=0, keepdims=True)
        result = inner_left(value, weights.astype(BF16))
        results.append(result[head * HD : (head + 1) * HD] * (1.0 / total))
        norms.append(top + jnp.log(total))
    out_ref[0] = jnp.concatenate(results, 0).T.astype(out_ref.dtype)
    norm_ref[0, 0] = jnp.concatenate(norms, 0)


def attend(proj, mark, veto):
    rows, seq_len, columns = proj.shape
    part_len = mark.shape[1]
    pairs = columns // (3 * PAIR)
    return pl.pallas_call(
        functools.partial(attend_body, part_len),
        grid=(rows, pairs),
        in_specs=[
            pl.BlockSpec((1, seq_len, 3 * PAIR), lambda r, j: (r, 0, j)),
            pl.BlockSpec((1, part_len, PAIR), lambda r, j: (r, 0, 0)),
            pl.BlockSpec((1, seq_len, PAIR), lambda r, j: (r, 0, 0)),
        ],
        out_specs=[
            pl.BlockSpec((1, part_len, PAIR), lambda r, j: (r, 0, j)),
            pl.BlockSpec((1, 1, 2, part_len), lambda r, j: (r, j, 0, 0)),
        ],
        out_shape=[
            jax.ShapeDtypeStruct((rows, part_len, pairs * PAIR), BF16),
            jax.ShapeDtypeStruct((rows, pairs, 2, part_len), F32),
        ],
        compiler_params=pltpu.CompilerParams(vmem_limit_bytes=VMEM),
        cost_estimate=LIGHT,
        name="attend",
    )(proj, mark, veto)


def attend_back_body(
    part_len, proj_ref, mark_ref, veto_ref, grad_ref, result_ref, norm_ref, out_ref, sums_ref
):
    block = proj_ref[0]
    seq_len = block.shape[0]
    query, keys, value = (
        block[:part_len, :PAIR],
        block[:, PAIR : 2 * PAIR],
        block[:, 2 * PAIR :],
    )
    scaled = query * jnp.asarray(HD**-0.5, BF16)
    keys_marked = jnp.concatenate([keys, veto_ref[0]], 1)
    grad = grad_ref[0]
    product = (grad.astype(F32) * result_ref[0].astype(F32)).T
    d_query, d_keys, d_value = [], None, None
    for head in range(2):
        lanes = head_lanes(scaled.shape, head)
        alone = jnp.where(lanes, scaled, jnp.zeros_like(scaled))
        grad_alone = jnp.where(lanes, grad, jnp.zeros_like(grad))
        scores = inner_right(keys_marked, jnp.concatenate([alone, mark_ref[0]], 1))
        weights = jnp.exp(scores - norm_ref[0, 0, head : head + 1, :])
        d_weights = inner_right(value, grad_alone)
        inner = jnp.sum(product[head * HD : (head + 1) * HD], axis=0, keepdims=True)
        d_scores = (weights * (d_weights - inner)).astype(BF16)
        more_value = jnp.dot(weights.astype(BF16), grad_alone, preferred_element_type=F32)
        more_keys = jnp.dot(d_scores, alone, preferred_element_type=F32)
        d_value = more_value if d_value is None else d_value + more_value
        d_keys = more_keys if d_keys is None else d_keys + more_keys
        d_query.append(inner_left(keys, d_scores)[head * HD : (head + 1) * HD])
    d_query = jnp.concatenate(d_query, 0).T * HD**-0.5
    out_ref[0, :part_len, :PAIR] = d_query.astype(BF16)
    if seq_len > part_len:
        out_ref[0, part_len:, :PAIR] = jnp.zeros((seq_len - part_len, PAIR), BF16)
    out_ref[0, :, PAIR : 2 * PAIR] = d_keys.astype(BF16)
    out_ref[0, :, 2 * PAIR :] = d_value.astype(BF16)
    sums_ref[0, 0, 0:1] = jnp.sum(d_query, axis=0, keepdims=True)
    sums_ref[0, 0, 1:2] = jnp.sum(d_value, axis=0, keepdims=True)


def attend_back(part, proj, mark, veto, grad, result, norm):
    rows, seq_len, columns = proj.shape
    part_len = mark.shape[1]
    pairs = columns // (3 * PAIR) // 2
    own = pl.BlockSpec((1, part_len, PAIR), lambda r, j: (r, 0, part * pairs + j))
    return pl.pallas_call(
        functools.partial(attend_back_body, part_len),
        grid=(rows, pairs),
        in_specs=[
            pl.BlockSpec((1, seq_len, 3 * PAIR), lambda r, j: (r, 0, part * pairs + j)),
            pl.BlockSpec((1, part_len, PAIR), lambda r, j: (r, 0, 0)),
            pl.BlockSpec((1, seq_len, PAIR), lambda r, j: (r, 0, 0)),
            own,
            own,
            pl.BlockSpec((1, 1, 2, part_len), lambda r, j: (r, part * pairs + j, 0, 0)),
        ],
        out_specs=[
            pl.BlockSpec((1, seq_len, 3 * PAIR), lambda r, j: (r, 0, j)),
            pl.BlockSpec((1, 1, 2, PAIR), lambda r, j: (r, j, 0, 0)),
        ],
        out_shape=[
            jax.ShapeDtypeStruct((rows, seq_len, columns // 2), BF16),
            jax.ShapeDtypeStruct((rows, pairs, 2, PAIR), F32),
        ],
        compiler_params=pltpu.CompilerParams(vmem_limit_bytes=VMEM),
        cost_estimate=LIGHT,
        name="attend_back",
    )(proj, mark, veto, grad, result, norm)


CUTS = 2


def cuts(rows):
    step = rows // CUTS
    return [slice(i * step, (i + 1) * step) for i in range(CUTS)]


def mean_of(value):
    return jnp.mean(value, axis=-1, keepdims=True)


def normalise(value):
    center = value - mean_of(value)
    scale = lax.rsqrt(mean_of(center * center) + 1e-06)
    return center * scale, scale


def normalise_back(unit, scale, incoming, gain):
    edge = incoming * gain
    return scale * (edge - mean_of(edge) - unit * mean_of(edge * unit))


def total(value):
    return jnp.sum(value, axis=0, keepdims=True)


def whole_block(shape):
    return pl.BlockSpec(shape, lambda *_: (0,) * len(shape))


def down_block(packed):
    shards, rows, width = packed.shape
    return pl.BlockSpec((shards // 4, rows // 9 * 4, width), lambda k: (k, 0, 0))


def in_block(packed):
    shards, rows, width = packed.shape
    return pl.BlockSpec((shards, rows // 9, width), lambda k: (0, 4 + k, 0))


def out_block(packed):
    shards, rows, width = packed.shape
    return pl.BlockSpec((shards, rows // 9, width), lambda *_: (0, 8, 0))


def square(ref):
    return ref[...].reshape(-1, ref.shape[-1])


def kernel(body, grid, name, in_specs, outs, out_specs, scratch=()):
    return pl.pallas_call(
        body,
        grid=grid,
        in_specs=in_specs,
        out_shape=[jax.ShapeDtypeStruct(*out) for out in outs],
        out_specs=out_specs,
        scratch_shapes=scratch,
        compiler_params=pltpu.CompilerParams(vmem_limit_bytes=VMEM),
        cost_estimate=LIGHT,
        name=name,
    )


def first_norm_body(attended, tokens, weight, bias, gain, shift, unit, scale, low):
    matrix = square(weight)
    for cut in cuts(attended.shape[0]):
        branch = jnp.dot(attended[cut], matrix, preferred_element_type=F32) + bias[...]
        u, r = normalise(tokens[cut].astype(F32) + branch)
        unit[cut] = u
        scale[cut] = jnp.broadcast_to(r, (r.shape[0], PAIR))
        low[cut] = (u * gain[...] + shift[...]).astype(BF16)


def first_norm(attended, tokens, packed, bias, gain, shift):
    count, width = tokens.shape
    row, flat = whole_block((count, width)), whole_block((1, width))
    narrow = whole_block((count, PAIR))
    return kernel(
        first_norm_body,
        (1,),
        "first_norm",
        [row, row, out_block(packed), flat, flat, flat],
        [((count, width), F32), ((count, PAIR), F32), ((count, width), BF16)],
        [row, narrow, row],
    )(attended, tokens, packed, bias, gain, shift)


def hidden_body(low, weight, bias, active, slope):
    matrix = square(weight)
    for cut in cuts(low.shape[0]):
        hidden = jnp.dot(low[cut], matrix, preferred_element_type=F32) + bias[...]
        below = 0.5 * (1.0 + lax.erf(hidden * 0.7071067811865476))
        active[cut] = (hidden * below).astype(BF16)
        bell = 0.3989422804014327 * jnp.exp(-0.5 * hidden * hidden)
        slope[cut] = (below + hidden * bell).astype(BF16)


def hidden_layer(low, packed, bias):
    count, width = low.shape
    column = pl.BlockSpec((count, width), lambda k: (0, k))
    return kernel(
        hidden_body,
        (4,),
        "hidden_layer",
        [whole_block(low.shape), in_block(packed), pl.BlockSpec((1, width), lambda k: (0, k))],
        [((count, 4 * width), BF16)] * 2,
        [column] * 2,
    )(low, packed, bias)


def second_norm_body(
    active, weight, bias, unit, vectors, cotangent, outputs, second, low, sums, held
):
    step = pl.program_id(0)
    more = jnp.dot(active[...], square(weight), preferred_element_type=F32)

    @pl.when(step == 0)
    def _():
        held[...] = more

    @pl.when(step > 0)
    def _():
        held[...] += more

    @pl.when(step == pl.num_programs(0) - 1)
    def _():
        gain_one, shift_one, gain, shift = (vectors[i : i + 1] for i in range(4))
        totals = []
        for cut in cuts(held.shape[0]):
            normed = unit[cut] * gain_one + shift_one
            u, r = normalise(normed + held[cut] + bias[...])
            outputs[cut] = (u * gain + shift).astype(BF16)
            incoming = cotangent[cut]
            back = normalise_back(u, r, incoming, gain)
            second[cut] = back
            low[cut] = back.astype(BF16)
            totals.append((total(incoming * u), total(incoming), total(low[cut].astype(F32))))
        sums[...] = jnp.concatenate([sum(item) for item in zip(*totals, strict=True)], 0)


def second_norm(active, packed, bias, unit, vectors, cotangent):
    count, width = unit.shape
    row = whole_block((count, width))
    return kernel(
        second_norm_body,
        (4,),
        "second_norm",
        [
            pl.BlockSpec((count, width), lambda k: (0, k)),
            down_block(packed),
            whole_block((1, width)),
            row,
            whole_block((4, width)),
            row,
        ],
        [((count, width), BF16), ((count, width), F32), ((count, width), BF16), ((3, width), F32)],
        [row, row, row, whole_block((3, width))],
        [pltpu.VMEM((count, width), F32)],
    )(active, packed, bias, unit, vectors, cotangent)


def hidden_back_body(low, weight, slope, d_hidden, sums):
    matrix = square(weight)
    totals = []
    for cut in cuts(low.shape[0]):
        grad = (inner_right(low[cut], matrix) * slope[cut].astype(F32)).astype(BF16)
        d_hidden[cut] = grad
        totals.append(total(grad.astype(F32)))
    sums[...] = sum(totals)


def hidden_back(low, packed, slope):
    count, width = low.shape
    column = pl.BlockSpec((count, width), lambda k: (0, k))
    return kernel(
        hidden_back_body,
        (4,),
        "hidden_back",
        [whole_block(low.shape), down_block(packed), column],
        [((count, 4 * width), BF16), ((1, 4 * width), F32)],
        [column, pl.BlockSpec((1, width), lambda k: (0, k))],
    )(low, packed, slope)


def first_back_body(
    d_hidden, weight, last, second, unit, scale, gain, first, low, d_attended, sums, held
):
    step = pl.program_id(0)
    more = inner_right(d_hidden[...], square(weight))

    @pl.when(step == 0)
    def _():
        held[...] = second[...] + more

    @pl.when(step > 0)
    def _():
        held[...] += more

    @pl.when(step == pl.num_programs(0) - 1)
    def _():
        matrix = square(last)
        totals = []
        for cut in cuts(held.shape[0]):
            incoming, u = held[cut], unit[cut]
            back = normalise_back(u, scale[cut][:, :1], incoming, gain[...])
            first[cut] = back
            low[cut] = back.astype(BF16)
            d_attended[cut] = inner_right(low[cut], matrix).astype(BF16)
            totals.append((total(incoming * u), total(incoming), total(low[cut].astype(F32))))
        sums[...] = jnp.concatenate([sum(item) for item in zip(*totals, strict=True)], 0)


def first_back(d_hidden, packed, second, unit, scale, gain):
    count, width = unit.shape
    row = whole_block((count, width))
    return kernel(
        first_back_body,
        (4,),
        "first_back",
        [
            pl.BlockSpec((count, width), lambda k: (0, k)),
            in_block(packed),
            out_block(packed),
            row,
            row,
            whole_block((count, PAIR)),
            whole_block((1, width)),
        ],
        [((count, width), F32), ((count, width), BF16), ((count, width), BF16), ((3, width), F32)],
        [row, row, row, whole_block((3, width))],
        [pltpu.VMEM((count, width), F32)],
    )(d_hidden, packed, packed, second, unit, scale, gain)


def input_back_body(block, weight, more, first, *outs):
    step = pl.program_id(0)
    result = inner_right(block[...], weight[...])
    if len(outs) == 1:
        outs[0][...] = result.astype(BF16)
        return
    result = result + more[...].astype(F32)

    @pl.when(step == 0)
    def _():
        outs[0][...] = result + first[...]

    @pl.when(step > 0)
    def _():
        outs[1][...] = result.astype(BF16)


def input_back(part, block, w_qkv, more=None, first=None):
    rows, half = block.shape
    width = w_qkv.shape[0]
    mine = rows // 2
    row = pl.BlockSpec((mine, width), lambda i: (i, 0))
    last = more is not None
    body = input_back_body if last else lambda b, w, o: input_back_body(b, w, None, None, o)
    return kernel(
        body,
        (2,),
        "input_back",
        [
            pl.BlockSpec((mine, half), lambda i: (i, 0)),
            pl.BlockSpec((width, half), lambda i: (0, part)),
            *([row, whole_block((mine, width))] if last else []),
        ],
        [((mine, width), F32), ((mine, width), BF16)] if last else [((rows, width), BF16)],
        [whole_block((mine, width))] * 2 if last else [row],
    )(block, w_qkv, *([more, first] if last else []))


def own_first(value, axis):
    if lax.axis_size("ctx") == 2:
        return jnp.concatenate([value, swap(value, "ctx")], axis)
    whole = lax.all_gather(value, "ctx", axis=axis, tiled=True)
    return jnp.roll(whole, -lax.axis_index("ctx") * value.shape[axis], axis)


def sum_to_owners(value, own_len):
    own = value[:, :own_len].astype(F32)
    if lax.axis_size("ctx") == 2:
        return own + swap(value[:, own_len:].astype(BF16), "ctx").astype(F32)
    whole = jnp.roll(value, lax.axis_index("ctx") * own_len, 1).astype(BF16)
    return lax.psum_scatter(whole, "ctx", scatter_dimension=1, tiled=True).astype(F32)


def on_device(
    tokens,
    segments,
    w_qkv,
    qv_bias,
    w_out,
    out_bias,
    w_in,
    in_bias,
    w_down,
    down_bias,
    gains,
    shifts,
    cotangent,
):
    staged = lax.axis_size("shard") == 16 and lax.axis_size("ctx") == 2
    spot = place() if staged else None
    row_count, part_len, width = tokens.shape
    owned_rows = w_qkv.shape[0]
    pairs = H // 2
    token_count = row_count * part_len

    w_pairs = (
        w_qkv.reshape(owned_rows, 3, pairs, PAIR).transpose(0, 2, 1, 3).reshape(w_qkv.shape)
    )
    small = [qv_bias, out_bias, in_bias, down_bias, gains, shifts]
    sizes = [item.size for item in small]
    flat = jnp.concatenate([item.reshape(-1) for item in small])
    tokens_row = own_first(tokens, 1)
    segments_row = own_first(segments, 1)
    seq_len = tokens_row.shape[1]
    lanes = lax.iota(jnp.int32, PAIR)
    mark = (segments[:, :, None] == lanes).astype(BF16)
    veto = jnp.where(segments_row[:, :, None] == lanes, 0.0, FAR).astype(BF16)

    packed = jnp.concatenate(
        [
            w_down,
            w_in.reshape(owned_rows, 4, width).transpose(1, 0, 2).reshape(-1, width),
            w_out,
        ],
        0,
    )
    if staged:
        table = gather_small(flat)
        w_qkv_all, begun = gather_pairwise(w_pairs, spot, [table, tokens_row])
        packed = after(packed, begun)
    else:
        w_qkv_all = lax.all_gather(w_pairs, "shard", axis=0, tiled=True)
    packed = lax.all_gather(packed, "shard", axis=0)
    if not staged:
        table = lax.all_gather(flat, "shard", axis=0).astype(F32)
    pieces = jnp.split(table, [sum(sizes[:i]) for i in range(1, len(sizes))], axis=1)

    def two(piece):
        return piece.reshape(-1, 2, owned_rows).transpose(1, 0, 2).reshape(2, width)

    qv_all, gain_all, shift_all = two(pieces[0]), two(pieces[4]), two(pieces[5])
    out_all, in_all, down_all = (pieces[i].reshape(-1) for i in (1, 2, 3))

    flat_row = lax.optimization_barrier(tokens_row.reshape(row_count * seq_len, width))
    bias_row = jnp.stack(
        [qv_all[0].reshape(pairs, PAIR), jnp.zeros((pairs, PAIR), F32), qv_all[1].reshape(pairs, PAIR)],
        1,
    )
    raw = jnp.dot(flat_row, w_qkv_all, preferred_element_type=F32) + bias_row.reshape(-1)
    proj = raw.astype(BF16).reshape(row_count, seq_len, 3 * width)
    attended_rows, norm = attend(proj, mark, veto)
    attended = attended_rows.reshape(token_count, width)
    flat_tokens = tokens.reshape(token_count, width)
    unit, scale, normed_low = first_norm(
        attended, flat_tokens, packed, out_all[None], gain_all[:1], shift_all[:1]
    )
    active, slope = hidden_layer(normed_low, packed, in_all[None])
    vectors = jnp.stack([gain_all[0], shift_all[0], gain_all[1], shift_all[1]])
    outputs, d_second, d_mixed, second_sums = second_norm(
        active, packed, down_all[None], unit, vectors, cotangent.reshape(token_count, width)
    )
    outputs = outputs.reshape(row_count, part_len, width)
    part_down = inner_left(active, d_mixed).astype(BF16)
    d_hidden, in_sums = hidden_back(after(d_mixed, part_down), packed, slope)
    if staged:
        (far_in,) = product_pieces(normed_low, d_hidden, spot, 1)
        here_in = swap(far_in, "shard", CORE)
        d_hidden = after(d_hidden, far_in)
    else:
        grad_w_in = reduce_partial(inner_left(normed_low, d_hidden).astype(BF16))
    d_first, d_branch, d_attended, first_sums = first_back(
        d_hidden, packed, d_second, unit, scale, gain_all[:1]
    )
    d_attended = d_attended.reshape(attended_rows.shape)
    if staged:
        left = after(normed_low, d_branch)
        near_in = product_pieces(left, d_hidden, spot, 0, here_in, (), "both")
        inner = scatter_steps([(*near_in[:2], "ctx"), (*near_in[2:], "side")], spot)
        d_attended = after(d_attended, *next(inner))
    half = 3 * width // 2
    rows_flat = row_count * seq_len

    def d_tokens_of(part, block):
        return inner_right(block, lax.slice_in_dim(w_qkv_all, part * half, (part + 1) * half, axis=1))

    def attention_back(part, grad):
        block, sums = attend_back(part, proj, mark, veto, grad, attended_rows, norm)
        return block.reshape(rows_flat, half), jnp.sum(sums, axis=0)

    def column_sums(sums_one, sums_two):
        both = jnp.concatenate([sums_one, sums_two], 0).transpose(1, 0, 2).reshape(2, width)
        shards = lax.axis_size("shard")

        def owners(*vectors):
            stacked = jnp.stack(vectors).reshape(len(vectors), shards, -1)
            return stacked.transpose(1, 0, 2).reshape(shards, -1)

        return jnp.concatenate(
            [
                owners(both[0], both[1]),
                owners(first_sums[2]),
                owners(in_sums[0]),
                owners(second_sums[2]),
                owners(first_sums[0], second_sums[0]),
                owners(first_sums[1], second_sums[1]),
            ],
            axis=1,
        )

    d_one, sums_one = attention_back(0, d_attended)
    if staged:
        beside = (attended, d_branch)
        left = after(flat_row, *inner.send(d_one))
        (far,) = product_pieces(left, d_one, spot, 1, None, beside)
        here = swap(far, "shard", CORE)
        d_one = after(d_one, far)
        (d_tokens,) = input_back(0, d_one, w_qkv_all)
        left = after(flat_row, d_tokens)
        near = product_pieces(left, d_one, spot, 0, here, beside, "both")
        one = scatter_steps([(*near[:2], "ctx"), (*near[2:], "side")], spot)
        one_sent = next(one)
        inner_sent = inner.send(one_sent)
        owned_down = lax.psum_scatter(part_down, "shard", scatter_dimension=0, tiled=True)
        d_two, sums_two = attention_back(1, after(d_attended, *one_sent, *inner_sent))
        sent = one.send(d_two) + inner.send(d_two)
        (far,) = product_pieces(after(flat_row, *sent), d_two, spot, 1)
        here = swap(far, "shard", CORE)
        d_two = after(d_two, far)
        owned_down = after(owned_down, far)
        left = after(flat_row, owned_down)
        near = product_pieces(left, d_two, spot, 0, here, (), "side")
        two = scatter_steps([(*near, "side")], spot)
        two_sent = next(two)
        two_sent = [*two_sent, inner.send(two_sent)]
        down_here = swap(owned_down, "ctx")
        last = after(d_two, *two_sent)
        own_tokens, d_tokens = input_back(1, last, w_qkv_all, d_tokens, d_first)
        tokens_here = swap(d_tokens, "ctx")
        sent = one.send(d_tokens)
        (grad_w_down,) = meet((owned_down, after(down_here, *sent)), dtype=F32)
        table = column_sums(sums_one, after(sums_two, grad_w_down))
        small_sums = small_steps(table)
        sent = two.send([next(small_sums)])
        sent = one.send(sent)
        sent = [one.send(sent)]
        sent = [small_sums.send(sent)]
        grad_tokens = own_tokens + after(tokens_here, *sent).astype(F32)
        grad_tokens = grad_tokens.reshape(row_count, part_len, width)
        sent = two.send([*sent, grad_tokens])
        sent = [small_sums.send(sent)]
        sent = two.send(sent)
        sent = [small_sums.send(sent)]
        sent = [two.send(sent)]
        sent = [small_sums.send(sent)]
        owned = small_sums.send(sent)[0]
        grad_w_in = owned_rows_of(next(inner))
        second, first = next(two), next(one)
        grad_pairs = owned_rows_of(jnp.concatenate([first[..., : 3 * PAIR], second], 0))
        grad_w_out = owned_rows_of(first[..., 3 * PAIR :])
    else:
        d_two, sums_two = attention_back(1, d_attended)
        d_tokens = (d_tokens_of(0, d_one) + d_tokens_of(1, d_two)).reshape(row_count, seq_len, width)
        grad_tokens = d_first.reshape(row_count, part_len, width) + sum_to_owners(d_tokens, part_len)
        grad_w_down = reduce_partial(part_down)
        grad_w_out = reduce_partial(inner_left(attended, d_branch).astype(BF16))
        together = inner_left(flat_row, jnp.concatenate([d_one, d_two], 1))
        grad_pairs = reduce_partial(together.astype(BF16))
        owned = reduce_small(column_sums(sums_one, sums_two))[0]
    grad_w_qkv = (
        grad_pairs.reshape(owned_rows, pairs, 3, PAIR).transpose(0, 2, 1, 3).reshape(w_qkv.shape)
    )
    owned = jnp.split(owned, [sum(sizes[:i]) for i in range(1, len(sizes))])
    return (
        outputs,
        grad_tokens,
        grad_w_qkv,
        owned[0].reshape(qv_bias.shape),
        grad_w_out,
        owned[1],
        grad_w_in,
        owned[2],
        grad_w_down,
        owned[3],
        owned[4].reshape(gains.shape),
        owned[5].reshape(shifts.shape),
    )


def solution(mesh):
    row, flat = P("shard", None), P("shard")
    wide, whole = P(None, "shard"), P("shard", "ctx", None)
    return jax.shard_map(
        on_device,
        mesh=mesh,
        in_specs=(
            whole,
            P("shard", "ctx"),
            row,
            wide,
            row,
            flat,
            row,
            flat,
            row,
            flat,
            wide,
            wide,
            whole,
        ),
        out_specs=(whole, whole, row, wide, row, flat, row, flat, row, flat, wide, wide),
        check_vma=False,
    )
```

```python
import functools

import jax
import jax.numpy as jnp
from jax import lax
from jax.experimental import pallas as pl
from jax.experimental.pallas import tpu as pltpu
from jax.sharding import PartitionSpec as P

H = 16
HD = 64
PAIR = 2 * HD
FAR = -1e30
LIGHT = pl.CostEstimate(flops=0, bytes_accessed=0, transcendentals=0)
VMEM = 60 * 1024 * 1024
CORE, SIDE, NEAR, WIDE = 1, 2, 4, 8

F32 = jnp.float32
BF16 = jnp.bfloat16


def inner_left(left, right):
    return lax.dot_general(left, right, (((0,), (0,)), ((), ())), preferred_element_type=F32)


def inner_right(left, right):
    return lax.dot_general(left, right, (((1,), (1,)), ((), ())), preferred_element_type=F32)


def swap(value, axis, bit=1):
    return lax.ppermute(value, axis, [(i, i ^ bit) for i in range(lax.axis_size(axis))])


def by_side(own_is_first, own, other, axis):
    return jnp.where(
        own_is_first,
        jnp.concatenate([own, other], axis),
        jnp.concatenate([other, own], axis),
    )


def place():
    shard, ctx = lax.axis_index("shard"), lax.axis_index("ctx")
    return shard % 2, (shard // 2) % 2, (shard // 4) % 2, shard // 8, ctx


def assemble_body(depth, width, where_ref, *refs):
    pieces, out, sems = refs[:2], refs[2], refs[3]
    core, side, near, wide, ctx = (where_ref[i] for i in range(5))
    copies = []
    for index in range(16):
        far_core, part, second, first = index // 8, (index // 4) % 2, (index // 2) % 2, index % 2
        side_rel, ctx_rel = (first, second) if part == 0 else (second, first)
        column = ((core ^ far_core) * 2 + (ctx ^ ctx_rel)) * 2 + part
        for k in range(4):
            row = (((wide ^ (k % 2)) * 2 + (near ^ (k // 2))) * 2) + (side ^ side_rel)
            target = out.at[
                pl.ds(pl.multiple_of(row * depth, depth), depth),
                pl.ds(pl.multiple_of(column * width, width), width),
            ]
            source = pieces[far_core].at[index % 8 * 4 + k]
            copies.append(pltpu.make_async_copy(source, target, sems.at[len(copies)]))
    for copy in copies:
        copy.start()
    for copy in copies:
        copy.wait()


def gather_pairwise(shard, spot, others):
    rows, columns = shard.shape
    width = columns // 8
    core, side, near, wide, ctx = spot
    split = shard.reshape(rows, 8, width).transpose(1, 0, 2).reshape(2, 2, 2, rows, width)
    mine = lax.dynamic_index_in_dim(split, ctx, 1, False)
    own = lax.dynamic_index_in_dim(mine, core, 0, False)
    other = lax.dynamic_index_in_dim(mine, 1 - core, 0, False)
    held = by_side(core == 0, own, swap(other, "shard", CORE), 1)[None]
    for bit in (WIDE, NEAR):
        held = jnp.concatenate([held, swap(held, "shard", bit)], 0)
        begun = held if bit == WIDE else begun
    held = [held[:, 0], held[:, 1]]
    along = (("shard", SIDE), ("ctx", 1))
    for routes in (along, along[::-1]):
        held = [
            jnp.concatenate([value, swap(value, *route)], 0)
            for value, route in zip(held, routes, strict=True)
        ]
        if routes is along:
            held = [after(value, *others) for value in held]
    here = jnp.concatenate(held, 0)
    whole = pl.pallas_call(
        functools.partial(assemble_body, 2 * rows, width),
        out_shape=jax.ShapeDtypeStruct((16 * rows, columns), BF16),
        in_specs=[pl.BlockSpec(memory_space=pltpu.SMEM)]
        + [pl.BlockSpec(memory_space=pl.ANY)] * 2,
        out_specs=pl.BlockSpec(memory_space=pltpu.VMEM),
        scratch_shapes=[pltpu.SemaphoreType.DMA((64,))],
        compiler_params=pltpu.CompilerParams(vmem_limit_bytes=VMEM),
        cost_estimate=LIGHT,
        name="assemble",
    )(jnp.stack(spot).astype(jnp.int32), here, swap(here, "shard", CORE))
    return whole, begun


def gather_small(flat):
    held = flat[None]
    for bit in (CORE, SIDE, NEAR, WIDE):
        held = jnp.concatenate([held, swap(held, "shard", bit)], 0)
    return pick_rows(held)


def pick_rows(held):
    count = held.shape[0]
    index = lax.iota(jnp.int32, count) ^ lax.axis_index("shard")
    choose = (index[:, None] == lax.iota(jnp.int32, count)[None, :]).astype(F32)
    return jnp.dot(choose, held.astype(F32), precision=lax.Precision.HIGHEST)


def product_body(depth, beside, adds, split, where_ref, left_ref, right_ref, *refs):
    side, near, wide = (where_ref[i] for i in range(1, 4))
    result = inner_left(left_ref[...], right_ref[...])
    if beside:
        result = jnp.concatenate([result, inner_left(refs[0][...], refs[1][...])], 1)
    outs = refs[-4:] if split == "both" else refs[-2:] if split else refs[-1:]

    def values():
        for i in range(8):
            z, y = i // 2, i % 2
            row = (y ^ side) * 4 + ((z % 2) ^ near) * 2 + ((z // 2) ^ wide)
            value = result[i * depth : (i + 1) * depth]
            if adds:
                value = value + refs[2 * beside][0, row].astype(F32)
            yield y ^ side, row, value.astype(BF16)

    def by_ctx(pair, pick):
        for index in range(2):

            @pl.when(pl.program_id(0) == index)
            def _(index=index):
                for _, row, value in values():
                    pair[index][row] = pick(value)

    def by_row(pair, pick):
        for far_side, row, value in values():
            for index in range(2):

                @pl.when(far_side == index)
                def _(index=index, row=row, value=value):
                    pair[index][0, row - 4 * index] = pick(value)

    if split == "both":
        middle = outs[0].shape[-1]
        by_ctx(outs[:2], lambda value: value[:, :middle])
        by_row(outs[2:], lambda value: value[:, middle:])
    elif split == "ctx":
        by_ctx(outs, lambda value: value)
    elif split == "side":
        by_row(outs, lambda value: value)
    else:
        for _, row, value in values():
            outs[0][0, row] = value


def product_pieces(left, right, spot, far, received=None, beside=(), split=None):
    tokens, rows = left.shape
    depth = rows // 8
    pairs = [(left, right), *([beside] if beside else [])]
    specs, full = [], 0
    for one, two in pairs:
        width = two.shape[1] // 4
        full += width
        specs += [
            pl.BlockSpec(one.shape, lambda j, w: (0, 0)),
            pl.BlockSpec((two.shape[0], width), lambda j, w: (0, (w[0] ^ far) * 2 + (w[4] ^ j))),
        ]
    out_spec = pl.BlockSpec((1, 8, depth, full), lambda j, w: (j, 0, 0, 0))
    in_specs = specs + ([out_spec] if received is not None else [])
    along_ctx = lambda n: ((8, depth, n), pl.BlockSpec((8, depth, n), lambda j, w: (0, 0, 0)))
    along_side = lambda n: (
        (2, 4, depth, n),
        pl.BlockSpec((1, 4, depth, n), lambda j, w: (j, 0, 0, 0)),
    )
    if split == "both":
        last = full // 2 if not beside else width
        outs = [along_ctx(full - last)] * 2 + [along_side(last)] * 2
    elif split:
        outs = [along_ctx(full) if split == "ctx" else along_side(full)] * 2
    else:
        outs = [((2, 8, depth, full), out_spec)]
    adds = received is not None
    return pl.pallas_call(
        functools.partial(product_body, depth, bool(beside), adds, split),
        grid_spec=pltpu.PrefetchScalarGridSpec(
            num_scalar_prefetch=1,
            grid=(2,),
            in_specs=in_specs,
            out_specs=[spec for _, spec in outs],
        ),
        out_shape=[jax.ShapeDtypeStruct(shape, BF16) for shape, _ in outs],
        compiler_params=pltpu.CompilerParams(vmem_limit_bytes=VMEM),
        cost_estimate=LIGHT,
        name="weight_gradient",
    )(jnp.stack(spot).astype(jnp.int32), left, right, *beside, *([received] if adds else []))


def meet_body(parts, refs, outs):
    value = [
        refs[2 * i][...].astype(F32) + refs[2 * i + 1][...].astype(F32) for i in range(parts)
    ]
    value = value[0] if parts == 1 else jnp.concatenate(value, -1)
    if len(outs) == 1:
        outs[0][...] = value.astype(outs[0].dtype)
    else:
        outs[0][...] = value[0].astype(BF16)
        outs[1][...] = value[1].astype(BF16)


def meet(*pairs, dtype=BF16):
    rows = pairs[0][0].shape[-2]
    halves = pairs[0][0].ndim == 3
    widths = [left.shape[-1] for left, _ in pairs]
    columns = sum(widths)
    steps = 4 if rows % 64 == 0 and rows * columns > 1 << 18 else 1
    count = 2 * len(pairs)

    def spec(width, leading):
        if leading:
            return pl.BlockSpec((2, rows // steps, width), lambda i: (0, i, 0))
        return pl.BlockSpec((rows // steps, width), lambda i: (i, 0))

    outs = 2 if halves else 1
    return pl.pallas_call(
        lambda *refs: meet_body(len(pairs), refs[:count], refs[count:]),
        grid=(steps,),
        in_specs=[spec(width, halves) for width in widths for _ in range(2)],
        out_specs=[spec(columns, False)] * outs,
        out_shape=[jax.ShapeDtypeStruct((rows, columns), dtype)] * outs,
        compiler_params=pltpu.CompilerParams(vmem_limit_bytes=VMEM),
        cost_estimate=LIGHT,
        name="meet",
    )(*[item for pair in pairs for item in pair])


def gather_sum(*values):
    def body(*refs):
        refs[-1][...] = sum(ref[...].astype(F32) for ref in refs[:-1]).astype(BF16)

    spec = whole_block(values[0].shape)
    outs = [(values[0].shape, BF16)]
    return kernel(body, (1,), "gather_sum", [spec] * len(values), outs, [spec])(*values)


def scatter_steps(parts, spot):
    depth = parts[0][0].shape[-2]
    core, ctx = spot[0], spot[4]

    def both(value):
        return value.reshape(2, value.size // value.shape[-1] // 2, value.shape[-1])

    def gated(dep, got):
        return got if dep is None else lax.optimization_barrier((got, dep))[0]

    along = {"side": ("shard", SIDE), "ctx": ("ctx", 1)}
    other = {"side": "ctx", "ctx": "side"}
    dep = yield [sent for _, sent, _ in parts]
    moved = []
    for keep, sent, name in parts:
        got = gated(dep, swap(sent, *along[name]))
        keep, sent = meet((both(keep), both(got)))
        moved.append((keep, sent, other[name]))
    dep = yield [sent for _, sent, _ in moved]
    keep, sent = meet(
        *[(both(keep), both(gated(dep, swap(sent, *along[name])))) for keep, sent, name in moved]
    )
    keep, sent = both(keep), both(sent)
    dep = yield [keep, sent]
    bits = (WIDE, NEAR, NEAR ^ WIDE)
    got = [swap(v, "shard", bit) for v, bit in zip((keep[1], sent[0], sent[1]), bits, strict=True)]
    (held,) = gather_sum(keep[0], *[gated(dep, value) for value in got])
    yield [held]
    rows = depth // 2
    mine = lax.dynamic_slice_in_dim(held, core * rows, rows, 0)
    other = lax.dynamic_slice_in_dim(held, (1 - core) * rows, rows, 0)
    shards = lax.axis_size("shard")
    across = [(i, i ^ 3) for i in range(2 * shards)]
    corner = lax.ppermute(other, ("shard", "ctx"), across)
    here = by_side(ctx == 0, mine[None], swap(mine, "ctx")[None], 0)
    there = by_side(ctx == 0, swap(other, "shard", CORE)[None], corner[None], 0)
    yield by_side(core == 0, here, there, 0)


def owned_rows_of(pieces):
    count, rows, width = pieces.shape
    return pieces.transpose(1, 0, 2).reshape(rows, count * width).astype(F32)


def reduce_partial(partial):
    owned = lax.psum_scatter(partial, "shard", scatter_dimension=0, tiled=True)
    return lax.psum(owned, "ctx").astype(F32)


def after(value, *others):
    return lax.optimization_barrier((value, *others))[0]


def small_steps(table):
    held = pick_rows(table)
    for axis, bit in (("shard", WIDE), ("shard", NEAR), ("shard", SIDE), ("shard", CORE), ("ctx", 1)):
        half = held.shape[0] // 2
        keep, sent = (held, held) if axis == "ctx" else (held[:half], held[half:])
        sent = sent.astype(BF16)
        dep = yield sent
        got = lax.optimization_barrier((swap(sent, axis, bit), dep))[0]
        held = keep + got.astype(F32)
    yield held


def reduce_small(table):
    owned = lax.psum_scatter(table.astype(BF16), "shard", scatter_dimension=0, tiled=True)
    return lax.psum(owned, "ctx").astype(F32)


def head_lanes(shape, head):
    lane = lax.broadcasted_iota(jnp.int32, shape, 1)
    return (lane // HD) == head


def attend_body(part_len, proj_ref, mark_ref, veto_ref, out_ref, norm_ref):
    block = proj_ref[0]
    query, keys, value = (
        block[:part_len, :PAIR],
        block[:, PAIR : 2 * PAIR],
        block[:, 2 * PAIR :],
    )
    scaled = query * jnp.asarray(HD**-0.5, BF16)
    keys_marked = jnp.concatenate([keys, veto_ref[0]], 1)
    results, norms = [], []
    for head in range(2):
        alone = jnp.where(head_lanes(scaled.shape, head), scaled, jnp.zeros_like(scaled))
        scores = inner_right(keys_marked, jnp.concatenate([alone, mark_ref[0]], 1))
        top = jnp.max(scores, axis=0, keepdims=True)
        weights = jnp.exp(scores - top)
        total = jnp.sum(weights, axis=0, keepdims=True)
        result = inner_left(value, weights.astype(BF16))
        results.append(result[head * HD : (head + 1) * HD] * (1.0 / total))
        norms.append(top + jnp.log(total))
    out_ref[0] = jnp.concatenate(results, 0).T.astype(out_ref.dtype)
    norm_ref[0, 0] = jnp.concatenate(norms, 0)


def attend(proj, mark, veto):
    rows, seq_len, columns = proj.shape
    part_len = mark.shape[1]
    pairs = columns // (3 * PAIR)
    return pl.pallas_call(
        functools.partial(attend_body, part_len),
        grid=(rows, pairs),
        in_specs=[
            pl.BlockSpec((1, seq_len, 3 * PAIR), lambda r, j: (r, 0, j)),
            pl.BlockSpec((1, part_len, PAIR), lambda r, j: (r, 0, 0)),
            pl.BlockSpec((1, seq_len, PAIR), lambda r, j: (r, 0, 0)),
        ],
        out_specs=[
            pl.BlockSpec((1, part_len, PAIR), lambda r, j: (r, 0, j)),
            pl.BlockSpec((1, 1, 2, part_len), lambda r, j: (r, j, 0, 0)),
        ],
        out_shape=[
            jax.ShapeDtypeStruct((rows, part_len, pairs * PAIR), BF16),
            jax.ShapeDtypeStruct((rows, pairs, 2, part_len), F32),
        ],
        compiler_params=pltpu.CompilerParams(vmem_limit_bytes=VMEM),
        cost_estimate=LIGHT,
        name="attend",
    )(proj, mark, veto)


def attend_back_body(
    part_len, proj_ref, mark_ref, veto_ref, grad_ref, result_ref, norm_ref, out_ref, sums_ref
):
    block = proj_ref[0]
    seq_len = block.shape[0]
    query, keys, value = (
        block[:part_len, :PAIR],
        block[:, PAIR : 2 * PAIR],
        block[:, 2 * PAIR :],
    )
    scaled = query * jnp.asarray(HD**-0.5, BF16)
    keys_marked = jnp.concatenate([keys, veto_ref[0]], 1)
    grad = grad_ref[0]
    product = (grad.astype(F32) * result_ref[0].astype(F32)).T
    d_query, d_keys, d_value = [], None, None
    for head in range(2):
        lanes = head_lanes(scaled.shape, head)
        alone = jnp.where(lanes, scaled, jnp.zeros_like(scaled))
        grad_alone = jnp.where(lanes, grad, jnp.zeros_like(grad))
        scores = inner_right(keys_marked, jnp.concatenate([alone, mark_ref[0]], 1))
        weights = jnp.exp(scores - norm_ref[0, 0, head : head + 1, :])
        d_weights = inner_right(value, grad_alone)
        inner = jnp.sum(product[head * HD : (head + 1) * HD], axis=0, keepdims=True)
        d_scores = (weights * (d_weights - inner)).astype(BF16)
        more_value = jnp.dot(weights.astype(BF16), grad_alone, preferred_element_type=F32)
        more_keys = jnp.dot(d_scores, alone, preferred_element_type=F32)
        d_value = more_value if d_value is None else d_value + more_value
        d_keys = more_keys if d_keys is None else d_keys + more_keys
        d_query.append(inner_left(keys, d_scores)[head * HD : (head + 1) * HD])
    d_query = jnp.concatenate(d_query, 0).T * HD**-0.5
    out_ref[0, :part_len, :PAIR] = d_query.astype(BF16)
    if seq_len > part_len:
        out_ref[0, part_len:, :PAIR] = jnp.zeros((seq_len - part_len, PAIR), BF16)
    out_ref[0, :, PAIR : 2 * PAIR] = d_keys.astype(BF16)
    out_ref[0, :, 2 * PAIR :] = d_value.astype(BF16)
    sums_ref[0, 0, 0:1] = jnp.sum(d_query, axis=0, keepdims=True)
    sums_ref[0, 0, 1:2] = jnp.sum(d_value, axis=0, keepdims=True)


def attend_back(part, proj, mark, veto, grad, result, norm):
    rows, seq_len, columns = proj.shape
    part_len = mark.shape[1]
    pairs = columns // (3 * PAIR) // 2
    own = pl.BlockSpec((1, part_len, PAIR), lambda r, j: (r, 0, part * pairs + j))
    return pl.pallas_call(
        functools.partial(attend_back_body, part_len),
        grid=(rows, pairs),
        in_specs=[
            pl.BlockSpec((1, seq_len, 3 * PAIR), lambda r, j: (r, 0, part * pairs + j)),
            pl.BlockSpec((1, part_len, PAIR), lambda r, j: (r, 0, 0)),
            pl.BlockSpec((1, seq_len, PAIR), lambda r, j: (r, 0, 0)),
            own,
            own,
            pl.BlockSpec((1, 1, 2, part_len), lambda r, j: (r, part * pairs + j, 0, 0)),
        ],
        out_specs=[
            pl.BlockSpec((1, seq_len, 3 * PAIR), lambda r, j: (r, 0, j)),
            pl.BlockSpec((1, 1, 2, PAIR), lambda r, j: (r, j, 0, 0)),
        ],
        out_shape=[
            jax.ShapeDtypeStruct((rows, seq_len, columns // 2), BF16),
            jax.ShapeDtypeStruct((rows, pairs, 2, PAIR), F32),
        ],
        compiler_params=pltpu.CompilerParams(vmem_limit_bytes=VMEM),
        cost_estimate=LIGHT,
        name="attend_back",
    )(proj, mark, veto, grad, result, norm)


CUTS = 2


def cuts(rows):
    step = rows // CUTS
    return [slice(i * step, (i + 1) * step) for i in range(CUTS)]


def mean_of(value):
    return jnp.mean(value, axis=-1, keepdims=True)


def normalise(value):
    center = value - mean_of(value)
    scale = lax.rsqrt(mean_of(center * center) + 1e-06)
    return center * scale, scale


def normalise_back(unit, scale, incoming, gain):
    edge = incoming * gain
    return scale * (edge - mean_of(edge) - unit * mean_of(edge * unit))


def total(value):
    return jnp.sum(value, axis=0, keepdims=True)


def whole_block(shape):
    return pl.BlockSpec(shape, lambda *_: (0,) * len(shape))


def square(ref):
    return ref[...].reshape(-1, ref.shape[-1])


def kernel(body, grid, name, in_specs, outs, out_specs, scratch=()):
    return pl.pallas_call(
        body,
        grid=grid,
        in_specs=in_specs,
        out_shape=[jax.ShapeDtypeStruct(*out) for out in outs],
        out_specs=out_specs,
        scratch_shapes=scratch,
        compiler_params=pltpu.CompilerParams(vmem_limit_bytes=VMEM),
        cost_estimate=LIGHT,
        name=name,
    )


def middle_body(
    attended,
    tokens,
    w_out,
    w_in,
    w_down,
    in_bias,
    vectors,
    cotangent,
    low,
    active,
    outputs,
    mixed,
    d_hidden,
    first,
    branch,
    d_attended,
    in_sums,
    sums,
    unit,
    scale,
    slope,
    held,
):
    step = pl.program_id(0)
    out_bias, gain_one, shift_one, down_bias, gain_two, shift_two = (
        vectors[i : i + 1] for i in range(6)
    )
    parts = cuts(held.shape[0])

    @pl.when(step == 0)
    def _():
        matrix = square(w_out)
        for cut in parts:
            value = jnp.dot(attended[cut], matrix, preferred_element_type=F32) + out_bias
            u, r = normalise(tokens[cut].astype(F32) + value)
            unit[cut] = u
            scale[cut] = jnp.broadcast_to(r, (r.shape[0], PAIR))
            normed = u * gain_one + shift_one
            low[cut] = normed.astype(BF16)
            held[cut] = normed + down_bias

    @pl.when(step < 4)
    def _():
        up, down = square(w_in), square(w_down)
        for cut in parts:
            hidden = jnp.dot(low[cut], up, preferred_element_type=F32) + in_bias[...]
            below = 0.5 * (1.0 + lax.erf(hidden * 0.7071067811865476))
            active[cut] = (hidden * below).astype(BF16)
            bell = 0.3989422804014327 * jnp.exp(-0.5 * hidden * hidden)
            slope[step, cut] = (below + hidden * bell).astype(BF16)
        for cut in parts:
            held[cut] += jnp.dot(active[cut], down, preferred_element_type=F32)

    @pl.when(step == 3)
    def _():
        totals = []
        for cut in parts:
            u, r = normalise(held[cut])
            outputs[cut] = (u * gain_two + shift_two).astype(BF16)
            incoming = cotangent[cut]
            back = normalise_back(u, r, incoming, gain_two)
            held[cut] = back
            mixed[cut] = back.astype(BF16)
            totals.append((total(incoming * u), total(incoming), total(mixed[cut].astype(F32))))
        for i, item in enumerate(zip(*totals, strict=True)):
            sums[i : i + 1] = sum(item)

    @pl.when(step >= 4)
    def _():
        up, down = square(w_in), square(w_down)
        totals = []
        for cut in parts:
            grad = (inner_right(mixed[cut], down) * slope[step - 4, cut].astype(F32)).astype(BF16)
            d_hidden[cut] = grad
            totals.append(total(grad.astype(F32)))
        in_sums[...] = sum(totals)
        for cut in parts:
            held[cut] += inner_right(d_hidden[cut], up)

    @pl.when(step == 7)
    def _():
        matrix = square(w_out)
        totals = []
        for cut in parts:
            incoming, u = held[cut], unit[cut]
            back = normalise_back(u, scale[cut][:, :1], incoming, gain_one)
            first[cut] = back
            branch[cut] = back.astype(BF16)
            totals.append((total(incoming * u), total(incoming), total(branch[cut].astype(F32))))
        for cut in parts:
            d_attended[cut] = inner_right(branch[cut], matrix).astype(BF16)
        for i, item in enumerate(zip(*totals, strict=True)):
            sums[3 + i : 4 + i] = sum(item)


def middle(attended, tokens, packed, in_bias, vectors, cotangent):
    count, width = tokens.shape
    shards, rows, _ = packed.shape
    once = pl.Buffered(buffer_count=1)
    row = pl.BlockSpec((count, width), lambda s: (0, 0), pipeline_mode=once)
    kept = whole_block((count, width))

    def block(index, depth=shards):
        return pl.BlockSpec((depth, rows // 9 * (shards // depth), width), index)

    forward = pl.BlockSpec((count, width), lambda s: (0, jnp.minimum(s, 3)))
    backward = pl.BlockSpec((count, width), lambda s: (0, jnp.maximum(s - 4, 0)))
    low, tall = ((count, width), BF16), ((count, 4 * width), BF16)
    return kernel(
        middle_body,
        (8,),
        "middle",
        [
            row,
            row,
            pl.BlockSpec((shards, rows // 9, width), lambda s: (0, 8, 0), pipeline_mode=once),
            block(lambda s: (0, 4 + lax.rem(s, 4), 0)),
            block(lambda s: (lax.rem(s, 4), 0, 0), shards // 4),
            pl.BlockSpec((1, width), lambda s: (0, jnp.minimum(s, 3))),
            whole_block((6, width)),
            row,
        ],
        [low, tall, low, low, tall, ((count, width), F32), low, low]
        + [((1, 4 * width), F32), ((6, width), F32)],
        [kept, forward, kept, kept, backward, kept, kept, kept]
        + [pl.BlockSpec((1, width), lambda s: (0, jnp.maximum(s - 4, 0))), whole_block((6, width))],
        [
            pltpu.VMEM((count, width), F32),
            pltpu.VMEM((count, PAIR), F32),
            pltpu.VMEM((4, count, width), BF16),
            pltpu.VMEM((count, width), F32),
        ],
    )(attended, tokens, packed, packed, packed, in_bias, vectors, cotangent)


def input_back_body(block, weight, more, first, *outs):
    step = pl.program_id(0)
    result = inner_right(block[...], weight[...])
    if len(outs) == 1:
        outs[0][...] = result.astype(BF16)
        return
    result = result + more[...].astype(F32)

    @pl.when(step == 0)
    def _():
        outs[0][...] = result + first[...]

    @pl.when(step > 0)
    def _():
        outs[1][...] = result.astype(BF16)


def input_back(part, block, w_qkv, more=None, first=None):
    rows, half = block.shape
    width = w_qkv.shape[0]
    mine = rows // 2
    row = pl.BlockSpec((mine, width), lambda i: (i, 0))
    last = more is not None
    body = input_back_body if last else lambda b, w, o: input_back_body(b, w, None, None, o)
    return kernel(
        body,
        (2,),
        "input_back",
        [
            pl.BlockSpec((mine, half), lambda i: (i, 0)),
            pl.BlockSpec((width, half), lambda i: (0, part)),
            *([row, whole_block((mine, width))] if last else []),
        ],
        [((mine, width), F32), ((mine, width), BF16)] if last else [((rows, width), BF16)],
        [whole_block((mine, width))] * 2 if last else [row],
    )(block, w_qkv, *([more, first] if last else []))


def own_first(value, axis):
    if lax.axis_size("ctx") == 2:
        return jnp.concatenate([value, swap(value, "ctx")], axis)
    whole = lax.all_gather(value, "ctx", axis=axis, tiled=True)
    return jnp.roll(whole, -lax.axis_index("ctx") * value.shape[axis], axis)


def sum_to_owners(value, own_len):
    own = value[:, :own_len].astype(F32)
    if lax.axis_size("ctx") == 2:
        return own + swap(value[:, own_len:].astype(BF16), "ctx").astype(F32)
    whole = jnp.roll(value, lax.axis_index("ctx") * own_len, 1).astype(BF16)
    return lax.psum_scatter(whole, "ctx", scatter_dimension=1, tiled=True).astype(F32)


def on_device(
    tokens,
    segments,
    w_qkv,
    qv_bias,
    w_out,
    out_bias,
    w_in,
    in_bias,
    w_down,
    down_bias,
    gains,
    shifts,
    cotangent,
):
    staged = lax.axis_size("shard") == 16 and lax.axis_size("ctx") == 2
    spot = place() if staged else None
    row_count, part_len, width = tokens.shape
    owned_rows = w_qkv.shape[0]
    pairs = H // 2
    token_count = row_count * part_len

    w_pairs = (
        w_qkv.reshape(owned_rows, 3, pairs, PAIR).transpose(0, 2, 1, 3).reshape(w_qkv.shape)
    )
    small = [qv_bias, out_bias, in_bias, down_bias, gains, shifts]
    sizes = [item.size for item in small]
    flat = jnp.concatenate([item.reshape(-1) for item in small])
    tokens_row = own_first(tokens, 1)
    segments_row = own_first(segments, 1)
    seq_len = tokens_row.shape[1]
    lanes = lax.iota(jnp.int32, PAIR)
    mark = (segments[:, :, None] == lanes).astype(BF16)
    veto = jnp.where(segments_row[:, :, None] == lanes, 0.0, FAR).astype(BF16)

    packed = jnp.concatenate(
        [
            w_down,
            w_in.reshape(owned_rows, 4, width).transpose(1, 0, 2).reshape(-1, width),
            w_out,
        ],
        0,
    )
    if staged:
        table = gather_small(flat)
        w_qkv_all, begun = gather_pairwise(w_pairs, spot, [table, tokens_row])
        packed = after(packed, begun)
    else:
        w_qkv_all = lax.all_gather(w_pairs, "shard", axis=0, tiled=True)
    packed = lax.all_gather(packed, "shard", axis=0)
    if not staged:
        table = lax.all_gather(flat, "shard", axis=0).astype(F32)
    pieces = jnp.split(table, [sum(sizes[:i]) for i in range(1, len(sizes))], axis=1)

    def two(piece):
        return piece.reshape(-1, 2, owned_rows).transpose(1, 0, 2).reshape(2, width)

    qv_all, gain_all, shift_all = two(pieces[0]), two(pieces[4]), two(pieces[5])
    out_all, in_all, down_all = (pieces[i].reshape(-1) for i in (1, 2, 3))

    flat_row = lax.optimization_barrier(tokens_row.reshape(row_count * seq_len, width))
    bias_row = jnp.stack(
        [qv_all[0].reshape(pairs, PAIR), jnp.zeros((pairs, PAIR), F32), qv_all[1].reshape(pairs, PAIR)],
        1,
    )
    raw = jnp.dot(flat_row, w_qkv_all, preferred_element_type=F32) + bias_row.reshape(-1)
    proj = raw.astype(BF16).reshape(row_count, seq_len, 3 * width)
    attended_rows, norm = attend(proj, mark, veto)
    attended = attended_rows.reshape(token_count, width)
    flat_tokens = tokens.reshape(token_count, width)
    vectors = [out_all, gain_all[0], shift_all[0], down_all, gain_all[1], shift_all[1]]
    (
        normed_low,
        active,
        outputs,
        d_mixed,
        d_hidden,
        d_first,
        d_branch,
        d_attended,
        in_sums,
        sums,
    ) = middle(
        attended,
        flat_tokens,
        packed,
        in_all[None],
        jnp.stack(vectors),
        cotangent.reshape(token_count, width),
    )
    outputs = outputs.reshape(row_count, part_len, width)
    d_attended = d_attended.reshape(attended_rows.shape)
    if staged:
        (far_in,) = product_pieces(normed_low, d_hidden, spot, 1)
        here_in = swap(far_in, "shard", CORE)
        active = after(active, far_in)
    part_down = inner_left(active, d_mixed).astype(BF16)
    if staged:
        left = after(normed_low, part_down)
        near_in = product_pieces(left, d_hidden, spot, 0, here_in, (), "both")
        inner = scatter_steps([(*near_in[:2], "ctx"), (*near_in[2:], "side")], spot)
        d_attended = after(d_attended, *next(inner))
    else:
        grad_w_in = reduce_partial(inner_left(normed_low, d_hidden).astype(BF16))
    half = 3 * width // 2
    rows_flat = row_count * seq_len

    def d_tokens_of(part, block):
        return inner_right(block, lax.slice_in_dim(w_qkv_all, part * half, (part + 1) * half, axis=1))

    def attention_back(part, grad):
        block, sums = attend_back(part, proj, mark, veto, grad, attended_rows, norm)
        return block.reshape(rows_flat, half), jnp.sum(sums, axis=0)

    def column_sums(sums_one, sums_two):
        both = jnp.concatenate([sums_one, sums_two], 0).transpose(1, 0, 2).reshape(2, width)
        shards = lax.axis_size("shard")

        def owners(*vectors):
            stacked = jnp.stack(vectors).reshape(len(vectors), shards, -1)
            return stacked.transpose(1, 0, 2).reshape(shards, -1)

        return jnp.concatenate(
            [
                owners(both[0], both[1]),
                owners(sums[5]),
                owners(in_sums[0]),
                owners(sums[2]),
                owners(sums[3], sums[0]),
                owners(sums[4], sums[1]),
            ],
            axis=1,
        )

    d_one, sums_one = attention_back(0, d_attended)
    if staged:
        beside = (attended, d_branch)
        left = after(flat_row, *inner.send(d_one))
        (far,) = product_pieces(left, d_one, spot, 1, None, beside)
        here = swap(far, "shard", CORE)
        d_one = after(d_one, far)
        (d_tokens,) = input_back(0, d_one, w_qkv_all)
        left = after(flat_row, d_tokens)
        near = product_pieces(left, d_one, spot, 0, here, beside, "both")
        one = scatter_steps([(*near[:2], "ctx"), (*near[2:], "side")], spot)
        one_sent = next(one)
        inner_sent = inner.send(one_sent)
        owned_down = lax.psum_scatter(part_down, "shard", scatter_dimension=0, tiled=True)
        d_two, sums_two = attention_back(1, after(d_attended, *one_sent, *inner_sent))
        sent = one.send(d_two) + inner.send(d_two)
        (far,) = product_pieces(after(flat_row, *sent), d_two, spot, 1)
        here = swap(far, "shard", CORE)
        d_two = after(d_two, far)
        owned_down = after(owned_down, far)
        left = after(flat_row, owned_down)
        near = product_pieces(left, d_two, spot, 0, here, (), "ctx")
        two = scatter_steps([(*near, "ctx")], spot)
        two_sent = next(two)
        two_sent = [*two_sent, *one.send(two_sent)]
        down_here = swap(owned_down, "ctx")
        last = after(d_two, *two_sent)
        own_tokens, d_tokens = input_back(1, last, w_qkv_all, d_tokens, d_first)
        tokens_here = swap(d_tokens, "ctx")
        (grad_w_down,) = meet((owned_down, after(down_here, d_tokens)), dtype=F32)
        table = column_sums(sums_one, after(sums_two, grad_w_down))
        small_sums = small_steps(table)
        sent = two.send([next(small_sums)])
        sent = one.send(sent)
        sent = [small_sums.send(sent)]
        sent = two.send(sent)
        sent = [small_sums.send(sent)]
        grad_tokens = own_tokens + after(tokens_here, *sent).astype(F32)
        grad_tokens = grad_tokens.reshape(row_count, part_len, width)
        sent = two.send([*sent, grad_tokens])
        sent = [small_sums.send(sent)]
        sent = [small_sums.send(sent)]
        owned = small_sums.send(sent)[0]
        grad_w_in = owned_rows_of(next(inner))
        second, first = next(two), next(one)
        grad_pairs = owned_rows_of(jnp.concatenate([first[..., : 3 * PAIR], second], 0))
        grad_w_out = owned_rows_of(first[..., 3 * PAIR :])
    else:
        d_two, sums_two = attention_back(1, d_attended)
        d_tokens = (d_tokens_of(0, d_one) + d_tokens_of(1, d_two)).reshape(row_count, seq_len, width)
        grad_tokens = d_first.reshape(row_count, part_len, width) + sum_to_owners(d_tokens, part_len)
        grad_w_down = reduce_partial(part_down)
        grad_w_out = reduce_partial(inner_left(attended, d_branch).astype(BF16))
        together = inner_left(flat_row, jnp.concatenate([d_one, d_two], 1))
        grad_pairs = reduce_partial(together.astype(BF16))
        owned = reduce_small(column_sums(sums_one, sums_two))[0]
    grad_w_qkv = (
        grad_pairs.reshape(owned_rows, pairs, 3, PAIR).transpose(0, 2, 1, 3).reshape(w_qkv.shape)
    )
    owned = jnp.split(owned, [sum(sizes[:i]) for i in range(1, len(sizes))])
    return (
        outputs,
        grad_tokens,
        grad_w_qkv,
        owned[0].reshape(qv_bias.shape),
        grad_w_out,
        owned[1],
        grad_w_in,
        owned[2],
        grad_w_down,
        owned[3],
        owned[4].reshape(gains.shape),
        owned[5].reshape(shifts.shape),
    )


def solution(mesh):
    row, flat = P("shard", None), P("shard")
    wide, whole = P(None, "shard"), P("shard", "ctx", None)
    return jax.shard_map(
        on_device,
        mesh=mesh,
        in_specs=(
            whole,
            P("shard", "ctx"),
            row,
            wide,
            row,
            flat,
            row,
            flat,
            row,
            flat,
            wide,
            wide,
            whole,
        ),
        out_specs=(whole, whole, row, wide, row, flat, row, flat, row, flat, wide, wide),
        check_vma=False,
    )
```

```python
import functools

import jax
import jax.numpy as jnp
from jax import lax
from jax.experimental import pallas as pl
from jax.experimental.pallas import tpu as pltpu
from jax.sharding import PartitionSpec as P

H = 16
HD = 64
PAIR = 2 * HD
FAR = -1e30
LIGHT = pl.CostEstimate(flops=0, bytes_accessed=0, transcendentals=0)
VMEM = 60 * 1024 * 1024
CORE, SIDE, NEAR, WIDE = 1, 2, 4, 8

F32 = jnp.float32
BF16 = jnp.bfloat16


def inner_left(left, right):
    return lax.dot_general(left, right, (((0,), (0,)), ((), ())), preferred_element_type=F32)


def inner_right(left, right):
    return lax.dot_general(left, right, (((1,), (1,)), ((), ())), preferred_element_type=F32)


def swap(value, axis, bit=1):
    return lax.ppermute(value, axis, [(i, i ^ bit) for i in range(lax.axis_size(axis))])


def by_side(own_is_first, own, other, axis):
    return jnp.where(
        own_is_first,
        jnp.concatenate([own, other], axis),
        jnp.concatenate([other, own], axis),
    )


def place():
    shard, ctx = lax.axis_index("shard"), lax.axis_index("ctx")
    return shard % 2, (shard // 2) % 2, (shard // 4) % 2, shard // 8, ctx


def assemble_body(depth, width, where_ref, *refs):
    pieces, out, sems = refs[:2], refs[2], refs[3]
    core, side, near, wide, ctx = (where_ref[i] for i in range(5))
    copies = []
    for index in range(16):
        far_core, part, second, first = index // 8, (index // 4) % 2, (index // 2) % 2, index % 2
        side_rel, ctx_rel = (first, second) if part == 0 else (second, first)
        column = ((core ^ far_core) * 2 + (ctx ^ ctx_rel)) * 2 + part
        for k in range(4):
            row = (((wide ^ (k % 2)) * 2 + (near ^ (k // 2))) * 2) + (side ^ side_rel)
            target = out.at[
                pl.ds(pl.multiple_of(row * depth, depth), depth),
                pl.ds(pl.multiple_of(column * width, width), width),
            ]
            source = pieces[far_core].at[index % 8 * 4 + k]
            copies.append(pltpu.make_async_copy(source, target, sems.at[len(copies)]))
    for copy in copies:
        copy.start()
    for copy in copies:
        copy.wait()


def gather_pairwise(shard, spot, others):
    rows, columns = shard.shape
    width = columns // 8
    core, side, near, wide, ctx = spot
    split = shard.reshape(rows, 8, width).transpose(1, 0, 2).reshape(2, 2, 2, rows, width)
    mine = lax.dynamic_index_in_dim(split, ctx, 1, False)
    own = lax.dynamic_index_in_dim(mine, core, 0, False)
    other = lax.dynamic_index_in_dim(mine, 1 - core, 0, False)
    held = by_side(core == 0, own, swap(other, "shard", CORE), 1)[None]
    for bit in (WIDE, NEAR):
        held = jnp.concatenate([held, swap(held, "shard", bit)], 0)
        begun = held if bit == WIDE else begun
    held = [held[:, 0], held[:, 1]]
    along = (("shard", SIDE), ("ctx", 1))
    for routes in (along, along[::-1]):
        held = [
            jnp.concatenate([value, swap(value, *route)], 0)
            for value, route in zip(held, routes, strict=True)
        ]
        if routes is along:
            held = [after(value, *others) for value in held]
    here = jnp.concatenate(held, 0)
    whole = pl.pallas_call(
        functools.partial(assemble_body, 2 * rows, width),
        out_shape=jax.ShapeDtypeStruct((16 * rows, columns), BF16),
        in_specs=[pl.BlockSpec(memory_space=pltpu.SMEM)]
        + [pl.BlockSpec(memory_space=pl.ANY)] * 2,
        out_specs=pl.BlockSpec(memory_space=pltpu.VMEM),
        scratch_shapes=[pltpu.SemaphoreType.DMA((64,))],
        compiler_params=pltpu.CompilerParams(vmem_limit_bytes=VMEM),
        cost_estimate=LIGHT,
        name="assemble",
    )(jnp.stack(spot).astype(jnp.int32), here, swap(here, "shard", CORE))
    return whole, begun


def gather_small(flat):
    held = flat[None]
    for bit in (CORE, SIDE, NEAR, WIDE):
        held = jnp.concatenate([held, swap(held, "shard", bit)], 0)
    return pick_rows(held)


def pick_rows(held):
    count = held.shape[0]
    index = lax.iota(jnp.int32, count) ^ lax.axis_index("shard")
    choose = (index[:, None] == lax.iota(jnp.int32, count)[None, :]).astype(F32)
    return jnp.dot(choose, held.astype(F32), precision=lax.Precision.HIGHEST)


def product_body(depth, beside, adds, split, where_ref, left_ref, right_ref, *refs):
    side, near, wide = (where_ref[i] for i in range(1, 4))
    result = inner_left(left_ref[...], right_ref[...])
    if beside:
        result = jnp.concatenate([result, inner_left(refs[0][...], refs[1][...])], 1)
    outs = refs[-4:] if split == "both" else refs[-2:] if split else refs[-1:]

    def values():
        for i in range(8):
            z, y = i // 2, i % 2
            row = (y ^ side) * 4 + ((z % 2) ^ near) * 2 + ((z // 2) ^ wide)
            value = result[i * depth : (i + 1) * depth]
            if adds:
                value = value + refs[2 * beside][0, row].astype(F32)
            yield y ^ side, row, value.astype(BF16)

    def by_ctx(pair, pick):
        for index in range(2):

            @pl.when(pl.program_id(0) == index)
            def _(index=index):
                for _, row, value in values():
                    pair[index][row] = pick(value)

    def by_row(pair, pick):
        for far_side, row, value in values():
            for index in range(2):

                @pl.when(far_side == index)
                def _(index=index, row=row, value=value):
                    pair[index][0, row - 4 * index] = pick(value)

    if split == "both":
        middle = outs[0].shape[-1]
        by_ctx(outs[:2], lambda value: value[:, :middle])
        by_row(outs[2:], lambda value: value[:, middle:])
    elif split == "ctx":
        by_ctx(outs, lambda value: value)
    elif split == "side":
        by_row(outs, lambda value: value)
    else:
        for _, row, value in values():
            outs[0][0, row] = value


def product_pieces(left, right, spot, far, received=None, beside=(), split=None):
    tokens, rows = left.shape
    depth = rows // 8
    pairs = [(left, right), *([beside] if beside else [])]
    specs, full = [], 0
    for one, two in pairs:
        width = two.shape[1] // 4
        full += width
        specs += [
            pl.BlockSpec(one.shape, lambda j, w: (0, 0)),
            pl.BlockSpec((two.shape[0], width), lambda j, w: (0, (w[0] ^ far) * 2 + (w[4] ^ j))),
        ]
    out_spec = pl.BlockSpec((1, 8, depth, full), lambda j, w: (j, 0, 0, 0))
    in_specs = specs + ([out_spec] if received is not None else [])
    along_ctx = lambda n: ((8, depth, n), pl.BlockSpec((8, depth, n), lambda j, w: (0, 0, 0)))
    along_side = lambda n: (
        (2, 4, depth, n),
        pl.BlockSpec((1, 4, depth, n), lambda j, w: (j, 0, 0, 0)),
    )
    if split == "both":
        last = full // 256 * 128
        outs = [along_ctx(full - last)] * 2 + [along_side(last)] * 2
    elif split:
        outs = [along_ctx(full) if split == "ctx" else along_side(full)] * 2
    else:
        outs = [((2, 8, depth, full), out_spec)]
    adds = received is not None
    return pl.pallas_call(
        functools.partial(product_body, depth, bool(beside), adds, split),
        grid_spec=pltpu.PrefetchScalarGridSpec(
            num_scalar_prefetch=1,
            grid=(2,),
            in_specs=in_specs,
            out_specs=[spec for _, spec in outs],
        ),
        out_shape=[jax.ShapeDtypeStruct(shape, BF16) for shape, _ in outs],
        compiler_params=pltpu.CompilerParams(vmem_limit_bytes=VMEM),
        cost_estimate=LIGHT,
        name="weight_gradient",
    )(jnp.stack(spot).astype(jnp.int32), left, right, *beside, *([received] if adds else []))


def meet_body(parts, refs, outs):
    value = [
        refs[2 * i][...].astype(F32) + refs[2 * i + 1][...].astype(F32) for i in range(parts)
    ]
    value = value[0] if parts == 1 else jnp.concatenate(value, -1)
    if len(outs) == 1:
        outs[0][...] = value.astype(outs[0].dtype)
    else:
        outs[0][...] = value[0].astype(BF16)
        outs[1][...] = value[1].astype(BF16)


def meet(*pairs, dtype=BF16):
    rows = pairs[0][0].shape[-2]
    halves = pairs[0][0].ndim == 3
    widths = [left.shape[-1] for left, _ in pairs]
    columns = sum(widths)
    steps = 4 if rows % 64 == 0 and rows * columns > 1 << 18 else 1
    count = 2 * len(pairs)

    def spec(width, leading):
        if leading:
            return pl.BlockSpec((2, rows // steps, width), lambda i: (0, i, 0))
        return pl.BlockSpec((rows // steps, width), lambda i: (i, 0))

    outs = 2 if halves else 1
    return pl.pallas_call(
        lambda *refs: meet_body(len(pairs), refs[:count], refs[count:]),
        grid=(steps,),
        in_specs=[spec(width, halves) for width in widths for _ in range(2)],
        out_specs=[spec(columns, False)] * outs,
        out_shape=[jax.ShapeDtypeStruct((rows, columns), dtype)] * outs,
        compiler_params=pltpu.CompilerParams(vmem_limit_bytes=VMEM),
        cost_estimate=LIGHT,
        name="meet",
    )(*[item for pair in pairs for item in pair])


def owner_body(active, mixed, attended, branch, out):
    down = inner_left(active[...], mixed[...]).astype(BF16)
    outer = inner_left(attended[...], branch[...]).astype(BF16)
    tall, short = down.shape[0] // 2, outer.shape[0] // 2
    for i in range(2):
        out[i, :tall] = down[i * tall : (i + 1) * tall]
        out[i, tall:] = outer[i * short : (i + 1) * short]


def owner_gradients(active, mixed, attended, branch, shards):
    count, width = mixed.shape
    tall, short = active.shape[1] // shards, width // shards
    return pl.pallas_call(
        owner_body,
        grid=(shards // 2,),
        in_specs=[
            pl.BlockSpec((count, 2 * tall), lambda i: (0, i)),
            pl.BlockSpec((count, width), lambda i: (0, 0)),
            pl.BlockSpec((count, 2 * short), lambda i: (0, i)),
            pl.BlockSpec((count, width), lambda i: (0, 0)),
        ],
        out_specs=pl.BlockSpec((2, tall + short, width), lambda i: (i, 0, 0)),
        out_shape=jax.ShapeDtypeStruct((shards, tall + short, width), BF16),
        compiler_params=pltpu.CompilerParams(vmem_limit_bytes=VMEM),
        cost_estimate=LIGHT,
        name="owner_gradients",
    )(active, mixed, attended, branch)


def scatter_steps(parts, spot):
    depth = parts[0][0].shape[-2]
    core, ctx = spot[0], spot[4]

    def both(value):
        return value.reshape(2, value.size // value.shape[-1] // 2, value.shape[-1])

    def gated(dep, got):
        return got if dep is None else lax.optimization_barrier((got, dep))[0]

    along = {"side": ("shard", SIDE), "ctx": ("ctx", 1)}
    other = {"side": "ctx", "ctx": "side"}
    dep = yield [sent for _, sent, _ in parts]
    moved = []
    for keep, sent, name in parts:
        got = gated(dep, swap(sent, *along[name]))
        keep, sent = meet((both(keep), both(got)))
        moved.append((keep, sent, other[name]))
    dep = yield [sent for _, sent, _ in moved]
    keep, sent = meet(
        *[(both(keep), both(gated(dep, swap(sent, *along[name])))) for keep, sent, name in moved]
    )
    dep = yield [sent]
    keep, sent = meet((both(keep), both(gated(dep, swap(sent, "shard", NEAR)))))
    dep = yield [sent]
    (held,) = meet((keep, gated(dep, swap(sent, "shard", WIDE))))
    yield [held]
    rows = depth // 2
    mine = lax.dynamic_slice_in_dim(held, core * rows, rows, 0)
    other = lax.dynamic_slice_in_dim(held, (1 - core) * rows, rows, 0)
    shards = lax.axis_size("shard")
    across = [(i, i ^ 3) for i in range(2 * shards)]
    corner = lax.ppermute(other, ("shard", "ctx"), across)
    here = by_side(ctx == 0, mine[None], swap(mine, "ctx")[None], 0)
    there = by_side(ctx == 0, swap(other, "shard", CORE)[None], corner[None], 0)
    yield by_side(core == 0, here, there, 0)


def owned_rows_of(pieces):
    count, rows, width = pieces.shape
    return pieces.transpose(1, 0, 2).reshape(rows, count * width).astype(F32)


def reduce_partial(partial):
    owned = lax.psum_scatter(partial, "shard", scatter_dimension=0, tiled=True)
    return lax.psum(owned, "ctx").astype(F32)


def after(value, *others):
    return lax.optimization_barrier((value, *others))[0]


def small_steps(table):
    held = pick_rows(table)
    for axis, bit in (("shard", WIDE), ("shard", NEAR), ("shard", SIDE), ("shard", CORE), ("ctx", 1)):
        half = held.shape[0] // 2
        keep, sent = (held, held) if axis == "ctx" else (held[:half], held[half:])
        sent = sent.astype(BF16)
        dep = yield sent
        got = lax.optimization_barrier((swap(sent, axis, bit), dep))[0]
        held = keep + got.astype(F32)
    yield held


def reduce_small(table):
    owned = lax.psum_scatter(table.astype(BF16), "shard", scatter_dimension=0, tiled=True)
    return lax.psum(owned, "ctx").astype(F32)


def head_lanes(shape, head):
    lane = lax.broadcasted_iota(jnp.int32, shape, 1)
    return (lane // HD) == head


def attend_body(part_len, proj_ref, mark_ref, veto_ref, out_ref, norm_ref):
    block = proj_ref[0]
    query, keys, value = (
        block[:part_len, :PAIR],
        block[:, PAIR : 2 * PAIR],
        block[:, 2 * PAIR :],
    )
    scaled = query * jnp.asarray(HD**-0.5, BF16)
    keys_marked = jnp.concatenate([keys, veto_ref[0]], 1)
    results, norms = [], []
    for head in range(2):
        alone = jnp.where(head_lanes(scaled.shape, head), scaled, jnp.zeros_like(scaled))
        scores = inner_right(keys_marked, jnp.concatenate([alone, mark_ref[0]], 1))
        top = jnp.max(scores, axis=0, keepdims=True)
        weights = jnp.exp(scores - top)
        total = jnp.sum(weights, axis=0, keepdims=True)
        result = inner_left(value, weights.astype(BF16))
        results.append(result[head * HD : (head + 1) * HD] * (1.0 / total))
        norms.append(top + jnp.log(total))
    out_ref[0] = jnp.concatenate(results, 0).T.astype(out_ref.dtype)
    norm_ref[0, 0] = jnp.concatenate(norms, 0)


def attend(proj, mark, veto):
    rows, seq_len, columns = proj.shape
    part_len = mark.shape[1]
    pairs = columns // (3 * PAIR)
    return pl.pallas_call(
        functools.partial(attend_body, part_len),
        grid=(rows, pairs),
        in_specs=[
            pl.BlockSpec((1, seq_len, 3 * PAIR), lambda r, j: (r, 0, j)),
            pl.BlockSpec((1, part_len, PAIR), lambda r, j: (r, 0, 0)),
            pl.BlockSpec((1, seq_len, PAIR), lambda r, j: (r, 0, 0)),
        ],
        out_specs=[
            pl.BlockSpec((1, part_len, PAIR), lambda r, j: (r, 0, j)),
            pl.BlockSpec((1, 1, 2, part_len), lambda r, j: (r, j, 0, 0)),
        ],
        out_shape=[
            jax.ShapeDtypeStruct((rows, part_len, pairs * PAIR), BF16),
            jax.ShapeDtypeStruct((rows, pairs, 2, part_len), F32),
        ],
        compiler_params=pltpu.CompilerParams(vmem_limit_bytes=VMEM),
        cost_estimate=LIGHT,
        name="attend",
    )(proj, mark, veto)


def attend_back_body(
    part_len, proj_ref, mark_ref, veto_ref, grad_ref, result_ref, norm_ref, out_ref, sums_ref
):
    block = proj_ref[0]
    seq_len = block.shape[0]
    query, keys, value = (
        block[:part_len, :PAIR],
        block[:, PAIR : 2 * PAIR],
        block[:, 2 * PAIR :],
    )
    scaled = query * jnp.asarray(HD**-0.5, BF16)
    keys_marked = jnp.concatenate([keys, veto_ref[0]], 1)
    grad = grad_ref[0]
    product = (grad.astype(F32) * result_ref[0].astype(F32)).T
    d_query, d_keys, d_value = [], None, None
    for head in range(2):
        lanes = head_lanes(scaled.shape, head)
        alone = jnp.where(lanes, scaled, jnp.zeros_like(scaled))
        grad_alone = jnp.where(lanes, grad, jnp.zeros_like(grad))
        scores = inner_right(keys_marked, jnp.concatenate([alone, mark_ref[0]], 1))
        weights = jnp.exp(scores - norm_ref[0, 0, head : head + 1, :])
        d_weights = inner_right(value, grad_alone)
        inner = jnp.sum(product[head * HD : (head + 1) * HD], axis=0, keepdims=True)
        d_scores = (weights * (d_weights - inner)).astype(BF16)
        more_value = jnp.dot(weights.astype(BF16), grad_alone, preferred_element_type=F32)
        more_keys = jnp.dot(d_scores, alone, preferred_element_type=F32)
        d_value = more_value if d_value is None else d_value + more_value
        d_keys = more_keys if d_keys is None else d_keys + more_keys
        d_query.append(inner_left(keys, d_scores)[head * HD : (head + 1) * HD])
    d_query = jnp.concatenate(d_query, 0).T * HD**-0.5
    out_ref[0, :part_len, :PAIR] = d_query.astype(BF16)
    if seq_len > part_len:
        out_ref[0, part_len:, :PAIR] = jnp.zeros((seq_len - part_len, PAIR), BF16)
    out_ref[0, :, PAIR : 2 * PAIR] = d_keys.astype(BF16)
    out_ref[0, :, 2 * PAIR :] = d_value.astype(BF16)
    sums_ref[0, 0, 0:1] = jnp.sum(d_query, axis=0, keepdims=True)
    sums_ref[0, 0, 1:2] = jnp.sum(d_value, axis=0, keepdims=True)


def attend_back(part, proj, mark, veto, grad, result, norm):
    rows, seq_len, columns = proj.shape
    part_len = mark.shape[1]
    pairs = columns // (3 * PAIR) // 2
    own = pl.BlockSpec((1, part_len, PAIR), lambda r, j: (r, 0, part * pairs + j))
    return pl.pallas_call(
        functools.partial(attend_back_body, part_len),
        grid=(rows, pairs),
        in_specs=[
            pl.BlockSpec((1, seq_len, 3 * PAIR), lambda r, j: (r, 0, part * pairs + j)),
            pl.BlockSpec((1, part_len, PAIR), lambda r, j: (r, 0, 0)),
            pl.BlockSpec((1, seq_len, PAIR), lambda r, j: (r, 0, 0)),
            own,
            own,
            pl.BlockSpec((1, 1, 2, part_len), lambda r, j: (r, part * pairs + j, 0, 0)),
        ],
        out_specs=[
            pl.BlockSpec((1, seq_len, 3 * PAIR), lambda r, j: (r, 0, j)),
            pl.BlockSpec((1, 1, 2, PAIR), lambda r, j: (r, j, 0, 0)),
        ],
        out_shape=[
            jax.ShapeDtypeStruct((rows, seq_len, columns // 2), BF16),
            jax.ShapeDtypeStruct((rows, pairs, 2, PAIR), F32),
        ],
        compiler_params=pltpu.CompilerParams(vmem_limit_bytes=VMEM),
        cost_estimate=LIGHT,
        name="attend_back",
    )(proj, mark, veto, grad, result, norm)


CUTS = 2


def cuts(rows):
    step = rows // CUTS
    return [slice(i * step, (i + 1) * step) for i in range(CUTS)]


def mean_of(value):
    return jnp.mean(value, axis=-1, keepdims=True)


def normalise(value):
    center = value - mean_of(value)
    scale = lax.rsqrt(mean_of(center * center) + 1e-06)
    return center * scale, scale


def normalise_back(unit, scale, incoming, gain):
    edge = incoming * gain
    return scale * (edge - mean_of(edge) - unit * mean_of(edge * unit))


def total(value):
    return jnp.sum(value, axis=0, keepdims=True)


def whole_block(shape):
    return pl.BlockSpec(shape, lambda *_: (0,) * len(shape))


def square(ref):
    return ref[...].reshape(-1, ref.shape[-1])


def kernel(body, grid, name, in_specs, outs, out_specs, scratch=()):
    return pl.pallas_call(
        body,
        grid=grid,
        in_specs=in_specs,
        out_shape=[jax.ShapeDtypeStruct(*out) for out in outs],
        out_specs=out_specs,
        scratch_shapes=scratch,
        compiler_params=pltpu.CompilerParams(vmem_limit_bytes=VMEM),
        cost_estimate=LIGHT,
        name=name,
    )


def middle_body(
    attended,
    tokens,
    w_out,
    w_in,
    w_down,
    in_bias,
    vectors,
    cotangent,
    low,
    active,
    outputs,
    mixed,
    d_hidden,
    first,
    branch,
    d_attended,
    in_sums,
    sums,
    unit,
    scale,
    slope,
    held,
):
    step = pl.program_id(0)
    out_bias, gain_one, shift_one, down_bias, gain_two, shift_two = (
        vectors[i : i + 1] for i in range(6)
    )
    parts = cuts(held.shape[0])

    @pl.when(step == 0)
    def _():
        matrix = square(w_out)
        for cut in parts:
            value = jnp.dot(attended[cut], matrix, preferred_element_type=F32) + out_bias
            u, r = normalise(tokens[cut].astype(F32) + value)
            unit[cut] = u
            scale[cut] = jnp.broadcast_to(r, (r.shape[0], PAIR))
            normed = u * gain_one + shift_one
            low[cut] = normed.astype(BF16)
            held[cut] = normed + down_bias

    @pl.when(step < 4)
    def _():
        up, down = square(w_in), square(w_down)
        for cut in parts:
            hidden = jnp.dot(low[cut], up, preferred_element_type=F32) + in_bias[...]
            below = 0.5 * (1.0 + lax.erf(hidden * 0.7071067811865476))
            active[cut] = (hidden * below).astype(BF16)
            bell = 0.3989422804014327 * jnp.exp(-0.5 * hidden * hidden)
            slope[step, cut] = (below + hidden * bell).astype(BF16)
        for cut in parts:
            held[cut] += jnp.dot(active[cut], down, preferred_element_type=F32)

    @pl.when(step == 3)
    def _():
        totals = []
        for cut in parts:
            u, r = normalise(held[cut])
            outputs[cut] = (u * gain_two + shift_two).astype(BF16)
            incoming = cotangent[cut]
            back = normalise_back(u, r, incoming, gain_two)
            held[cut] = back
            mixed[cut] = back.astype(BF16)
            totals.append((total(incoming * u), total(incoming), total(mixed[cut].astype(F32))))
        for i, item in enumerate(zip(*totals, strict=True)):
            sums[i : i + 1] = sum(item)

    @pl.when(step >= 4)
    def _():
        up, down = square(w_in), square(w_down)
        totals = []
        for cut in parts:
            grad = (inner_right(mixed[cut], down) * slope[step - 4, cut].astype(F32)).astype(BF16)
            d_hidden[cut] = grad
            totals.append(total(grad.astype(F32)))
        in_sums[...] = sum(totals)
        for cut in parts:
            held[cut] += inner_right(d_hidden[cut], up)

    @pl.when(step == 7)
    def _():
        matrix = square(w_out)
        totals = []
        for cut in parts:
            incoming, u = held[cut], unit[cut]
            back = normalise_back(u, scale[cut][:, :1], incoming, gain_one)
            first[cut] = back
            branch[cut] = back.astype(BF16)
            totals.append((total(incoming * u), total(incoming), total(branch[cut].astype(F32))))
        for cut in parts:
            d_attended[cut] = inner_right(branch[cut], matrix).astype(BF16)
        for i, item in enumerate(zip(*totals, strict=True)):
            sums[3 + i : 4 + i] = sum(item)


def middle(attended, tokens, packed, in_bias, vectors, cotangent):
    count, width = tokens.shape
    shards, rows, _ = packed.shape
    once = pl.Buffered(buffer_count=1)
    row = pl.BlockSpec((count, width), lambda s: (0, 0), pipeline_mode=once)
    kept = whole_block((count, width))

    def block(index, depth=shards):
        return pl.BlockSpec((depth, rows // 9 * (shards // depth), width), index)

    forward = pl.BlockSpec((count, width), lambda s: (0, jnp.minimum(s, 3)))
    backward = pl.BlockSpec((count, width), lambda s: (0, jnp.maximum(s - 4, 0)))
    low, tall = ((count, width), BF16), ((count, 4 * width), BF16)
    return kernel(
        middle_body,
        (8,),
        "middle",
        [
            row,
            row,
            pl.BlockSpec((shards, rows // 9, width), lambda s: (0, 8, 0), pipeline_mode=once),
            block(lambda s: (0, 4 + lax.rem(s, 4), 0)),
            block(lambda s: (lax.rem(s, 4), 0, 0), shards // 4),
            pl.BlockSpec((1, width), lambda s: (0, jnp.minimum(s, 3))),
            whole_block((6, width)),
            row,
        ],
        [low, tall, low, low, tall, ((count, width), F32), low, low]
        + [((1, 4 * width), F32), ((6, width), F32)],
        [kept, forward, kept, kept, backward, kept, kept, kept]
        + [pl.BlockSpec((1, width), lambda s: (0, jnp.maximum(s - 4, 0))), whole_block((6, width))],
        [
            pltpu.VMEM((count, width), F32),
            pltpu.VMEM((count, PAIR), F32),
            pltpu.VMEM((4, count, width), BF16),
            pltpu.VMEM((count, width), F32),
        ],
    )(attended, tokens, packed, packed, packed, in_bias, vectors, cotangent)


def input_back_body(block, weight, more, first, *outs):
    step = pl.program_id(0)
    result = inner_right(block[...], weight[...])
    if len(outs) == 1:
        outs[0][...] = result.astype(BF16)
        return
    result = result + more[...].astype(F32)

    @pl.when(step == 0)
    def _():
        outs[0][...] = result + first[...]

    @pl.when(step > 0)
    def _():
        outs[1][...] = result.astype(BF16)


def input_back(part, block, w_qkv, more=None, first=None):
    rows, half = block.shape
    width = w_qkv.shape[0]
    mine = rows // 2
    row = pl.BlockSpec((mine, width), lambda i: (i, 0))
    last = more is not None
    body = input_back_body if last else lambda b, w, o: input_back_body(b, w, None, None, o)
    return kernel(
        body,
        (2,),
        "input_back",
        [
            pl.BlockSpec((mine, half), lambda i: (i, 0)),
            pl.BlockSpec((width, half), lambda i: (0, part)),
            *([row, whole_block((mine, width))] if last else []),
        ],
        [((mine, width), F32), ((mine, width), BF16)] if last else [((rows, width), BF16)],
        [whole_block((mine, width))] * 2 if last else [row],
    )(block, w_qkv, *([more, first] if last else []))


def own_first(value, axis):
    if lax.axis_size("ctx") == 2:
        return jnp.concatenate([value, swap(value, "ctx")], axis)
    whole = lax.all_gather(value, "ctx", axis=axis, tiled=True)
    return jnp.roll(whole, -lax.axis_index("ctx") * value.shape[axis], axis)


def sum_to_owners(value, own_len):
    own = value[:, :own_len].astype(F32)
    if lax.axis_size("ctx") == 2:
        return own + swap(value[:, own_len:].astype(BF16), "ctx").astype(F32)
    whole = jnp.roll(value, lax.axis_index("ctx") * own_len, 1).astype(BF16)
    return lax.psum_scatter(whole, "ctx", scatter_dimension=1, tiled=True).astype(F32)


def on_device(
    tokens,
    segments,
    w_qkv,
    qv_bias,
    w_out,
    out_bias,
    w_in,
    in_bias,
    w_down,
    down_bias,
    gains,
    shifts,
    cotangent,
):
    staged = lax.axis_size("shard") == 16 and lax.axis_size("ctx") == 2
    spot = place() if staged else None
    row_count, part_len, width = tokens.shape
    owned_rows = w_qkv.shape[0]
    pairs = H // 2
    token_count = row_count * part_len

    w_pairs = (
        w_qkv.reshape(owned_rows, 3, pairs, PAIR).transpose(0, 2, 1, 3).reshape(w_qkv.shape)
    )
    small = [qv_bias, out_bias, in_bias, down_bias, gains, shifts]
    sizes = [item.size for item in small]
    flat = jnp.concatenate([item.reshape(-1) for item in small])
    tokens_row = own_first(tokens, 1)
    segments_row = own_first(segments, 1)
    seq_len = tokens_row.shape[1]
    lanes = lax.iota(jnp.int32, PAIR)
    mark = (segments[:, :, None] == lanes).astype(BF16)
    veto = jnp.where(segments_row[:, :, None] == lanes, 0.0, FAR).astype(BF16)

    packed = jnp.concatenate(
        [
            w_down,
            w_in.reshape(owned_rows, 4, width).transpose(1, 0, 2).reshape(-1, width),
            w_out,
        ],
        0,
    )
    if staged:
        table = gather_small(flat)
        w_qkv_all, begun = gather_pairwise(w_pairs, spot, [table, tokens_row])
        packed = after(packed, begun)
    else:
        w_qkv_all = lax.all_gather(w_pairs, "shard", axis=0, tiled=True)
    packed = lax.all_gather(packed, "shard", axis=0)
    if not staged:
        table = lax.all_gather(flat, "shard", axis=0).astype(F32)
    pieces = jnp.split(table, [sum(sizes[:i]) for i in range(1, len(sizes))], axis=1)

    def two(piece):
        return piece.reshape(-1, 2, owned_rows).transpose(1, 0, 2).reshape(2, width)

    qv_all, gain_all, shift_all = two(pieces[0]), two(pieces[4]), two(pieces[5])
    out_all, in_all, down_all = (pieces[i].reshape(-1) for i in (1, 2, 3))

    flat_row = lax.optimization_barrier(tokens_row.reshape(row_count * seq_len, width))
    bias_row = jnp.stack(
        [qv_all[0].reshape(pairs, PAIR), jnp.zeros((pairs, PAIR), F32), qv_all[1].reshape(pairs, PAIR)],
        1,
    )
    raw = jnp.dot(flat_row, w_qkv_all, preferred_element_type=F32) + bias_row.reshape(-1)
    proj = raw.astype(BF16).reshape(row_count, seq_len, 3 * width)
    attended_rows, norm = attend(proj, mark, veto)
    attended = attended_rows.reshape(token_count, width)
    flat_tokens = tokens.reshape(token_count, width)
    vectors = [out_all, gain_all[0], shift_all[0], down_all, gain_all[1], shift_all[1]]
    (
        normed_low,
        active,
        outputs,
        d_mixed,
        d_hidden,
        d_first,
        d_branch,
        d_attended,
        in_sums,
        sums,
    ) = middle(
        attended,
        flat_tokens,
        packed,
        in_all[None],
        jnp.stack(vectors),
        cotangent.reshape(token_count, width),
    )
    outputs = outputs.reshape(row_count, part_len, width)
    d_attended = d_attended.reshape(attended_rows.shape)
    if staged:
        (far_in,) = product_pieces(normed_low, d_hidden, spot, 1)
        here_in = swap(far_in, "shard", CORE)
        active = after(active, far_in)
    if staged:
        part_down = owner_gradients(active, d_mixed, attended, d_branch, lax.axis_size("shard"))
        left = after(normed_low, part_down)
        near_in = product_pieces(left, d_hidden, spot, 0, here_in, (), "both")
        inner = scatter_steps([(*near_in[:2], "ctx"), (*near_in[2:], "side")], spot)
        d_attended = after(d_attended, *next(inner))
    else:
        grad_w_in = reduce_partial(inner_left(normed_low, d_hidden).astype(BF16))
    half = 3 * width // 2
    rows_flat = row_count * seq_len

    def d_tokens_of(part, block):
        return inner_right(block, lax.slice_in_dim(w_qkv_all, part * half, (part + 1) * half, axis=1))

    def attention_back(part, grad):
        block, sums = attend_back(part, proj, mark, veto, grad, attended_rows, norm)
        return block.reshape(rows_flat, half), jnp.sum(sums, axis=0)

    def column_sums(sums_one, sums_two):
        both = jnp.concatenate([sums_one, sums_two], 0).transpose(1, 0, 2).reshape(2, width)
        shards = lax.axis_size("shard")

        def owners(*vectors):
            stacked = jnp.stack(vectors).reshape(len(vectors), shards, -1)
            return stacked.transpose(1, 0, 2).reshape(shards, -1)

        return jnp.concatenate(
            [
                owners(both[0], both[1]),
                owners(sums[5]),
                owners(in_sums[0]),
                owners(sums[2]),
                owners(sums[3], sums[0]),
                owners(sums[4], sums[1]),
            ],
            axis=1,
        )

    d_one, sums_one = attention_back(0, d_attended)
    if staged:
        left = after(flat_row, *inner.send(d_one))
        (far,) = product_pieces(left, d_one, spot, 1)
        here = swap(far, "shard", CORE)
        d_one = after(d_one, far)
        (d_tokens,) = input_back(0, d_one, w_qkv_all)
        left = after(flat_row, d_tokens)
        near = product_pieces(left, d_one, spot, 0, here, (), "both")
        one = scatter_steps([(*near[:2], "ctx"), (*near[2:], "side")], spot)
        one_sent = next(one)
        inner_sent = inner.send(one_sent)
        owned_down = lax.psum_scatter(part_down, "shard", scatter_dimension=0, tiled=True)[0]
        d_two, sums_two = attention_back(1, after(d_attended, *one_sent, *inner_sent))
        sent = one.send(d_two) + inner.send(d_two)
        (far,) = product_pieces(after(flat_row, *sent), d_two, spot, 1)
        here = swap(far, "shard", CORE)
        d_two = after(d_two, far)
        owned_down = after(owned_down, far)
        left = after(flat_row, owned_down)
        near = product_pieces(left, d_two, spot, 0, here, (), "ctx")
        two = scatter_steps([(*near, "ctx")], spot)
        two_sent = next(two)
        two_sent = [*two_sent, *inner.send(two_sent), *one.send(two_sent)]
        down_here = swap(owned_down, "ctx")
        last = after(d_two, *two_sent)
        own_tokens, d_tokens = input_back(1, last, w_qkv_all, d_tokens, d_first)
        tokens_here = swap(d_tokens, "ctx")
        (grad_owned,) = meet((owned_down, after(down_here, d_tokens)), dtype=F32)
        grad_w_down, grad_w_out = grad_owned[: 4 * owned_rows], grad_owned[4 * owned_rows :]
        table = column_sums(sums_one, after(sums_two, grad_owned))
        small_sums = small_steps(table)
        sent = two.send([next(small_sums)])
        sent = one.send(sent)
        sent = [small_sums.send(sent)]
        sent = two.send(sent)
        sent = one.send(sent)
        sent = [small_sums.send(sent)]
        grad_tokens = own_tokens + after(tokens_here, *sent).astype(F32)
        grad_tokens = grad_tokens.reshape(row_count, part_len, width)
        sent = two.send([*sent, grad_tokens])
        sent = [small_sums.send(sent)]
        sent = two.send(sent)
        sent = [small_sums.send(sent)]
        owned = small_sums.send(sent)[0]
        grad_w_in = owned_rows_of(next(inner))
        second, first = next(two), next(one)
        grad_pairs = owned_rows_of(jnp.concatenate([first, second], 0))
    else:
        d_two, sums_two = attention_back(1, d_attended)
        d_tokens = (d_tokens_of(0, d_one) + d_tokens_of(1, d_two)).reshape(row_count, seq_len, width)
        grad_tokens = d_first.reshape(row_count, part_len, width) + sum_to_owners(d_tokens, part_len)
        grad_w_down = reduce_partial(inner_left(active, d_mixed).astype(BF16))
        grad_w_out = reduce_partial(inner_left(attended, d_branch).astype(BF16))
        together = inner_left(flat_row, jnp.concatenate([d_one, d_two], 1))
        grad_pairs = reduce_partial(together.astype(BF16))
        owned = reduce_small(column_sums(sums_one, sums_two))[0]
    grad_w_qkv = (
        grad_pairs.reshape(owned_rows, pairs, 3, PAIR).transpose(0, 2, 1, 3).reshape(w_qkv.shape)
    )
    owned = jnp.split(owned, [sum(sizes[:i]) for i in range(1, len(sizes))])
    return (
        outputs,
        grad_tokens,
        grad_w_qkv,
        owned[0].reshape(qv_bias.shape),
        grad_w_out,
        owned[1],
        grad_w_in,
        owned[2],
        grad_w_down,
        owned[3],
        owned[4].reshape(gains.shape),
        owned[5].reshape(shifts.shape),
    )


def solution(mesh):
    row, flat = P("shard", None), P("shard")
    wide, whole = P(None, "shard"), P("shard", "ctx", None)
    return jax.shard_map(
        on_device,
        mesh=mesh,
        in_specs=(
            whole,
            P("shard", "ctx"),
            row,
            wide,
            row,
            flat,
            row,
            flat,
            row,
            flat,
            wide,
            wide,
            whole,
        ),
        out_specs=(whole, whole, row, wide, row, flat, row, flat, row, flat, wide, wide),
        check_vma=False,
    )
```

```python
import functools

import jax
import jax.numpy as jnp
from jax import lax
from jax.experimental import pallas as pl
from jax.experimental.pallas import tpu as pltpu
from jax.sharding import PartitionSpec as P

H = 16
HD = 64
PAIR = 2 * HD
FAR = -1e30
LIGHT = pl.CostEstimate(flops=0, bytes_accessed=0, transcendentals=0)
VMEM = 60 * 1024 * 1024
CORE, SIDE, NEAR, WIDE = 1, 2, 4, 8

F32 = jnp.float32
BF16 = jnp.bfloat16


def inner_left(left, right):
    return lax.dot_general(left, right, (((0,), (0,)), ((), ())), preferred_element_type=F32)


def inner_right(left, right):
    return lax.dot_general(left, right, (((1,), (1,)), ((), ())), preferred_element_type=F32)


def swap(value, axis, bit=1):
    return lax.ppermute(value, axis, [(i, i ^ bit) for i in range(lax.axis_size(axis))])


def by_side(own_is_first, own, other, axis):
    return jnp.where(
        own_is_first,
        jnp.concatenate([own, other], axis),
        jnp.concatenate([other, own], axis),
    )


def place():
    shard, ctx = lax.axis_index("shard"), lax.axis_index("ctx")
    return shard % 2, (shard // 2) % 2, (shard // 4) % 2, shard // 8, ctx


def assemble_body(depth, width, where_ref, *refs):
    pieces, out, sems = refs[:2], refs[2], refs[3]
    core, side, near, wide, ctx = (where_ref[i] for i in range(5))
    copies = []
    for index in range(16):
        far_core, part, second, first = index // 8, (index // 4) % 2, (index // 2) % 2, index % 2
        side_rel, ctx_rel = (first, second) if part == 0 else (second, first)
        column = ((core ^ far_core) * 2 + (ctx ^ ctx_rel)) * 2 + part
        for k in range(4):
            row = (((wide ^ (k % 2)) * 2 + (near ^ (k // 2))) * 2) + (side ^ side_rel)
            target = out.at[
                pl.ds(pl.multiple_of(row * depth, depth), depth),
                pl.ds(pl.multiple_of(column * width, width), width),
            ]
            source = pieces[far_core].at[index % 8 * 4 + k]
            copies.append(pltpu.make_async_copy(source, target, sems.at[len(copies)]))
    for copy in copies:
        copy.start()
    for copy in copies:
        copy.wait()


def gather_pairwise(shard, spot, others):
    rows, columns = shard.shape
    width = columns // 8
    core, side, near, wide, ctx = spot
    split = shard.reshape(rows, 8, width).transpose(1, 0, 2).reshape(2, 2, 2, rows, width)
    mine = lax.dynamic_index_in_dim(split, ctx, 1, False)
    own = lax.dynamic_index_in_dim(mine, core, 0, False)
    other = lax.dynamic_index_in_dim(mine, 1 - core, 0, False)
    held = by_side(core == 0, own, swap(other, "shard", CORE), 1)[None]
    for bit in (WIDE, NEAR):
        held = jnp.concatenate([held, swap(held, "shard", bit)], 0)
        begun = held if bit == WIDE else begun
    held = [held[:, 0], held[:, 1]]
    along = (("shard", SIDE), ("ctx", 1))
    for routes in (along, along[::-1]):
        held = [
            jnp.concatenate([value, swap(value, *route)], 0)
            for value, route in zip(held, routes, strict=True)
        ]
        if routes is along:
            held = [after(value, *others) for value in held]
    here = jnp.concatenate(held, 0)
    whole = pl.pallas_call(
        functools.partial(assemble_body, 2 * rows, width),
        out_shape=jax.ShapeDtypeStruct((16 * rows, columns), BF16),
        in_specs=[pl.BlockSpec(memory_space=pltpu.SMEM)]
        + [pl.BlockSpec(memory_space=pl.ANY)] * 2,
        out_specs=pl.BlockSpec(memory_space=pltpu.VMEM),
        scratch_shapes=[pltpu.SemaphoreType.DMA((64,))],
        compiler_params=pltpu.CompilerParams(vmem_limit_bytes=VMEM),
        cost_estimate=LIGHT,
        name="assemble",
    )(jnp.stack(spot).astype(jnp.int32), here, swap(here, "shard", CORE))
    return whole, begun


def gather_small(flat):
    held = flat[None]
    for bit in (CORE, SIDE, NEAR, WIDE):
        held = jnp.concatenate([held, swap(held, "shard", bit)], 0)
    return pick_rows(held)


def pick_rows(held):
    count = held.shape[0]
    index = lax.iota(jnp.int32, count) ^ lax.axis_index("shard")
    choose = (index[:, None] == lax.iota(jnp.int32, count)[None, :]).astype(F32)
    return jnp.dot(choose, held.astype(F32), precision=lax.Precision.HIGHEST)


def product_body(depth, beside, adds, split, where_ref, left_ref, right_ref, *refs):
    side, near, wide = (where_ref[i] for i in range(1, 4))
    result = inner_left(left_ref[...], right_ref[...])
    if beside:
        result = jnp.concatenate([result, inner_left(refs[0][...], refs[1][...])], 1)
    outs = refs[-4:] if split == "both" else refs[-2:] if split else refs[-1:]

    def values():
        for i in range(8):
            z, y = i // 2, i % 2
            row = (y ^ side) * 4 + ((z % 2) ^ near) * 2 + ((z // 2) ^ wide)
            value = result[i * depth : (i + 1) * depth]
            if adds:
                value = value + refs[2 * beside][0, row].astype(F32)
            yield y ^ side, row, value.astype(BF16)

    def by_ctx(pair, pick):
        for index in range(2):

            @pl.when(pl.program_id(0) == index)
            def _(index=index):
                for _, row, value in values():
                    pair[index][row] = pick(value)

    def by_row(pair, pick):
        for far_side, row, value in values():
            for index in range(2):

                @pl.when(far_side == index)
                def _(index=index, row=row, value=value):
                    pair[index][0, row - 4 * index] = pick(value)

    if split == "both":
        middle = outs[0].shape[-1]
        by_ctx(outs[:2], lambda value: value[:, :middle])
        by_row(outs[2:], lambda value: value[:, middle:])
    elif split == "ctx":
        by_ctx(outs, lambda value: value)
    elif split == "side":
        by_row(outs, lambda value: value)
    else:
        for _, row, value in values():
            outs[0][0, row] = value


def product_pieces(left, right, spot, far, received=None, beside=(), split=None):
    tokens, rows = left.shape
    depth = rows // 8
    pairs = [(left, right), *([beside] if beside else [])]
    specs, full = [], 0
    for one, two in pairs:
        width = two.shape[1] // 4
        full += width
        specs += [
            pl.BlockSpec(one.shape, lambda j, w: (0, 0)),
            pl.BlockSpec((two.shape[0], width), lambda j, w: (0, (w[0] ^ far) * 2 + (w[4] ^ j))),
        ]
    out_spec = pl.BlockSpec((1, 8, depth, full), lambda j, w: (j, 0, 0, 0))
    in_specs = specs + ([out_spec] if received is not None else [])
    along_ctx = lambda n: ((8, depth, n), pl.BlockSpec((8, depth, n), lambda j, w: (0, 0, 0)))
    along_side = lambda n: (
        (2, 4, depth, n),
        pl.BlockSpec((1, 4, depth, n), lambda j, w: (j, 0, 0, 0)),
    )
    if split == "both":
        last = full * 3 // 8 // 128 * 128
        outs = [along_ctx(full - last)] * 2 + [along_side(last)] * 2
    elif split:
        outs = [along_ctx(full) if split == "ctx" else along_side(full)] * 2
    else:
        outs = [((2, 8, depth, full), out_spec)]
    adds = received is not None
    return pl.pallas_call(
        functools.partial(product_body, depth, bool(beside), adds, split),
        grid_spec=pltpu.PrefetchScalarGridSpec(
            num_scalar_prefetch=1,
            grid=(2,),
            in_specs=in_specs,
            out_specs=[spec for _, spec in outs],
        ),
        out_shape=[jax.ShapeDtypeStruct(shape, BF16) for shape, _ in outs],
        compiler_params=pltpu.CompilerParams(vmem_limit_bytes=VMEM),
        cost_estimate=LIGHT,
        name="weight_gradient",
    )(jnp.stack(spot).astype(jnp.int32), left, right, *beside, *([received] if adds else []))


def meet_body(parts, refs, outs):
    value = [
        refs[2 * i][...].astype(F32) + refs[2 * i + 1][...].astype(F32) for i in range(parts)
    ]
    value = value[0] if parts == 1 else jnp.concatenate(value, -1)
    if len(outs) == 1:
        outs[0][...] = value.astype(outs[0].dtype)
    else:
        outs[0][...] = value[0].astype(BF16)
        outs[1][...] = value[1].astype(BF16)


def meet(*pairs, dtype=BF16):
    rows = pairs[0][0].shape[-2]
    halves = pairs[0][0].ndim == 3
    widths = [left.shape[-1] for left, _ in pairs]
    columns = sum(widths)
    steps = 4 if rows % 64 == 0 and rows * columns > 1 << 18 else 1
    count = 2 * len(pairs)

    def spec(width, leading):
        if leading:
            return pl.BlockSpec((2, rows // steps, width), lambda i: (0, i, 0))
        return pl.BlockSpec((rows // steps, width), lambda i: (i, 0))

    outs = 2 if halves else 1
    return pl.pallas_call(
        lambda *refs: meet_body(len(pairs), refs[:count], refs[count:]),
        grid=(steps,),
        in_specs=[spec(width, halves) for width in widths for _ in range(2)],
        out_specs=[spec(columns, False)] * outs,
        out_shape=[jax.ShapeDtypeStruct((rows, columns), dtype)] * outs,
        compiler_params=pltpu.CompilerParams(vmem_limit_bytes=VMEM),
        cost_estimate=LIGHT,
        name="meet",
    )(*[item for pair in pairs for item in pair])


def owner_body(active, mixed, attended, branch, out):
    down = inner_left(active[...], mixed[...]).astype(BF16)
    outer = inner_left(attended[...], branch[...]).astype(BF16)
    tall, short = down.shape[0] // 2, outer.shape[0] // 2
    for i in range(2):
        out[i, :tall] = down[i * tall : (i + 1) * tall]
        out[i, tall:] = outer[i * short : (i + 1) * short]


def owner_gradients(active, mixed, attended, branch, shards):
    count, width = mixed.shape
    tall, short = active.shape[1] // shards, width // shards
    return pl.pallas_call(
        owner_body,
        grid=(shards // 2,),
        in_specs=[
            pl.BlockSpec((count, 2 * tall), lambda i: (0, i)),
            pl.BlockSpec((count, width), lambda i: (0, 0)),
            pl.BlockSpec((count, 2 * short), lambda i: (0, i)),
            pl.BlockSpec((count, width), lambda i: (0, 0)),
        ],
        out_specs=pl.BlockSpec((2, tall + short, width), lambda i: (i, 0, 0)),
        out_shape=jax.ShapeDtypeStruct((shards, tall + short, width), BF16),
        compiler_params=pltpu.CompilerParams(vmem_limit_bytes=VMEM),
        cost_estimate=LIGHT,
        name="owner_gradients",
    )(active, mixed, attended, branch)


def scatter_steps(parts, spot):
    depth = parts[0][0].shape[-2]
    core, ctx = spot[0], spot[4]

    def both(value):
        return value.reshape(2, value.size // value.shape[-1] // 2, value.shape[-1])

    def gated(dep, got):
        return got if dep is None else lax.optimization_barrier((got, dep))[0]

    along = {"side": ("shard", SIDE), "ctx": ("ctx", 1)}
    other = {"side": "ctx", "ctx": "side"}
    dep = yield [sent for _, sent, _ in parts]
    moved = []
    for keep, sent, name in parts:
        got = gated(dep, swap(sent, *along[name]))
        keep, sent = meet((both(keep), both(got)))
        moved.append((keep, sent, other[name]))
    dep = yield [sent for _, sent, _ in moved]
    keep, sent = meet(
        *[(both(keep), both(gated(dep, swap(sent, *along[name])))) for keep, sent, name in moved]
    )
    dep = yield [sent]
    keep, sent = meet((both(keep), both(gated(dep, swap(sent, "shard", NEAR)))))
    dep = yield [sent]
    (held,) = meet((keep, gated(dep, swap(sent, "shard", WIDE))))
    yield [held]
    rows = depth // 2
    mine = lax.dynamic_slice_in_dim(held, core * rows, rows, 0)
    other = lax.dynamic_slice_in_dim(held, (1 - core) * rows, rows, 0)
    shards = lax.axis_size("shard")
    across = [(i, i ^ 3) for i in range(2 * shards)]
    corner = lax.ppermute(other, ("shard", "ctx"), across)
    here = by_side(ctx == 0, mine[None], swap(mine, "ctx")[None], 0)
    there = by_side(ctx == 0, swap(other, "shard", CORE)[None], corner[None], 0)
    yield by_side(core == 0, here, there, 0)


def owned_rows_of(pieces):
    count, rows, width = pieces.shape
    return pieces.transpose(1, 0, 2).reshape(rows, count * width).astype(F32)


def reduce_partial(partial):
    owned = lax.psum_scatter(partial, "shard", scatter_dimension=0, tiled=True)
    return lax.psum(owned, "ctx").astype(F32)


def after(value, *others):
    return lax.optimization_barrier((value, *others))[0]


def small_steps(table):
    held = pick_rows(table)
    for axis, bit in (("shard", WIDE), ("shard", NEAR), ("shard", SIDE), ("shard", CORE), ("ctx", 1)):
        half = held.shape[0] // 2
        keep, sent = (held, held) if axis == "ctx" else (held[:half], held[half:])
        sent = sent.astype(BF16)
        dep = yield sent
        got = lax.optimization_barrier((swap(sent, axis, bit), dep))[0]
        held = keep + got.astype(F32)
    yield held


def reduce_small(table):
    owned = lax.psum_scatter(table.astype(BF16), "shard", scatter_dimension=0, tiled=True)
    return lax.psum(owned, "ctx").astype(F32)


def head_lanes(shape, head):
    lane = lax.broadcasted_iota(jnp.int32, shape, 1)
    return (lane // HD) == head


def attend_body(part_len, proj_ref, mark_ref, veto_ref, out_ref, norm_ref):
    block = proj_ref[0]
    query, keys, value = (
        block[:part_len, :PAIR],
        block[:, PAIR : 2 * PAIR],
        block[:, 2 * PAIR :],
    )
    scaled = query * jnp.asarray(HD**-0.5, BF16)
    keys_marked = jnp.concatenate([keys, veto_ref[0]], 1)
    results, norms = [], []
    for head in range(2):
        alone = jnp.where(head_lanes(scaled.shape, head), scaled, jnp.zeros_like(scaled))
        scores = inner_right(keys_marked, jnp.concatenate([alone, mark_ref[0]], 1))
        top = jnp.max(scores, axis=0, keepdims=True)
        weights = jnp.exp(scores - top)
        total = jnp.sum(weights, axis=0, keepdims=True)
        result = inner_left(value, weights.astype(BF16))
        results.append(result[head * HD : (head + 1) * HD] * (1.0 / total))
        norms.append(top + jnp.log(total))
    out_ref[0] = jnp.concatenate(results, 0).T.astype(out_ref.dtype)
    norm_ref[0, 0] = jnp.concatenate(norms, 0)


def attend(proj, mark, veto):
    rows, seq_len, columns = proj.shape
    part_len = mark.shape[1]
    pairs = columns // (3 * PAIR)
    return pl.pallas_call(
        functools.partial(attend_body, part_len),
        grid=(rows, pairs),
        in_specs=[
            pl.BlockSpec((1, seq_len, 3 * PAIR), lambda r, j: (r, 0, j)),
            pl.BlockSpec((1, part_len, PAIR), lambda r, j: (r, 0, 0)),
            pl.BlockSpec((1, seq_len, PAIR), lambda r, j: (r, 0, 0)),
        ],
        out_specs=[
            pl.BlockSpec((1, part_len, PAIR), lambda r, j: (r, 0, j)),
            pl.BlockSpec((1, 1, 2, part_len), lambda r, j: (r, j, 0, 0)),
        ],
        out_shape=[
            jax.ShapeDtypeStruct((rows, part_len, pairs * PAIR), BF16),
            jax.ShapeDtypeStruct((rows, pairs, 2, part_len), F32),
        ],
        compiler_params=pltpu.CompilerParams(vmem_limit_bytes=VMEM),
        cost_estimate=LIGHT,
        name="attend",
    )(proj, mark, veto)


def attend_back_body(
    part_len, proj_ref, mark_ref, veto_ref, grad_ref, result_ref, norm_ref, out_ref, sums_ref
):
    block = proj_ref[0]
    seq_len = block.shape[0]
    query, keys, value = (
        block[:part_len, :PAIR],
        block[:, PAIR : 2 * PAIR],
        block[:, 2 * PAIR :],
    )
    scaled = query * jnp.asarray(HD**-0.5, BF16)
    keys_marked = jnp.concatenate([keys, veto_ref[0]], 1)
    grad = grad_ref[0]
    product = (grad.astype(F32) * result_ref[0].astype(F32)).T
    d_query, d_keys, d_value = [], None, None
    for head in range(2):
        lanes = head_lanes(scaled.shape, head)
        alone = jnp.where(lanes, scaled, jnp.zeros_like(scaled))
        grad_alone = jnp.where(lanes, grad, jnp.zeros_like(grad))
        scores = inner_right(keys_marked, jnp.concatenate([alone, mark_ref[0]], 1))
        weights = jnp.exp(scores - norm_ref[0, 0, head : head + 1, :])
        d_weights = inner_right(value, grad_alone)
        inner = jnp.sum(product[head * HD : (head + 1) * HD], axis=0, keepdims=True)
        d_scores = (weights * (d_weights - inner)).astype(BF16)
        more_value = jnp.dot(weights.astype(BF16), grad_alone, preferred_element_type=F32)
        more_keys = jnp.dot(d_scores, alone, preferred_element_type=F32)
        d_value = more_value if d_value is None else d_value + more_value
        d_keys = more_keys if d_keys is None else d_keys + more_keys
        d_query.append(inner_left(keys, d_scores)[head * HD : (head + 1) * HD])
    d_query = jnp.concatenate(d_query, 0).T * HD**-0.5
    out_ref[0, :part_len, :PAIR] = d_query.astype(BF16)
    if seq_len > part_len:
        out_ref[0, part_len:, :PAIR] = jnp.zeros((seq_len - part_len, PAIR), BF16)
    out_ref[0, :, PAIR : 2 * PAIR] = d_keys.astype(BF16)
    out_ref[0, :, 2 * PAIR :] = d_value.astype(BF16)
    sums_ref[0, 0, 0:1] = jnp.sum(d_query, axis=0, keepdims=True)
    sums_ref[0, 0, 1:2] = jnp.sum(d_value, axis=0, keepdims=True)


def attend_back(part, proj, mark, veto, grad, result, norm):
    rows, seq_len, columns = proj.shape
    part_len = mark.shape[1]
    pairs = columns // (3 * PAIR) // 2
    own = pl.BlockSpec((1, part_len, PAIR), lambda r, j: (r, 0, part * pairs + j))
    return pl.pallas_call(
        functools.partial(attend_back_body, part_len),
        grid=(rows, pairs),
        in_specs=[
            pl.BlockSpec((1, seq_len, 3 * PAIR), lambda r, j: (r, 0, part * pairs + j)),
            pl.BlockSpec((1, part_len, PAIR), lambda r, j: (r, 0, 0)),
            pl.BlockSpec((1, seq_len, PAIR), lambda r, j: (r, 0, 0)),
            own,
            own,
            pl.BlockSpec((1, 1, 2, part_len), lambda r, j: (r, part * pairs + j, 0, 0)),
        ],
        out_specs=[
            pl.BlockSpec((1, seq_len, 3 * PAIR), lambda r, j: (r, 0, j)),
            pl.BlockSpec((1, 1, 2, PAIR), lambda r, j: (r, j, 0, 0)),
        ],
        out_shape=[
            jax.ShapeDtypeStruct((rows, seq_len, columns // 2), BF16),
            jax.ShapeDtypeStruct((rows, pairs, 2, PAIR), F32),
        ],
        compiler_params=pltpu.CompilerParams(vmem_limit_bytes=VMEM),
        cost_estimate=LIGHT,
        name="attend_back",
    )(proj, mark, veto, grad, result, norm)


CUTS = 2


def cuts(rows):
    step = rows // CUTS
    return [slice(i * step, (i + 1) * step) for i in range(CUTS)]


def mean_of(value):
    return jnp.mean(value, axis=-1, keepdims=True)


def normalise(value):
    center = value - mean_of(value)
    scale = lax.rsqrt(mean_of(center * center) + 1e-06)
    return center * scale, scale


def normalise_back(unit, scale, incoming, gain):
    edge = incoming * gain
    return scale * (edge - mean_of(edge) - unit * mean_of(edge * unit))


def total(value):
    return jnp.sum(value, axis=0, keepdims=True)


def whole_block(shape):
    return pl.BlockSpec(shape, lambda *_: (0,) * len(shape))


def square(ref):
    return ref[...].reshape(-1, ref.shape[-1])


def kernel(body, grid, name, in_specs, outs, out_specs, scratch=()):
    return pl.pallas_call(
        body,
        grid=grid,
        in_specs=in_specs,
        out_shape=[jax.ShapeDtypeStruct(*out) for out in outs],
        out_specs=out_specs,
        scratch_shapes=scratch,
        compiler_params=pltpu.CompilerParams(vmem_limit_bytes=VMEM),
        cost_estimate=LIGHT,
        name=name,
    )


def middle_body(
    attended,
    tokens,
    w_out,
    w_in,
    w_down,
    in_bias,
    vectors,
    cotangent,
    low,
    active,
    outputs,
    mixed,
    d_hidden,
    first,
    branch,
    d_attended,
    in_sums,
    sums,
    unit,
    scale,
    slope,
    held,
):
    step = pl.program_id(0)
    out_bias, gain_one, shift_one, down_bias, gain_two, shift_two = (
        vectors[i : i + 1] for i in range(6)
    )
    parts = cuts(held.shape[0])

    @pl.when(step == 0)
    def _():
        matrix = square(w_out)
        for cut in parts:
            value = jnp.dot(attended[cut], matrix, preferred_element_type=F32) + out_bias
            u, r = normalise(tokens[cut].astype(F32) + value)
            unit[cut] = u
            scale[cut] = jnp.broadcast_to(r, (r.shape[0], PAIR))
            normed = u * gain_one + shift_one
            low[cut] = normed.astype(BF16)
            held[cut] = normed + down_bias

    @pl.when(step < 4)
    def _():
        up, down = square(w_in), square(w_down)
        for cut in parts:
            hidden = jnp.dot(low[cut], up, preferred_element_type=F32) + in_bias[...]
            below = 0.5 * (1.0 + lax.erf(hidden * 0.7071067811865476))
            active[cut] = (hidden * below).astype(BF16)
            bell = 0.3989422804014327 * jnp.exp(-0.5 * hidden * hidden)
            slope[step, cut] = (below + hidden * bell).astype(BF16)
        for cut in parts:
            held[cut] += jnp.dot(active[cut], down, preferred_element_type=F32)

    @pl.when(step == 3)
    def _():
        totals = []
        for cut in parts:
            u, r = normalise(held[cut])
            outputs[cut] = (u * gain_two + shift_two).astype(BF16)
            incoming = cotangent[cut]
            back = normalise_back(u, r, incoming, gain_two)
            held[cut] = back
            mixed[cut] = back.astype(BF16)
            totals.append((total(incoming * u), total(incoming), total(mixed[cut].astype(F32))))
        for i, item in enumerate(zip(*totals, strict=True)):
            sums[i : i + 1] = sum(item)

    @pl.when(step >= 4)
    def _():
        up, down = square(w_in), square(w_down)
        totals = []
        for cut in parts:
            grad = (inner_right(mixed[cut], down) * slope[step - 4, cut].astype(F32)).astype(BF16)
            d_hidden[cut] = grad
            totals.append(total(grad.astype(F32)))
        in_sums[...] = sum(totals)
        for cut in parts:
            held[cut] += inner_right(d_hidden[cut], up)

    @pl.when(step == 7)
    def _():
        matrix = square(w_out)
        totals = []
        for cut in parts:
            incoming, u = held[cut], unit[cut]
            back = normalise_back(u, scale[cut][:, :1], incoming, gain_one)
            first[cut] = back
            branch[cut] = back.astype(BF16)
            totals.append((total(incoming * u), total(incoming), total(branch[cut].astype(F32))))
        for cut in parts:
            d_attended[cut] = inner_right(branch[cut], matrix).astype(BF16)
        for i, item in enumerate(zip(*totals, strict=True)):
            sums[3 + i : 4 + i] = sum(item)


def middle(attended, tokens, packed, in_bias, vectors, cotangent):
    count, width = tokens.shape
    shards, rows, _ = packed.shape
    once = pl.Buffered(buffer_count=1)
    row = pl.BlockSpec((count, width), lambda s: (0, 0), pipeline_mode=once)
    kept = whole_block((count, width))

    def block(index, depth=shards):
        return pl.BlockSpec((depth, rows // 9 * (shards // depth), width), index)

    forward = pl.BlockSpec((count, width), lambda s: (0, jnp.minimum(s, 3)))
    backward = pl.BlockSpec((count, width), lambda s: (0, jnp.maximum(s - 4, 0)))
    low, tall = ((count, width), BF16), ((count, 4 * width), BF16)
    return kernel(
        middle_body,
        (8,),
        "middle",
        [
            row,
            row,
            pl.BlockSpec((shards, rows // 9, width), lambda s: (0, 8, 0), pipeline_mode=once),
            block(lambda s: (0, 4 + lax.rem(s, 4), 0)),
            block(lambda s: (lax.rem(s, 4), 0, 0), shards // 4),
            pl.BlockSpec((1, width), lambda s: (0, jnp.minimum(s, 3))),
            whole_block((6, width)),
            row,
        ],
        [low, tall, low, low, tall, ((count, width), F32), low, low]
        + [((1, 4 * width), F32), ((6, width), F32)],
        [kept, forward, kept, kept, backward, kept, kept, kept]
        + [pl.BlockSpec((1, width), lambda s: (0, jnp.maximum(s - 4, 0))), whole_block((6, width))],
        [
            pltpu.VMEM((count, width), F32),
            pltpu.VMEM((count, PAIR), F32),
            pltpu.VMEM((4, count, width), BF16),
            pltpu.VMEM((count, width), F32),
        ],
    )(attended, tokens, packed, packed, packed, in_bias, vectors, cotangent)


def input_back_body(block, weight, more, first, *outs):
    step = pl.program_id(0)
    result = inner_right(block[...], weight[...])
    if len(outs) == 1:
        outs[0][...] = result.astype(BF16)
        return
    result = result + more[...].astype(F32)

    @pl.when(step == 0)
    def _():
        outs[0][...] = result + first[...]

    @pl.when(step > 0)
    def _():
        outs[1][...] = result.astype(BF16)


def input_back(part, block, w_qkv, more=None, first=None):
    rows, half = block.shape
    width = w_qkv.shape[0]
    mine = rows // 2
    row = pl.BlockSpec((mine, width), lambda i: (i, 0))
    last = more is not None
    body = input_back_body if last else lambda b, w, o: input_back_body(b, w, None, None, o)
    return kernel(
        body,
        (2,),
        "input_back",
        [
            pl.BlockSpec((mine, half), lambda i: (i, 0)),
            pl.BlockSpec((width, half), lambda i: (0, part)),
            *([row, whole_block((mine, width))] if last else []),
        ],
        [((mine, width), F32), ((mine, width), BF16)] if last else [((rows, width), BF16)],
        [whole_block((mine, width))] * 2 if last else [row],
    )(block, w_qkv, *([more, first] if last else []))


def own_first(value, axis):
    if lax.axis_size("ctx") == 2:
        return jnp.concatenate([value, swap(value, "ctx")], axis)
    whole = lax.all_gather(value, "ctx", axis=axis, tiled=True)
    return jnp.roll(whole, -lax.axis_index("ctx") * value.shape[axis], axis)


def sum_to_owners(value, own_len):
    own = value[:, :own_len].astype(F32)
    if lax.axis_size("ctx") == 2:
        return own + swap(value[:, own_len:].astype(BF16), "ctx").astype(F32)
    whole = jnp.roll(value, lax.axis_index("ctx") * own_len, 1).astype(BF16)
    return lax.psum_scatter(whole, "ctx", scatter_dimension=1, tiled=True).astype(F32)


def on_device(
    tokens,
    segments,
    w_qkv,
    qv_bias,
    w_out,
    out_bias,
    w_in,
    in_bias,
    w_down,
    down_bias,
    gains,
    shifts,
    cotangent,
):
    staged = lax.axis_size("shard") == 16 and lax.axis_size("ctx") == 2
    spot = place() if staged else None
    row_count, part_len, width = tokens.shape
    owned_rows = w_qkv.shape[0]
    pairs = H // 2
    token_count = row_count * part_len

    w_pairs = (
        w_qkv.reshape(owned_rows, 3, pairs, PAIR).transpose(0, 2, 1, 3).reshape(w_qkv.shape)
    )
    small = [qv_bias, out_bias, in_bias, down_bias, gains, shifts]
    sizes = [item.size for item in small]
    flat = jnp.concatenate([item.reshape(-1) for item in small])
    tokens_row = own_first(tokens, 1)
    segments_row = own_first(segments, 1)
    seq_len = tokens_row.shape[1]
    lanes = lax.iota(jnp.int32, PAIR)
    mark = (segments[:, :, None] == lanes).astype(BF16)
    veto = jnp.where(segments_row[:, :, None] == lanes, 0.0, FAR).astype(BF16)

    packed = jnp.concatenate(
        [
            w_down,
            w_in.reshape(owned_rows, 4, width).transpose(1, 0, 2).reshape(-1, width),
            w_out,
        ],
        0,
    )
    if staged:
        table = gather_small(flat)
        w_qkv_all, begun = gather_pairwise(w_pairs, spot, [table, tokens_row])
        packed = after(packed, begun)
    else:
        w_qkv_all = lax.all_gather(w_pairs, "shard", axis=0, tiled=True)
    packed = lax.all_gather(packed, "shard", axis=0)
    if not staged:
        table = lax.all_gather(flat, "shard", axis=0).astype(F32)
    pieces = jnp.split(table, [sum(sizes[:i]) for i in range(1, len(sizes))], axis=1)

    def two(piece):
        return piece.reshape(-1, 2, owned_rows).transpose(1, 0, 2).reshape(2, width)

    qv_all, gain_all, shift_all = two(pieces[0]), two(pieces[4]), two(pieces[5])
    out_all, in_all, down_all = (pieces[i].reshape(-1) for i in (1, 2, 3))

    flat_row = lax.optimization_barrier(tokens_row.reshape(row_count * seq_len, width))
    bias_row = jnp.stack(
        [qv_all[0].reshape(pairs, PAIR), jnp.zeros((pairs, PAIR), F32), qv_all[1].reshape(pairs, PAIR)],
        1,
    )
    raw = jnp.dot(flat_row, w_qkv_all, preferred_element_type=F32) + bias_row.reshape(-1)
    proj = raw.astype(BF16).reshape(row_count, seq_len, 3 * width)
    attended_rows, norm = attend(proj, mark, veto)
    attended = attended_rows.reshape(token_count, width)
    flat_tokens = tokens.reshape(token_count, width)
    vectors = [out_all, gain_all[0], shift_all[0], down_all, gain_all[1], shift_all[1]]
    (
        normed_low,
        active,
        outputs,
        d_mixed,
        d_hidden,
        d_first,
        d_branch,
        d_attended,
        in_sums,
        sums,
    ) = middle(
        attended,
        flat_tokens,
        packed,
        in_all[None],
        jnp.stack(vectors),
        cotangent.reshape(token_count, width),
    )
    outputs = outputs.reshape(row_count, part_len, width)
    d_attended = d_attended.reshape(attended_rows.shape)
    if staged:
        (far_in,) = product_pieces(normed_low, d_hidden, spot, 1)
        here_in = swap(far_in, "shard", CORE)
        active = after(active, far_in)
    if staged:
        part_down = owner_gradients(active, d_mixed, attended, d_branch, lax.axis_size("shard"))
        left = after(normed_low, part_down)
        near_in = product_pieces(left, d_hidden, spot, 0, here_in, (), "both")
        inner = scatter_steps([(*near_in[:2], "ctx"), (*near_in[2:], "side")], spot)
        d_attended = after(d_attended, *next(inner))
    else:
        grad_w_in = reduce_partial(inner_left(normed_low, d_hidden).astype(BF16))
    half = 3 * width // 2
    rows_flat = row_count * seq_len

    def d_tokens_of(part, block):
        return inner_right(block, lax.slice_in_dim(w_qkv_all, part * half, (part + 1) * half, axis=1))

    def attention_back(part, grad):
        block, sums = attend_back(part, proj, mark, veto, grad, attended_rows, norm)
        return block.reshape(rows_flat, half), jnp.sum(sums, axis=0)

    def column_sums(sums_one, sums_two):
        both = jnp.concatenate([sums_one, sums_two], 0).transpose(1, 0, 2).reshape(2, width)
        shards = lax.axis_size("shard")

        def owners(*vectors):
            stacked = jnp.stack(vectors).reshape(len(vectors), shards, -1)
            return stacked.transpose(1, 0, 2).reshape(shards, -1)

        return jnp.concatenate(
            [
                owners(both[0], both[1]),
                owners(sums[5]),
                owners(in_sums[0]),
                owners(sums[2]),
                owners(sums[3], sums[0]),
                owners(sums[4], sums[1]),
            ],
            axis=1,
        )

    d_one, sums_one = attention_back(0, d_attended)
    if staged:
        left = after(flat_row, *inner.send(d_one))
        (far,) = product_pieces(left, d_one, spot, 1)
        here = swap(far, "shard", CORE)
        d_one = after(d_one, far)
        (d_tokens,) = input_back(0, d_one, w_qkv_all)
        left = after(flat_row, d_tokens)
        near = product_pieces(left, d_one, spot, 0, here, (), "both")
        one = scatter_steps([(*near[:2], "ctx"), (*near[2:], "side")], spot)
        one_sent = next(one)
        inner_sent = inner.send(one_sent)
        owned_down = lax.psum_scatter(part_down, "shard", scatter_dimension=0, tiled=True)[0]
        d_two, sums_two = attention_back(1, after(d_attended, *one_sent, *inner_sent))
        sent = one.send(d_two) + inner.send(d_two)
        (far,) = product_pieces(after(flat_row, *sent), d_two, spot, 1)
        here = swap(far, "shard", CORE)
        d_two = after(d_two, far)
        owned_down = after(owned_down, far)
        left = after(flat_row, owned_down)
        near = product_pieces(left, d_two, spot, 0, here, (), "ctx")
        two = scatter_steps([(*near, "ctx")], spot)
        two_sent = next(two)
        two_sent = [*two_sent, *inner.send(two_sent), *one.send(two_sent)]
        down_here = swap(owned_down, "ctx")
        last = after(d_two, *two_sent)
        own_tokens, d_tokens = input_back(1, last, w_qkv_all, d_tokens, d_first)
        tokens_here = swap(d_tokens, "ctx")
        (grad_owned,) = meet((owned_down, after(down_here, d_tokens)), dtype=F32)
        grad_w_down, grad_w_out = grad_owned[: 4 * owned_rows], grad_owned[4 * owned_rows :]
        table = column_sums(sums_one, after(sums_two, grad_owned))
        small_sums = small_steps(table)
        sent = two.send([next(small_sums)])
        sent = one.send(sent)
        sent = [small_sums.send(sent)]
        sent = two.send(sent)
        sent = one.send(sent)
        sent = [small_sums.send(sent)]
        grad_tokens = own_tokens + after(tokens_here, *sent).astype(F32)
        grad_tokens = grad_tokens.reshape(row_count, part_len, width)
        sent = two.send([*sent, grad_tokens])
        sent = [small_sums.send(sent)]
        sent = two.send(sent)
        sent = [small_sums.send(sent)]
        owned = small_sums.send(sent)[0]
        grad_w_in = owned_rows_of(next(inner))
        second, first = next(two), next(one)
        grad_pairs = owned_rows_of(jnp.concatenate([first, second], 0))
    else:
        d_two, sums_two = attention_back(1, d_attended)
        d_tokens = (d_tokens_of(0, d_one) + d_tokens_of(1, d_two)).reshape(row_count, seq_len, width)
        grad_tokens = d_first.reshape(row_count, part_len, width) + sum_to_owners(d_tokens, part_len)
        grad_w_down = reduce_partial(inner_left(active, d_mixed).astype(BF16))
        grad_w_out = reduce_partial(inner_left(attended, d_branch).astype(BF16))
        together = inner_left(flat_row, jnp.concatenate([d_one, d_two], 1))
        grad_pairs = reduce_partial(together.astype(BF16))
        owned = reduce_small(column_sums(sums_one, sums_two))[0]
    grad_w_qkv = (
        grad_pairs.reshape(owned_rows, pairs, 3, PAIR).transpose(0, 2, 1, 3).reshape(w_qkv.shape)
    )
    owned = jnp.split(owned, [sum(sizes[:i]) for i in range(1, len(sizes))])
    return (
        outputs,
        grad_tokens,
        grad_w_qkv,
        owned[0].reshape(qv_bias.shape),
        grad_w_out,
        owned[1],
        grad_w_in,
        owned[2],
        grad_w_down,
        owned[3],
        owned[4].reshape(gains.shape),
        owned[5].reshape(shifts.shape),
    )


def solution(mesh):
    row, flat = P("shard", None), P("shard")
    wide, whole = P(None, "shard"), P("shard", "ctx", None)
    return jax.shard_map(
        on_device,
        mesh=mesh,
        in_specs=(
            whole,
            P("shard", "ctx"),
            row,
            wide,
            row,
            flat,
            row,
            flat,
            row,
            flat,
            wide,
            wide,
            whole,
        ),
        out_specs=(whole, whole, row, wide, row, flat, row, flat, row, flat, wide, wide),
        check_vma=False,
    )
```
